32 devices in a mesh: orb: 2 (over y), grid: 16 (over z, x, core).
Axes of the slice: x: 2, y: 2, z: 4, core: 2. Of those that a mesh axis runs over, the one named last changes fastest.
Arguments:
- random_orbitals: float32 [2, 256, 256, 256], P('orb', 'grid'), may hold values from -6 to 6
- potential: float32 [256, 256, 256], P('grid'), may hold values from -1.5 to 0.5
- sphere_cells: int32 [256, 2, 128], P('grid'), may hold values from 0 to 65535, as said below
- projectors: float32 [256, 4, 128], P('grid'), may hold values from -0.9 to 0.9
- kb_energy: float32 [4], replicated, may hold values from 0.5 to 1.5
- cheb_coef: float32 [3], replicated, may hold values from 0.5 to 1.5
Outputs:
- density: float32 [256, 256, 256], P('grid')
The draws below stay inside these ranges and needn't reach their ends.
Inputs may be any that keep to these rules, and one draw needn't show every extreme that they name: `sphere_cells`: for each atom a the 128 points are distinct cells: the 128 offsets (dz, dy, dx) with |dz|, |dy|, |dx| <= 3 nearest to the atom's centre, ties broken by the order of (dz, dy, dx) from smallest to largest, added to the centre with periodic wrap along each dimension; row 0 holds the z-plane and row 1 the cell y * 256 + x. The centre's z lies in the slab of planes (a // 16) * 16 to (a // 16) * 16 + 15. Spheres of different atoms may share cells.
All inputs are finite; a program needn't handle non-finite values.
Results may differ from the reference program's by a relative error of at most 0.0002.
Values sent between devices are 32-bit elements; how exact they have to be, the bound alone decides.
No kernel may reach another device: no remote copies, remote signals or barrier semaphores. Data moves between devices by JAX's collectives and lax.ppermute only.
A program may use at most 64 MiB of HBM per device.

```python
import math
import jax
import jax.numpy as jnp
from jax import lax

NX = 256
NY = 256
NZ = 256
SPH = 128
PROJ = 4
REACH = 3
ATOM_DEV = 16
CZ = 16
ATOMS = 256
NSTOCH = 2


def sphere_offsets():
    width = 2 * REACH + 1
    count = width * width * width
    order_ids = jnp.arange(count, dtype=jnp.int32)
    off_z = order_ids // (width * width) - REACH
    off_y = order_ids // width % width - REACH
    off_x = order_ids % width - REACH
    radius = off_z * off_z + off_y * off_y + off_x * off_x
    ranking = jnp.argsort(radius * count + order_ids, stable=True)[:SPH]
    points = jnp.stack([off_z, off_y, off_x], axis=1)
    return points[ranking].astype(jnp.int32)


def draw_sphere_cells(key, part):
    offsets = sphere_offsets()
    key_z, key_y, key_x = jax.random.split(key, 3)
    atom_ids = jnp.arange(ATOMS)
    centre_z = atom_ids // ATOM_DEV * CZ + jax.random.randint(key_z, (ATOMS,), 0, CZ)
    centre_y = jax.random.randint(key_y, (ATOMS,), 0, NY)
    centre_x = jax.random.randint(key_x, (ATOMS,), 0, NX)
    centre_z = centre_z.at[0].set(0).at[ATOMS - 1].set(NZ - 1)
    centre_y = centre_y.at[0].set(0).at[ATOMS - 1].set(NY - 1)
    centre_x = centre_x.at[0].set(0).at[ATOMS - 1].set(NX - 1)
    cell_z = (centre_z[:, None] + offsets[None, :, 0]) % NZ
    cell_y = (centre_y[:, None] + offsets[None, :, 1]) % NY
    cell_x = (centre_x[:, None] + offsets[None, :, 2]) % NX
    in_plane = cell_y * NX + cell_x
    return jnp.stack([cell_z, in_plane], axis=1).astype(jnp.int32)


def block_levels(stream_key, dims, cuts, low, high):
    def one(axis_at, parts):
        draws = jax.random.uniform(jax.random.fold_in(jax.random.fold_in(stream_key, 6), axis_at), (parts,), jnp.float32, low / len(cuts), high / len(cuts))
        return jnp.repeat(jnp.exp(draws), dims[axis_at] // parts).reshape((-1,) + (1,) * (len(dims) - axis_at - 1))

    gain = one(*cuts[0])
    for cut in cuts[1:]:
        gain = gain * one(*cut)
    return gain


def bell_draw(key, extent, scale, most, pieces=(), kind=jnp.bfloat16):
    result = jax.random.normal(key, extent, jnp.float32) * scale
    if len(pieces) > 0:
        result = block_levels(key, extent, pieces, -0.22, 0.18) * result
    return jnp.clip(result, min=-most, max=most).astype(kind)


def setup_inputs(seed: int = 0) -> dict:
    seeds = jax.random.split(jax.random.key(seed), 7)
    return {
        "random_orbitals": bell_draw(seeds[0], (NSTOCH, NZ, NY, NX), 1.0, 6.0, ((0, 2), (1, 16)), jnp.float32),
        "potential": jnp.clip(-1.5 + 2.0 * jax.random.uniform(seeds[1], (NZ, NY, NX), jnp.float32) ** block_levels(seeds[1], (NZ, NY, NX), ((0, 16),), -0.2, 0.2), -1.5, 0.5),
        "sphere_cells": draw_sphere_cells(jax.random.fold_in(seeds[6], 71), 0),
        "projectors": bell_draw(seeds[3], (ATOMS, PROJ, SPH), 0.15, 0.9, ((0, 16),), jnp.float32),
        "kb_energy": jnp.clip(jax.random.uniform(seeds[4], (PROJ,), jnp.float32, 0.5, 1.5), 0.5, 1.5),
        "cheb_coef": jnp.clip(jax.random.uniform(seeds[5], (3,), jnp.float32, 0.5, 1.5), 0.5, 1.5),
    }


PRECISE = lax.Precision.HIGHEST
CENTRE = 2.0
HALF_RANGE = 4.0


def kinetic_table(length):
    places = jnp.arange(length)
    offset = places[:, None] - places[None, :]
    parity = jnp.where(offset % 2 == 0, 1.0, -1.0).astype(jnp.float32)
    angle_half = offset.astype(jnp.float32) * (math.pi / length)
    sine = jnp.where(offset == 0, 1.0, jnp.sin(angle_half)).astype(jnp.float32)
    off_diag = parity / (2.0 * sine * sine)
    on_diag = jnp.float32(length * length / 12.0 + 1.0 / 6.0)
    return (jnp.where(offset == 0, on_diag, off_diag) * (4.0 / (length * length))).astype(jnp.float32)


def reference(random_orbitals, potential, sphere_cells, projectors, kb_energy, cheb_coef):
    kinetic_x = kinetic_table(NX)
    kinetic_y = kinetic_table(NY)
    kinetic_z = kinetic_table(NZ)
    cell_index = (sphere_cells[:, 0, :] * (NY * NX) + sphere_cells[:, 1, :]).astype(jnp.int32)
    flat_cells = cell_index.reshape(-1)

    def apply_hamiltonian(vector):
        kinetic = jnp.dot(vector.reshape(-1, NX), kinetic_x, precision=PRECISE).reshape(vector.shape)
        kinetic = kinetic + jnp.einsum("zyx,yw->zwx", vector, kinetic_y, precision=PRECISE)
        kinetic = kinetic + jnp.einsum("zyx,zw->wyx", vector, kinetic_z, precision=PRECISE)
        values = vector.reshape(-1)[cell_index]
        coeffs = jnp.einsum("aj,apj->ap", values, projectors, precision=PRECISE) * kb_energy
        spread = jnp.einsum("ap,apj->aj", coeffs, projectors, precision=PRECISE)
        nonlocal_part = jnp.zeros((NZ * NY * NX,), jnp.float32).at[flat_cells].add(spread.reshape(-1))
        summed = kinetic + potential * vector + nonlocal_part.reshape(vector.shape)
        return (summed - CENTRE * vector) / HALF_RANGE

    def one_orbital(orb_index, density):
        orbital = random_orbitals[orb_index].astype(jnp.float32)
        first_term = apply_hamiltonian(orbital)
        second_term = 2.0 * apply_hamiltonian(first_term) - orbital
        filtered = cheb_coef[0] * orbital + cheb_coef[1] * first_term + cheb_coef[2] * second_term
        return density + filtered * filtered

    density = lax.fori_loop(0, NSTOCH, one_orbital, jnp.zeros((NZ, NY, NX), jnp.float32))
    return density / NSTOCH
```

```python
import functools
import math

import jax
import jax.numpy as jnp
from jax import lax
from jax.experimental import pallas as pl
from jax.experimental.pallas import tpu as pltpu
from jax.sharding import PartitionSpec as P

REACH = 3
WIDE = 2 * REACH + 1
STRIDE = 16
PRECISE = lax.Precision.HIGHEST
CHUNKS = 2


def kinetic_table(length):
    places = jnp.arange(length)
    offset = places[:, None] - places[None, :]
    parity = jnp.where(offset % 2 == 0, 1.0, -1.0).astype(jnp.float32)
    angle_half = offset.astype(jnp.float32) * (math.pi / length)
    sine = jnp.where(offset == 0, 1.0, jnp.sin(angle_half))
    off_diag = parity / (2.0 * sine * sine)
    on_diag = jnp.float32(length * length / 12.0 + 1.0 / 6.0)
    return jnp.where(offset == 0, on_diag, off_diag) * (4.0 / (length * length))


def xor_route(size, bit):
    return [(i, i ^ bit) for i in range(size)]


def xor_bits(size):
    bits = []
    bit = size // 2
    while bit:
        bits.append(bit)
        bit //= 2
    return bits


def sum_over(block, axis):
    size = lax.axis_size(axis)
    for bit in xor_bits(size):
        block = block + lax.ppermute(block, axis, xor_route(size, bit))
    return block


def gather_over(block, axis):
    size = lax.axis_size(axis)
    place = lax.axis_index(axis)
    shape = block.shape
    bits = xor_bits(size)
    for bit in bits:
        other = lax.ppermute(block, axis, xor_route(size, bit))
        upper = (place & bit) != 0
        block = jnp.stack([jnp.where(upper, other, block), jnp.where(upper, block, other)])
    count = len(bits)
    block = jnp.transpose(block, tuple(range(count))[::-1] + tuple(range(count, block.ndim)))
    return block.reshape((size * shape[0],) + shape[1:])


def exchange(block, axis):
    return lax.all_to_all(block, axis, split_axis=0, concat_axis=0, tiled=True)


def window_tiles(starts, corner, atom, total, field_shape):
    planes, tiles = field_shape[0], field_shape[1]
    all_planes, all_tiles = total
    z_start, y_start, x_start = starts[atom, 0], starts[atom, 1], starts[atom, 2]
    z_ahead = lax.rem(z_start - corner[0] + all_planes, all_planes)
    z_behind = lax.rem(corner[0] - z_start + all_planes, all_planes)
    first = lax.rem(y_start // 8 - corner[1] + all_tiles, all_tiles)
    second = lax.rem(first + 1, all_tiles)
    rows = [(jnp.minimum(t, tiles - 1), t < tiles) for t in (first, second)]
    here = ((z_ahead < planes) | (z_behind < WIDE)) & (rows[0][1] | rows[1][1])
    depth = []
    for dz in range(WIDE):
        z = lax.rem(z_ahead + dz, all_planes)
        depth.append((jnp.minimum(z, planes - 1), z < planes))
    return here, depth, rows, y_start % 8, x_start


def pick_kernel(total, starts, corner, spots, field, values):
    values[...] = jnp.zeros_like(values)
    columns = field.shape[3]
    lane = lax.broadcasted_iota(jnp.int32, (8, 128), 1)
    row = lax.broadcasted_iota(jnp.int32, (8, 128), 0)
    slot = lax.broadcasted_iota(jnp.int32, (128, 128), 0)

    def one(atom, carry):
        here, depth, rows, shift, x_start = window_tiles(starts, corner, atom, total, field.shape)

        @pl.when(here)
        def _():
            halves = []
            for tile, row_in in rows:
                half = jnp.zeros((8, 128), jnp.float32)
                for dz, (z, z_in) in enumerate(depth):
                    turn = lax.rem(STRIDE * dz - x_start + columns, columns)
                    turned = pltpu.roll(field[z, tile], turn, 1)[:, :128]
                    mine = (lane >= STRIDE * dz) & (lane < STRIDE * dz + WIDE)
                    half = jnp.where(mine & (row_in & z_in), turned, half)
                halves.append(half)
            both = pltpu.roll(jnp.concatenate(halves, axis=0), lax.rem(16 - shift, 16), 0)[:8]
            spot = spots[atom]
            chosen = (slot == spot[1:2]).astype(jnp.float32)
            found = jnp.dot(both, chosen, precision=PRECISE, preferred_element_type=jnp.float32)
            found = jnp.where(row == spot[0:1], found, 0.0)
            values[pl.ds(atom, 1)] = jnp.sum(found, axis=0, keepdims=True)[None]

        return carry

    lax.fori_loop(0, values.shape[0], one, 0)


def put_kernel(total, starts, corner, spots, spread, base, field):
    field[...] = base[...]
    columns = field.shape[3]
    lane = lax.broadcasted_iota(jnp.int32, (8, 128), 1)
    row = lax.broadcasted_iota(jnp.int32, (8, 128), 0)
    slot = lax.broadcasted_iota(jnp.int32, (128, 128), 0)
    empty = jnp.zeros((8, columns - 128), jnp.float32)

    def one(atom, carry):
        here, depth, rows, shift, x_start = window_tiles(starts, corner, atom, total, field.shape)

        @pl.when(here)
        def _():
            spot = spots[atom]
            chosen = (slot == spot[1:2]).astype(jnp.float32)
            amounts = jnp.where(row == spot[0:1], spread[atom], 0.0)
            window = lax.dot_general(
                amounts,
                chosen,
                (((1,), (1,)), ((), ())),
                precision=PRECISE,
                preferred_element_type=jnp.float32,
            )
            both = pltpu.roll(jnp.concatenate([window, jnp.zeros_like(window)], axis=0), shift, 0)
            for half, (tile, row_in) in enumerate(rows):
                part = both[8 * half : 8 * half + 8]
                for dz, (z, z_in) in enumerate(depth):

                    @pl.when(row_in & z_in)
                    def _():
                        mine = (lane >= STRIDE * dz) & (lane < STRIDE * dz + WIDE)
                        piece = jnp.concatenate([jnp.where(mine, part, 0.0), empty], axis=1)
                        turn = lax.rem(x_start - STRIDE * dz + columns, columns)
                        field[z, tile] += pltpu.roll(piece, turn, 1)

        return carry

    lax.fori_loop(0, spread.shape[0], one, 0)


def tiled(field):
    return field.reshape(field.shape[0], field.shape[1] // 8, 8, field.shape[2])


SMEM = pl.BlockSpec(memory_space=pltpu.SMEM)
VMEM = pl.BlockSpec(memory_space=pltpu.VMEM)
PARAMS = pltpu.CompilerParams(vmem_limit_bytes=48 * 2**20)


def pick(total, starts, corner, spots, field):
    return pl.pallas_call(
        functools.partial(pick_kernel, total),
        out_shape=jax.ShapeDtypeStruct((starts.shape[0], 1, 128), jnp.float32),
        in_specs=[SMEM, SMEM, VMEM, VMEM],
        out_specs=VMEM,
        compiler_params=PARAMS,
        cost_estimate=pl.CostEstimate(flops=1 << 24, bytes_accessed=1 << 23, transcendentals=0),
        name="pick",
    )(starts, corner, spots, tiled(field))


def put(total, starts, corner, spots, spread, base):
    shaped = tiled(base)
    return pl.pallas_call(
        functools.partial(put_kernel, total),
        out_shape=jax.ShapeDtypeStruct(shaped.shape, jnp.float32),
        in_specs=[SMEM, SMEM, VMEM, VMEM, VMEM],
        out_specs=VMEM,
        compiler_params=PARAMS,
        cost_estimate=pl.CostEstimate(flops=1 << 24, bytes_accessed=1 << 23, transcendentals=0),
        name="put",
    )(starts, corner, spots, spread, shaped).reshape(base.shape)


def atom_windows(cells, all_planes, rows_y, cols_x):
    parts = []
    for coords, size in (
        (cells[:, 0], all_planes),
        (cells[:, 1] // cols_x, rows_y),
        (cells[:, 1] % cols_x, cols_x),
    ):
        anchor = coords[:, :1]
        apart = (coords - anchor + size // 2) % size - size // 2
        least = jnp.min(apart, axis=1, keepdims=True)
        parts.append(((anchor + least) % size, apart - least))
    starts = jnp.concatenate([start for start, _ in parts], axis=1)
    (_, off_z), (_, off_y), (_, off_x) = parts
    spots = jnp.stack([off_y, off_z * STRIDE + off_x], axis=1)
    return starts.astype(jnp.int32), spots.astype(jnp.int32)


def local(random_orbitals, potential, sphere_cells, projectors, kb_energy, cheb_coef):
    grid_count = lax.axis_size("grid")
    grid_pos = lax.axis_index("grid")
    orb_groups = lax.axis_size("orb")
    orb_pos = lax.axis_index("orb")
    planes, rows_y, cols_x = potential.shape
    all_planes = planes * grid_count
    rows = rows_y // grid_count
    orb_count = random_orbitals.shape[0]
    kinetic_x = kinetic_table(cols_x)
    kinetic_y = kinetic_table(rows_y)
    kinetic_z = kinetic_table(all_planes)
    c0, c1, c2 = cheb_coef[0], cheb_coef[1], cheb_coef[2]
    c1_4 = c1 / 4.0
    c2_8 = c2 / 8.0

    def to_blocks(field):
        wide = field.shape[2]
        parts = field.reshape(planes, grid_count, rows, wide).transpose(1, 0, 2, 3)
        return exchange(parts, "grid").reshape(all_planes, rows, wide)

    def to_slab(field):
        wide = field.shape[2]
        parts = exchange(field.reshape(grid_count, planes, rows, wide), "grid")
        return parts.transpose(1, 0, 2, 3).reshape(planes, rows_y, wide)

    def in_plane(field):
        along_x = jnp.dot(field.reshape(-1, cols_x), kinetic_x, precision=PRECISE).reshape(field.shape)
        return along_x + jnp.einsum("zyx,yw->zwx", field, kinetic_y, precision=PRECISE)

    def along_z(field):
        return jnp.einsum("wz,zyx->wyx", kinetic_z, field, precision=PRECISE)

    raw = jnp.concatenate([sphere_cells.astype(jnp.float32), projectors], axis=1)
    raw = gather_over(raw, "grid")
    cells = raw[:, :2].astype(jnp.int32)
    projs = raw[:, 2:]
    starts, spots = atom_windows(cells, all_planes, rows_y, cols_x)
    total = (all_planes, rows_y // 8)
    slab_corner = jnp.stack([grid_pos * planes, jnp.zeros_like(grid_pos)]).astype(jnp.int32)
    first_row = grid_pos * rows
    block_corner = jnp.stack([jnp.zeros_like(grid_pos), first_row // 8]).astype(jnp.int32)

    def pick_slab(field):
        return pick(total, starts, slab_corner, spots, field)

    def pick_block(field):
        if rows % 8:
            padded = jnp.zeros((all_planes, -(-rows // 8) * 8, cols_x), jnp.float32)
            field = lax.dynamic_update_slice(padded, field, (0, first_row % 8, 0))
        return pick(total, starts, block_corner, spots, field)

    def amounts(values):
        coeffs = jnp.einsum("aj,apj->ap", values[:, 0], projs, precision=PRECISE)
        coeffs = sum_over(coeffs, "grid") * kb_energy
        return jnp.einsum("ap,apj->aj", coeffs, projs, precision=PRECISE)[:, None]

    def put_slab(spread, base):
        return put(total, starts, slab_corner, spots, spread, base)

    part = cols_x // orb_groups

    def shared_blocks(after):
        mine = lax.dynamic_slice_in_dim(potential, orb_pos * part, part, axis=2)
        mine, after = lax.optimization_barrier((mine, after))
        got = to_blocks(mine)
        got = gather_over(got[None], "orb")
        return jnp.moveaxis(got, 0, 2).reshape(all_planes, rows, cols_x), after

    wide = cols_x // CHUNKS
    pieces = [[] for _ in range(CHUNKS)]
    block_potential = None
    for orb in range(orb_count):
        v = random_orbitals[orb]
        v_block = to_blocks(v)
        if block_potential is None:
            block_potential, v_block = shared_blocks(v_block)
        pv = in_plane(v)
        u = put_slab(amounts(pick_slab(v)), pv + (potential - 2.0) * v)
        g = pv + u
        a = along_z(v_block)
        bu = in_plane(u) + (potential - 2.0) * u
        base = (c0 - c2) * v + c1_4 * u + c2_8 * bu
        q = put_slab(c2_8 * amounts(pick_slab(u) + pick_block(a)), base)
        for i in range(CHUNKS):
            cols = slice(i * wide, (i + 1) * wide)
            g_block = to_blocks(g[:, :, cols])
            a_i = a[:, :, cols]
            m = along_z(c1_4 * v_block[:, :, cols] + c2_8 * (g_block + a_i))
            m = m + c2_8 * (block_potential[:, :, cols] - 2.0) * a_i
            filtered = q[:, :, cols] + to_slab(m)
            pieces[i].append(filtered * filtered)
    out = []
    for parts in pieces:
        own = functools.reduce(jnp.add, parts)
        out.append(sum_over(own, "orb") * (1.0 / (orb_count * orb_groups)))
    return jnp.concatenate(out, axis=2)


def solution(mesh):
    in_specs = (
        P("orb", "grid", None, None),
        P("grid", None, None),
        P("grid", None, None),
        P("grid", None, None),
        P(),
        P(),
    )
    out_specs = P("grid", None, None)
    return jax.shard_map(local, mesh=mesh, in_specs=in_specs, out_specs=out_specs, check_vma=False)
```

```python
import functools
import math

import jax
import jax.numpy as jnp
from jax import lax
from jax.experimental import pallas as pl
from jax.experimental.pallas import tpu as pltpu
from jax.sharding import PartitionSpec as P

REACH = 3
WIDE = 2 * REACH + 1
STRIDE = 16
PRECISE = lax.Precision.HIGHEST
TOGETHER = 4


def kinetic_table(length):
    places = jnp.arange(length)
    offset = places[:, None] - places[None, :]
    parity = jnp.where(offset % 2 == 0, 1.0, -1.0).astype(jnp.float32)
    angle_half = offset.astype(jnp.float32) * (math.pi / length)
    sine = jnp.where(offset == 0, 1.0, jnp.sin(angle_half))
    off_diag = parity / (2.0 * sine * sine)
    on_diag = jnp.float32(length * length / 12.0 + 1.0 / 6.0)
    return jnp.where(offset == 0, on_diag, off_diag) * (4.0 / (length * length))


def xor_route(size, bit):
    return [(i, i ^ bit) for i in range(size)]


def xor_bits(size):
    bits = []
    bit = size // 2
    while bit:
        bits.append(bit)
        bit //= 2
    return bits


def sum_over(block, axis):
    size = lax.axis_size(axis)
    for bit in xor_bits(size):
        block = block + lax.ppermute(block, axis, xor_route(size, bit))
    return block


def gather_over(block, axis):
    size = lax.axis_size(axis)
    place = lax.axis_index(axis)
    shape = block.shape
    bits = xor_bits(size)
    for bit in bits:
        other = lax.ppermute(block, axis, xor_route(size, bit))
        upper = (place & bit) != 0
        block = jnp.stack([jnp.where(upper, other, block), jnp.where(upper, block, other)])
    count = len(bits)
    block = jnp.transpose(block, tuple(range(count))[::-1] + tuple(range(count, block.ndim)))
    return block.reshape((size * shape[0],) + shape[1:])


def trade(blocks, axis):
    size = lax.axis_size(axis)
    place = lax.axis_index(axis)
    out = blocks
    for apart in range(1, size):
        sent = lax.dynamic_index_in_dim(blocks, place ^ apart, 0)
        got = lax.ppermute(sent, axis, xor_route(size, apart))
        out = lax.dynamic_update_slice_in_dim(out, got, place ^ apart, 0)
    return out


def exchange(block, axis):
    return lax.all_to_all(block, axis, split_axis=0, concat_axis=0, tiled=True)


def listed(starts, corner, first, limit, total, planes, tiles, listing):
    all_planes, all_tiles = total

    def one(k, count):
        atom = lax.rem(first + k, starts.shape[0])
        ahead = lax.rem(starts[atom, 0] - corner[0] + all_planes, all_planes)
        behind = lax.rem(corner[0] - starts[atom, 0] + all_planes, all_planes)
        tile = lax.rem(starts[atom, 1] // 8 - corner[1] + all_tiles, all_tiles)
        here = ((ahead < planes) | (behind < WIDE)) & ((tile < tiles) | (tile == all_tiles - 1))
        listing[count] = atom
        return count + here.astype(jnp.int32)

    return lax.fori_loop(0, limit, one, jnp.int32(0))


def split3(block):
    high = block.astype(jnp.bfloat16).astype(jnp.float32)
    rest = block - high
    middle = rest.astype(jnp.bfloat16).astype(jnp.float32)
    return jnp.concatenate([high, middle, rest - middle], axis=0).astype(jnp.bfloat16)


def placed(starts, corner, total, atom, planes, tiles, columns, lane):
    all_planes, all_tiles = total
    z_start, y_start, x_start = starts[atom, 0], starts[atom, 1], starts[atom, 2]
    ahead = lax.rem(z_start - corner[0] + all_planes, all_planes)
    depth = [jnp.minimum(lax.rem(ahead + dz, all_planes), planes - 1) for dz in range(WIDE)]
    z_in = lax.rem(ahead + lane // STRIDE, all_planes) < planes
    first = lax.rem(y_start // 8 - corner[1] + all_tiles, all_tiles)
    tile_pair = (first, lax.rem(first + 1, all_tiles))
    lane_pair = (x_start // 128, lax.rem(x_start // 128 + 1, columns // 128))
    return depth, z_in, tile_pair, lane_pair, lax.rem(y_start, 8), lax.rem(x_start, 128)


def corner_of(z, tile, group):
    return z, tile, slice(None), pl.ds(pl.multiple_of(group * 128, 128), 128)


def pick_kernel(total, limit, first, starts, corner, spots, field, values, listing):
    values[...] = jnp.zeros_like(values)
    planes, tiles, _, columns = field.shape
    lane = lax.broadcasted_iota(jnp.int32, (8, 128), 1)
    row = lax.broadcasted_iota(jnp.int32, (8, 128), 0)
    slot = lax.broadcasted_iota(jnp.int32, (128, 128), 0)
    count = listed(starts, corner, first[0], limit, total, planes, tiles, listing)

    def some(group, carry):
        for k in range(TOGETHER):
            atom = listing[jnp.minimum(group * TOGETHER + k, count - 1)]
            depth, z_in, tile_pair, groups, down, right = placed(
                starts, corner, total, atom, planes, tiles, columns, lane
            )
            t0, t1 = (jnp.minimum(t, tiles - 1) for t in tile_pair)
            window = jnp.zeros((8, 128), jnp.float32)
            for dz, z in enumerate(depth):
                upper = jnp.where(lane >= right, field[corner_of(z, t0, groups[0])], field[corner_of(z, t0, groups[1])])
                lower = jnp.where(lane >= right, field[corner_of(z, t1, groups[0])], field[corner_of(z, t1, groups[1])])
                met = jnp.where(row >= down, upper, lower)
                met = pltpu.roll(met, lax.rem(STRIDE * dz - right + 128, 128), 1)
                window = jnp.where(lane // STRIDE == dz, met, window)
            window = pltpu.roll(window, lax.rem(8 - down, 8), 0)
            tile_of = jnp.where(row < 8 - down, tile_pair[0], tile_pair[1])
            window = jnp.where(z_in & (tile_of < tiles), window, 0.0)
            spot = spots[atom]
            chosen = (slot == spot[1:2]).astype(jnp.float32).astype(jnp.bfloat16)
            found = jnp.dot(split3(window), chosen, preferred_element_type=jnp.float32)
            found = found[0:8] + found[8:16] + found[16:24]
            found = jnp.where(row == spot[0:1], found, 0.0)
            values[pl.ds(atom, 1)] = jnp.sum(found, axis=0, keepdims=True)[None]
        return carry

    lax.fori_loop(0, (count + TOGETHER - 1) // TOGETHER, some, 0)


def put_kernel(total, limit, first, starts, corner, spots, spread, base, field, listing):
    field[...] = base[...]
    planes, tiles, _, columns = field.shape
    lane = lax.broadcasted_iota(jnp.int32, (8, 128), 1)
    row = lax.broadcasted_iota(jnp.int32, (8, 128), 0)
    slot = lax.broadcasted_iota(jnp.int32, (128, 128), 0)
    count = listed(starts, corner, first[0], limit, total, planes, tiles, listing)

    def some(group, carry):
        for k in range(TOGETHER):
            at = group * TOGETHER + k
            atom = listing[jnp.minimum(at, count - 1)]
            depth, z_in, (t0, t1), groups, down, right = placed(
                starts, corner, total, atom, planes, tiles, columns, lane
            )
            spot = spots[atom]
            chosen = (slot == spot[1:2]).astype(jnp.float32).astype(jnp.bfloat16)
            amounts = jnp.where(row == spot[0:1], spread[atom], 0.0)
            window = lax.dot_general(
                split3(amounts), chosen, (((1,), (1,)), ((), ())), preferred_element_type=jnp.float32
            )
            window = window[0:8] + window[8:16] + window[16:24]
            window = jnp.where(z_in & (at < count), window, 0.0)
            window = pltpu.roll(window, down, 0)
            for dz, z in enumerate(depth):
                part = jnp.where(lane // STRIDE == dz, window, 0.0)
                part = pltpu.roll(part, lax.rem(right - STRIDE * dz + 128, 128), 1)
                places = [corner_of(z, t, g) for t in (t0, t1) for g in groups]
                before = [field[place] for place in places]
                for i, place in enumerate(places):
                    inside = ((row >= down) if i < 2 else (row < down)) & (
                        (lane >= right) if i % 2 == 0 else (lane < right)
                    )
                    field[place] = before[i] + jnp.where(inside, part, 0.0)
        return carry

    lax.fori_loop(0, (count + TOGETHER - 1) // TOGETHER, some, 0)


def planar_kernel(weights, field, extra, potential, table, low_table, first_out, second_out):
    block = field[0]
    high = block.astype(jnp.bfloat16)
    low = (block - high.astype(jnp.float32)).astype(jnp.bfloat16)

    def times(left, right):
        return jnp.dot(left, right, preferred_element_type=jnp.float32)

    kin = times(high, table[0]) + (times(high, low_table[0]) + times(low, table[0]))
    kin = kin + (times(table[1], high) + (times(low_table[1], high) + times(table[1], low)))
    total = kin + (potential[0] - 2.0) * block
    first_out[0] = weights[0] * kin + weights[1] * block + weights[2] * extra[0]
    second_out[0] = weights[3] * total + weights[4] * block + weights[5] * extra[0]


def tiled(field):
    return field.reshape(field.shape[0], field.shape[1] // 8, 8, field.shape[2])


SMEM = pl.BlockSpec(memory_space=pltpu.SMEM)
VMEM = pl.BlockSpec(memory_space=pltpu.VMEM)
PARAMS = pltpu.CompilerParams(vmem_limit_bytes=48 * 2**20)


def pick(total, limit, first, starts, corner, spots, field):
    return pl.pallas_call(
        functools.partial(pick_kernel, total, limit),
        out_shape=jax.ShapeDtypeStruct((starts.shape[0], 1, 128), jnp.float32),
        in_specs=[SMEM, SMEM, SMEM, VMEM, VMEM],
        out_specs=VMEM,
        scratch_shapes=[pltpu.SMEM((limit + 1,), jnp.int32)],
        compiler_params=PARAMS,
        cost_estimate=pl.CostEstimate(flops=1 << 24, bytes_accessed=1 << 24, transcendentals=0),
        name="pick",
    )(first, starts, corner, spots, tiled(field))


def put(total, limit, first, starts, corner, spots, spread, base):
    shaped = tiled(base)
    return pl.pallas_call(
        functools.partial(put_kernel, total, limit),
        out_shape=jax.ShapeDtypeStruct(shaped.shape, jnp.float32),
        in_specs=[SMEM, SMEM, SMEM, VMEM, VMEM, VMEM],
        out_specs=VMEM,
        scratch_shapes=[pltpu.SMEM((limit + 1,), jnp.int32)],
        compiler_params=PARAMS,
        cost_estimate=pl.CostEstimate(flops=1 << 24, bytes_accessed=1 << 24, transcendentals=0),
        name="put",
    )(first, starts, corner, spots, spread, shaped).reshape(base.shape)


def halves_of(table):
    high = lax.reduce_precision(table, 8, 7)
    return high.astype(jnp.bfloat16), (table - high).astype(jnp.bfloat16)


def planar(weights, field, extra, potential, kinetic_x, kinetic_y):
    planes, rows_y, cols_x = field.shape
    assert rows_y == cols_x
    highs, lows = zip(halves_of(kinetic_x), halves_of(kinetic_y))
    plane = pl.BlockSpec((1, rows_y, cols_x), lambda z: (z, 0, 0))
    tables = pl.BlockSpec((2, rows_y, cols_x), lambda z: (0, 0, 0))
    return pl.pallas_call(
        planar_kernel,
        grid=(planes,),
        out_shape=[jax.ShapeDtypeStruct(field.shape, jnp.float32)] * 2,
        in_specs=[SMEM, plane, plane, plane, tables, tables],
        out_specs=[plane, plane],
        compiler_params=PARAMS,
        cost_estimate=pl.CostEstimate(
            flops=12 * planes * rows_y * cols_x * (rows_y + cols_x) // 2,
            bytes_accessed=20 * planes * rows_y * cols_x,
            transcendentals=0,
        ),
        name="planar",
    )(weights, field, extra, potential, jnp.stack(highs), jnp.stack(lows))


def atom_windows(cells, all_planes, rows_y, cols_x):
    parts = []
    for coords, size in (
        (cells[:, 0], all_planes),
        (cells[:, 1] // cols_x, rows_y),
        (cells[:, 1] % cols_x, cols_x),
    ):
        anchor = coords[:, :1]
        apart = (coords - anchor + size // 2) % size - size // 2
        least = jnp.min(apart, axis=1, keepdims=True)
        parts.append(((anchor + least) % size, apart - least))
    starts = jnp.concatenate([start for start, _ in parts], axis=1)
    (_, off_z), (_, off_y), (_, off_x) = parts
    spots = jnp.stack([off_y, off_z * STRIDE + off_x], axis=1)
    return starts.astype(jnp.int32), spots.astype(jnp.int32)


def after(value, *others):
    return lax.optimization_barrier((value,) + others)[0]


def local(random_orbitals, potential, sphere_cells, projectors, kb_energy, cheb_coef):
    grid_count = lax.axis_size("grid")
    grid_pos = lax.axis_index("grid")
    orb_groups = lax.axis_size("orb")
    orb_pos = lax.axis_index("orb")
    planes, rows_y, cols_x = potential.shape
    all_planes = planes * grid_count
    rows = rows_y // grid_count
    orb_count = random_orbitals.shape[0]
    per_dev = sphere_cells.shape[0]
    atoms = per_dev * grid_count
    chunks = 2 if rows % 16 == 0 else 1
    some_rows = rows // chunks
    part = cols_x // orb_groups
    kinetic_x = kinetic_table(cols_x)
    kinetic_y = kinetic_table(rows_y)
    kinetic_z = kinetic_table(all_planes)
    c0, c1, c2 = cheb_coef[0], cheb_coef[1], cheb_coef[2]
    c1_4 = c1 / 4.0
    c2_8 = c2 / 8.0

    def to_blocks(field):
        got = exchange(field.transpose(1, 0, 2, 3), "grid")
        return got.reshape((all_planes,) + field.shape[2:])

    def along_z(field):
        return jnp.einsum("wz,zyx->wyx", kinetic_z, field, precision=PRECISE)

    raw = jnp.concatenate([sphere_cells.astype(jnp.float32), projectors], axis=1)
    raw = gather_over(raw, "grid")
    cells = raw[:, :2].astype(jnp.int32)
    projs = raw[:, 2:]
    starts, spots = atom_windows(cells, all_planes, rows_y, cols_x)
    total = (all_planes, rows_y // 8)
    zero = jnp.zeros_like(grid_pos)
    slab_corner = jnp.stack([grid_pos * planes, zero])
    first_row = grid_pos * rows
    block_corner = jnp.stack([zero, first_row // 8])
    near = min(3 * per_dev, atoms)
    near_first = ((grid_pos + grid_count - 1) * per_dev % atoms)[None]

    def pick_slab(field):
        return pick(total, near, near_first, starts, slab_corner, spots, field)

    def pick_block(field):
        if rows % 8:
            padded = jnp.zeros((all_planes, -(-rows // 8) * 8, cols_x), jnp.float32)
            field = lax.dynamic_update_slice(padded, field, (0, first_row % 8, 0))
        return pick(total, atoms, zero[None], starts, block_corner, spots, field)

    def amounts(values):
        coeffs = jnp.einsum("aj,apj->ap", values[:, 0], projs, precision=PRECISE)
        coeffs = sum_over(coeffs, "grid") * kb_energy
        return jnp.einsum("ap,apj->aj", coeffs, projs, precision=PRECISE)[:, None]

    def put_slab(spread, base):
        return put(total, near, near_first, starts, slab_corner, spots, spread, base)

    def cut(field):
        return field.reshape(planes, grid_count, rows, field.shape[2])

    block_potential = None
    sums = [0.0] * chunks
    for orb in range(orb_count):
        v = random_orbitals[orb]
        v_block = to_blocks(cut(v))
        if block_potential is None:
            mine = lax.dynamic_slice_in_dim(potential, orb_pos * part, part, axis=2)
            got = to_blocks(cut(after(mine, v_block)))
            got = gather_over(got[None], "orb")
            block_potential = jnp.moveaxis(got, 0, 2).reshape(all_planes, rows, cols_x)
        one = jnp.ones((), jnp.float32)
        none = jnp.zeros((), jnp.float32)
        pv, t = planar(jnp.stack([one, none, none, one, none, none]), v, v, potential, kinetic_x, kinetic_y)
        u = put_slab(amounts(pick_slab(v)), t)
        g = pv + u
        a = along_z(v_block)
        _, base = planar(jnp.stack([none, none, none, c2_8, c1_4, c0 - c2]), u, v, potential, kinetic_x, kinetic_y)
        q = put_slab(c2_8 * amounts(pick_slab(u) + pick_block(a)), base)
        q = q.reshape(planes, rows_y, orb_groups, part)
        q_all = trade(jnp.moveaxis(q, 2, 0), "orb")
        q_all = q_all.reshape(orb_groups, planes, grid_count, chunks, some_rows, part)
        c_block = c1_4 * v_block + c2_8 * a
        b_block = c2_8 * (block_potential - 2.0) * a
        ms = []
        for i in range(chunks):
            lines = slice(i * some_rows, (i + 1) * some_rows)
            send = cut(g)[:, :, lines]
            if i == 0:
                send = after(send, c_block)
            g_block = to_blocks(send)
            ms.append(along_z(c_block[:, lines] + c2_8 * g_block) + b_block[:, lines])
        for i in range(chunks):
            m = ms[i]
            if i > 0:
                m = after(m, q_all)
            m = m.reshape(grid_count, planes, some_rows, orb_groups, part).transpose(3, 0, 1, 2, 4)
            m = m.reshape((orb_groups * grid_count,) + m.shape[2:])
            m = exchange(m, ("orb", "grid")).reshape(orb_groups, grid_count, planes, some_rows, part)
            filtered = q_all[:, :, :, i] + m.transpose(0, 2, 1, 3, 4)
            sums[i] = sums[i] + jnp.sum(filtered * filtered, axis=0)
    out = []
    for own in sums:
        own = own * (1.0 / (orb_count * orb_groups))
        out.append(jnp.moveaxis(gather_over(own[None], "orb"), 0, 3))
    return jnp.stack(out, axis=2).reshape(planes, rows_y, cols_x)


def solution(mesh):
    in_specs = (
        P("orb", "grid", None, None),
        P("grid", None, None),
        P("grid", None, None),
        P("grid", None, None),
        P(),
        P(),
    )
    out_specs = P("grid", None, None)
    return jax.shard_map(local, mesh=mesh, in_specs=in_specs, out_specs=out_specs, check_vma=False)
```

```python
import functools
import math

import jax
import jax.numpy as jnp
from jax import lax
from jax.experimental import pallas as pl
from jax.experimental.pallas import tpu as pltpu
from jax.sharding import PartitionSpec as P

REACH = 3
WIDE = 2 * REACH + 1
STRIDE = 16
PRECISE = lax.Precision.HIGHEST
TOGETHER = 4


def kinetic_table(length):
    places = jnp.arange(length)
    offset = places[:, None] - places[None, :]
    parity = jnp.where(offset % 2 == 0, 1.0, -1.0).astype(jnp.float32)
    angle_half = offset.astype(jnp.float32) * (math.pi / length)
    sine = jnp.where(offset == 0, 1.0, jnp.sin(angle_half))
    off_diag = parity / (2.0 * sine * sine)
    on_diag = jnp.float32(length * length / 12.0 + 1.0 / 6.0)
    return jnp.where(offset == 0, on_diag, off_diag) * (4.0 / (length * length))


def xor_route(size, bit):
    return [(i, i ^ bit) for i in range(size)]


def xor_bits(size):
    bits = []
    bit = size // 2
    while bit:
        bits.append(bit)
        bit //= 2
    return bits


def after(value, *others):
    return lax.optimization_barrier((value,) + others)[0]


def gather_steps(block, axis, waits=()):
    size = lax.axis_size(axis)
    place = lax.axis_index(axis)
    shape = block.shape
    bits = xor_bits(size)
    for i, bit in enumerate(bits):
        if i < len(waits) and waits[i] is not None:
            block = after(block, waits[i])
        other = lax.ppermute(block, axis, xor_route(size, bit))
        upper = (place & bit) != 0
        block = jnp.stack([jnp.where(upper, other, block), jnp.where(upper, block, other)])
    count = len(bits)
    block = jnp.transpose(block, tuple(range(count))[::-1] + tuple(range(count, block.ndim)))
    return block.reshape((size * shape[0],) + shape[1:])


def trade(blocks, axis):
    size = lax.axis_size(axis)
    place = lax.axis_index(axis)
    out = blocks
    for apart in range(1, size):
        sent = lax.dynamic_index_in_dim(blocks, place ^ apart, 0)
        got = lax.ppermute(sent, axis, xor_route(size, apart))
        out = lax.dynamic_update_slice_in_dim(out, got, place ^ apart, 0)
    return out


def exchange(block, axis):
    return lax.all_to_all(block, axis, split_axis=0, concat_axis=0, tiled=True)


def listed(starts, corner, total, planes, tiles, listing):
    all_planes, all_tiles, _ = total

    def one(atom, count):
        ahead = lax.rem(starts[atom, 0] - corner[0] + all_planes, all_planes)
        behind = lax.rem(corner[0] - starts[atom, 0] + all_planes, all_planes)
        tile = lax.rem(starts[atom, 1] // 8 - corner[1] + all_tiles, all_tiles)
        here = ((ahead < planes) | (behind < WIDE)) & ((tile < tiles) | (tile == all_tiles - 1))
        listing[count] = atom
        return count + here.astype(jnp.int32)

    return lax.fori_loop(0, starts.shape[0], one, jnp.int32(0))


def split3(block):
    high = block.astype(jnp.bfloat16).astype(jnp.float32)
    rest = block - high
    middle = rest.astype(jnp.bfloat16).astype(jnp.float32)
    return jnp.concatenate([high, middle, rest - middle], axis=0).astype(jnp.bfloat16)


def placed(starts, corner, total, atom, planes, tiles, lane):
    all_planes, all_tiles, all_groups = total
    z_start, y_start, x_start = starts[atom, 0], starts[atom, 1], starts[atom, 2]
    ahead = lax.rem(z_start - corner[0] + all_planes, all_planes)
    depth = [jnp.minimum(lax.rem(ahead + dz, all_planes), planes - 1) for dz in range(WIDE)]
    z_in = lax.rem(ahead + lane // STRIDE, all_planes) < planes
    first = lax.rem(y_start // 8 - corner[1] + all_tiles, all_tiles)
    tile_pair = (first, lax.rem(first + 1, all_tiles))
    lane_pair = (x_start // 128, lax.rem(x_start // 128 + 1, all_groups))
    return depth, z_in, tile_pair, lane_pair, lax.rem(y_start, 8), lax.rem(x_start, 128)


def corner_of(z, tile, group):
    return z, tile, slice(None), pl.ds(pl.multiple_of(group * 128, 128), 128)


def pick_kernel(total, grouped, starts, corner, spots, field, values, listing):
    values[...] = jnp.zeros_like(values)
    planes, tiles = (field.shape[1], 1) if grouped else field.shape[:2]

    def at(z, tile, group):
        return field[group, z] if grouped else field[corner_of(z, tile, group)]

    lane = lax.broadcasted_iota(jnp.int32, (8, 128), 1)
    row = lax.broadcasted_iota(jnp.int32, (8, 128), 0)
    slot = lax.broadcasted_iota(jnp.int32, (128, 128), 0)
    count = listed(starts, corner, total, planes, tiles, listing)

    def some(group, carry):
        for k in range(TOGETHER):
            atom = listing[jnp.minimum(group * TOGETHER + k, count - 1)]
            depth, z_in, tile_pair, groups, down, right = placed(
                starts, corner, total, atom, planes, tiles, lane
            )
            t0, t1 = (jnp.minimum(t, tiles - 1) for t in tile_pair)
            window = jnp.zeros((8, 128), jnp.float32)
            for dz, z in enumerate(depth):
                upper = jnp.where(lane >= right, at(z, t0, groups[0]), at(z, t0, groups[1]))
                lower = jnp.where(lane >= right, at(z, t1, groups[0]), at(z, t1, groups[1]))
                met = jnp.where(row >= down, upper, lower)
                met = pltpu.roll(met, lax.rem(STRIDE * dz - right + 128, 128), 1)
                window = jnp.where(lane // STRIDE == dz, met, window)
            window = pltpu.roll(window, lax.rem(8 - down, 8), 0)
            tile_of = jnp.where(row < 8 - down, tile_pair[0], tile_pair[1])
            window = jnp.where(z_in & (tile_of < tiles), window, 0.0)
            spot = spots[atom]
            chosen = (slot == spot[1:2]).astype(jnp.float32).astype(jnp.bfloat16)
            found = jnp.dot(split3(window), chosen, preferred_element_type=jnp.float32)
            found = found[0:8] + found[8:16] + found[16:24]
            found = jnp.where(row == spot[0:1], found, 0.0)
            values[pl.ds(atom, 1)] = jnp.sum(found, axis=0, keepdims=True)[None]
        return carry

    lax.fori_loop(0, (count + TOGETHER - 1) // TOGETHER, some, 0)


def put_kernel(total, starts, corner, spots, spread, base, field, listing):
    field[...] = base[...]
    planes, tiles = field.shape[:2]
    lane = lax.broadcasted_iota(jnp.int32, (8, 128), 1)
    row = lax.broadcasted_iota(jnp.int32, (8, 128), 0)
    slot = lax.broadcasted_iota(jnp.int32, (128, 128), 0)
    count = listed(starts, corner, total, planes, tiles, listing)

    def some(group, carry):
        for k in range(TOGETHER):
            at = group * TOGETHER + k
            atom = listing[jnp.minimum(at, count - 1)]
            depth, z_in, (t0, t1), groups, down, right = placed(
                starts, corner, total, atom, planes, tiles, lane
            )
            spot = spots[atom]
            chosen = (slot == spot[1:2]).astype(jnp.float32).astype(jnp.bfloat16)
            amounts = jnp.where(row == spot[0:1], spread[atom], 0.0)
            window = lax.dot_general(
                split3(amounts), chosen, (((1,), (1,)), ((), ())), preferred_element_type=jnp.float32
            )
            window = window[0:8] + window[8:16] + window[16:24]
            window = jnp.where(z_in & (at < count), window, 0.0)
            window = pltpu.roll(window, down, 0)
            for dz, z in enumerate(depth):
                part = jnp.where(lane // STRIDE == dz, window, 0.0)
                part = pltpu.roll(part, lax.rem(right - STRIDE * dz + 128, 128), 1)
                spans = range(field.shape[3] // 128)
                places = [(i, g, corner_of(z, t, g)) for i, t in enumerate((t0, t1)) for g in spans]
                before = [field[place] for _, _, place in places]
                for old, (i, g, place) in zip(before, places):
                    inside = (row < down) if i else (row >= down)
                    inside = inside & (jnp.where(lane >= right, groups[0], groups[1]) == g + corner[2])
                    field[place] = old + jnp.where(inside, part, 0.0)
        return carry

    lax.fori_loop(0, (count + TOGETHER - 1) // TOGETHER, some, 0)


def bf16_pair(block):
    high = block.astype(jnp.bfloat16)
    return high, (block - high.astype(jnp.float32)).astype(jnp.bfloat16)


def times(left, right):
    return jnp.dot(left, right, preferred_element_type=jnp.float32)


def in_plane(block, high_tables, low_tables):
    high, low = bf16_pair(block)
    kin = times(high, high_tables[0]) + (times(high, low_tables[0]) + times(low, high_tables[0]))
    return kin + (times(high_tables[1], high) + (times(low_tables[1], high) + times(high_tables[1], low)))


def first_kernel(field, potential, high_tables, low_tables, kin_out, all_out):
    block = field[0]
    kin = in_plane(block, high_tables, low_tables)
    kin_out[0] = kin
    all_out[0] = kin + (potential[0] - 2.0) * block


def second_kernel(weights, field, extra, potential, high_tables, low_tables, out):
    block = field[0]
    total = in_plane(block, high_tables, low_tables) + (potential[0] - 2.0) * block
    total = weights[0] * total + weights[1] * block + weights[2] * extra[0]
    part = out.shape[3]
    for i in range(out.shape[0]):
        out[i, 0] = total[:, i * part : (i + 1) * part]


def depth_times(high_table, low_table, block):
    high, low = bf16_pair(block)
    return times(high_table[...], high) + (times(low_table[...], high) + times(high_table[...], low))


def lines_of(ref, group, start, rows, planes, r):
    line = pl.ds(start + group * planes * rows + r, planes, stride=rows)
    return jnp.concatenate([ref[d, line, :] for d in range(ref.shape[0])], axis=0)


def out_kernel(rows, weights, field, potential, high_table, low_table, a_out, c_out, b_out):
    groups, everywhere = a_out.shape[0], high_table.shape[0]
    planes = everywhere // field.shape[0]

    def one(r, carry):
        v = jnp.concatenate([lines_of(field, g, 0, rows, planes, r) for g in range(groups)], axis=1)
        a = depth_times(high_table, low_table, v)
        for g in range(groups):
            cols = slice(128 * g, 128 * g + 128)
            well = lines_of(potential.at[g], 0, 0, rows, planes, r) - 2.0
            line = pl.ds(r, everywhere, stride=rows)
            a_out[g, line, :] = a[:, cols]
            c_out[g, line, :] = weights[0] * v[:, cols] + weights[1] * a[:, cols]
            b_out[g, line, :] = weights[1] * well * a[:, cols]
        return carry

    lax.fori_loop(0, rows, one, 0)


def back_kernel(rows, weights, g_in, c_in, b_in, high_table, low_table, out):
    groups, everywhere = out.shape[0], high_table.shape[0]
    planes = everywhere // g_in.shape[0]

    def one(r, carry):
        line = pl.ds(r, everywhere, stride=rows)
        parts = [
            c_in[g, line, :] + weights[1] * lines_of(g_in, g, 0, rows, planes, r) for g in range(groups)
        ]
        m = depth_times(high_table, low_table, jnp.concatenate(parts, axis=1))
        for g in range(groups):
            out[g, line, :] = m[:, 128 * g : 128 * g + 128] + b_in[g, line, :]
        return carry

    lax.fori_loop(0, rows, one, 0)


def tiled(field):
    return field.reshape(field.shape[0], field.shape[1] // 8, 8, field.shape[2])


SMEM = pl.BlockSpec(memory_space=pltpu.SMEM)
VMEM = pl.BlockSpec(memory_space=pltpu.VMEM)
PARAMS = pltpu.CompilerParams(vmem_limit_bytes=48 * 2**20)


def pick(total, starts, corner, spots, field, grouped=False):
    return pl.pallas_call(
        functools.partial(pick_kernel, total, grouped),
        out_shape=jax.ShapeDtypeStruct((starts.shape[0], 1, 128), jnp.float32),
        in_specs=[SMEM, SMEM, VMEM, VMEM],
        out_specs=VMEM,
        scratch_shapes=[pltpu.SMEM((starts.shape[0] + 1,), jnp.int32)],
        compiler_params=PARAMS,
        cost_estimate=pl.CostEstimate(flops=1 << 24, bytes_accessed=1 << 24, transcendentals=0),
        name="pick",
    )(starts, corner, spots, field if grouped else tiled(field))


def put(total, starts, corner, spots, spread, base):
    shaped = tiled(base)
    return pl.pallas_call(
        functools.partial(put_kernel, total),
        out_shape=jax.ShapeDtypeStruct(shaped.shape, jnp.float32),
        in_specs=[SMEM, SMEM, VMEM, VMEM, VMEM],
        out_specs=VMEM,
        scratch_shapes=[pltpu.SMEM((starts.shape[0] + 1,), jnp.int32)],
        compiler_params=PARAMS,
        cost_estimate=pl.CostEstimate(flops=1 << 24, bytes_accessed=1 << 24, transcendentals=0),
        name="put",
    )(starts, corner, spots, spread, shaped).reshape(base.shape)


def halves_of(table):
    high = lax.reduce_precision(table, 8, 7)
    return high.astype(jnp.bfloat16), (table - high).astype(jnp.bfloat16)


def plane_specs(shape):
    plane = pl.BlockSpec((1,) + shape[1:], lambda z: (z, 0, 0))
    return plane, pl.BlockSpec((2,) + shape[1:], lambda z: (0, 0, 0))


def cost(flops, numbers):
    return pl.CostEstimate(flops=flops, bytes_accessed=4 * numbers, transcendentals=0)


def planar_first(field, potential, tables):
    plane, pair = plane_specs(field.shape)
    return pl.pallas_call(
        first_kernel,
        grid=field.shape[:1],
        out_shape=[jax.ShapeDtypeStruct(field.shape, jnp.float32)] * 2,
        in_specs=[plane, plane, pair, pair],
        out_specs=[plane, plane],
        compiler_params=PARAMS,
        cost_estimate=cost(12 * field.shape[2] * field.size, 4 * field.size),
        name="planar_first",
    )(field, potential, *tables)


def planar_second(weights, field, extra, potential, tables, parts):
    plane, pair = plane_specs(field.shape)
    planes, rows_y, cols_x = field.shape
    shape = (parts, planes, rows_y, cols_x // parts)
    return pl.pallas_call(
        second_kernel,
        grid=field.shape[:1],
        out_shape=jax.ShapeDtypeStruct(shape, jnp.float32),
        in_specs=[SMEM, plane, plane, plane, pair, pair],
        out_specs=pl.BlockSpec((parts, 1) + shape[2:], lambda z: (0, z, 0, 0)),
        compiler_params=PARAMS,
        cost_estimate=cost(12 * field.shape[2] * field.size, 4 * field.size),
        name="planar_second",
    )(weights, field, extra, potential, *tables)


def depth_out(weights, field, potential, rows, tables):
    groups = potential.shape[0]
    lines = tables[0].shape[0] * rows
    return pl.pallas_call(
        functools.partial(out_kernel, rows),
        out_shape=[jax.ShapeDtypeStruct((groups, lines, 128), jnp.float32)] * 3,
        in_specs=[SMEM, VMEM, VMEM, VMEM, VMEM],
        out_specs=[VMEM] * 3,
        compiler_params=PARAMS,
        cost_estimate=cost(6 * tables[0].size * rows * groups * 128, 5 * groups * lines * 128),
        name="depth_out",
    )(weights, field, potential, *tables)


def depth_back(weights, g, c, b, rows, tables):
    return pl.pallas_call(
        functools.partial(back_kernel, rows),
        out_shape=jax.ShapeDtypeStruct(c.shape, jnp.float32),
        in_specs=[SMEM] + [VMEM] * 5,
        out_specs=VMEM,
        compiler_params=PARAMS,
        cost_estimate=cost(6 * tables[0].shape[0] * c.size, 4 * c.size),
        name="depth_back",
    )(weights, g, c, b, *tables)


def atom_windows(cells, all_planes, rows_y, cols_x):
    parts = []
    for coords, size in (
        (cells[:, 0], all_planes),
        (cells[:, 1] // cols_x, rows_y),
        (cells[:, 1] % cols_x, cols_x),
    ):
        anchor = coords[:, :1]
        apart = (coords - anchor + size // 2) % size - size // 2
        least = jnp.min(apart, axis=1, keepdims=True)
        parts.append(((anchor + least) % size, apart - least))
    starts = jnp.concatenate([start for start, _ in parts], axis=1)
    (_, off_z), (_, off_y), (_, off_x) = parts
    spots = jnp.stack([off_y, off_z * STRIDE + off_x], axis=1)
    return starts.astype(jnp.int32), spots.astype(jnp.int32)


def local(random_orbitals, potential, sphere_cells, projectors, kb_energy, cheb_coef):
    grid_count = lax.axis_size("grid")
    grid_pos = lax.axis_index("grid")
    orb_groups = lax.axis_size("orb")
    orb_pos = lax.axis_index("orb")
    planes, rows_y, cols_x = potential.shape
    all_planes = planes * grid_count
    rows = rows_y // grid_count
    orb_count = random_orbitals.shape[0]
    per_dev, projs_each = projectors.shape[:2]
    atoms = per_dev * grid_count
    chunks = 2 if rows % 16 == 0 else 1
    some = rows // chunks
    part = cols_x // orb_groups
    put_late = part % 128 == 0
    c0, c1, c2 = cheb_coef[0], cheb_coef[1], cheb_coef[2]
    c1_4 = c1 / 4.0
    c2_8 = c2 / 8.0
    planar_tables = [jnp.stack(pair) for pair in zip(halves_of(kinetic_table(cols_x)), halves_of(kinetic_table(rows_y)))]
    depth_tables = halves_of(kinetic_table(all_planes))
    total = (all_planes, rows_y // 8, cols_x // 128)

    groups = cols_x // 128
    lines = groups * planes * some

    def pieces(field):
        field = field.reshape(planes, grid_count, chunks, some, groups, 128)
        return [field[:, :, i].transpose(1, 3, 0, 2, 4).reshape(grid_count, lines, 128) for i in range(chunks)]

    def exchange_with(piece, numbers, *others):
        more = -(-numbers.size // 1024) * 8
        extra = jnp.pad(numbers.reshape(-1), (0, more * 128 - numbers.size)).reshape(1, more, 128)
        send = jnp.concatenate([piece, jnp.broadcast_to(extra, (grid_count, more, 128))], axis=1)
        got = exchange(after(send, *others), "grid")
        summed = jnp.sum(got[:, lines:], axis=0).reshape(-1)[: numbers.size].reshape(numbers.shape)
        return got, summed

    def exchange_alone(piece, *others):
        return exchange(after(piece, *others), "grid")

    def joined(got):
        if planes % 8 == 0 and some % 8 == 0:
            return got
        got = got[:, :lines].reshape(grid_count, groups, planes * some, 128)
        return got.transpose(1, 0, 2, 3).reshape(1, grid_count * lines, 128)

    raw = jnp.concatenate([sphere_cells.astype(jnp.float32), projectors], axis=1)
    here = [(grid_pos + grid_count + step) % grid_count for step in (-1, 0, 1)]
    ahead = [(i, (i + 1) % grid_count) for i in range(grid_count)]
    behind = [(j, i) for i, j in ahead]
    near = jnp.concatenate([lax.ppermute(raw, "grid", ahead), raw, lax.ppermute(raw, "grid", behind)])
    near_projs = near[:, 2:]
    near_starts, near_spots = atom_windows(near[:, :2].astype(jnp.int32), all_planes, rows_y, cols_x)
    zero = jnp.zeros_like(grid_pos)
    slab_corner = jnp.stack([grid_pos * planes, zero, zero])

    def partial_slab(field):
        values = pick(total, near_starts, slab_corner, near_spots, field)
        coeffs = jnp.einsum("aj,apj->ap", values[:, 0], near_projs, precision=PRECISE)
        coeffs = coeffs.reshape(3, per_dev, projs_each)
        out = jnp.zeros((grid_count, per_dev, projs_each), jnp.float32)
        for i, slab in enumerate(here):
            out = lax.dynamic_update_slice_in_dim(out, coeffs[i : i + 1], slab, 0)
        return out.reshape(atoms, projs_each)

    def amounts(coeffs):
        coeffs = coeffs.reshape(grid_count, per_dev, projs_each)
        coeffs = jnp.concatenate([lax.dynamic_index_in_dim(coeffs, slab, 0, keepdims=False) for slab in here])
        return jnp.einsum("ap,apj->aj", coeffs * kb_energy, near_projs, precision=PRECISE)[:, None]

    def put_near(coeffs, base, corner=slab_corner):
        return put(total, near_starts, corner, near_spots, amounts(coeffs), base)

    mine = lax.dynamic_slice_in_dim(potential, orb_pos * part, part, axis=2)
    mine = mine.reshape(planes, grid_count, rows, part).transpose(1, 0, 2, 3)
    mine = after(mine, near_starts)
    got_potential = exchange_alone(mine)
    shared = gather_steps(got_potential[None], "orb")
    shared = jnp.moveaxis(shared.reshape(orb_groups, all_planes, rows, part), 0, 2)
    shared = jnp.moveaxis(shared.reshape(all_planes, rows, groups, 128), 2, 0)
    shared = shared.reshape(groups, grid_count, planes, chunks, some, 128)
    wells = [shared[:, :, :, i].reshape(groups, grid_count, planes * some, 128) for i in range(chunks)]
    if joined(jnp.zeros((grid_count, lines, 128))).shape[0] == 1:
        wells = [well.reshape(groups, 1, all_planes * some, 128) for well in wells]

    every = None
    sums = [0.0] * chunks
    for orb in range(orb_count):
        v = random_orbitals[orb]
        v_here = after(v, mine)
        v_sends = pieces(v_here)
        first = partial_slab(v_here)
        pv, t = planar_first(v_here, potential, planar_tables)
        v0, first = exchange_with(v_sends[0], first, got_potential)
        v_blocks = [v0]
        if every is None:
            every = gather_steps(raw, "grid", (None, mine, got_potential, v0))
            every_projs = every[:, 2:]
            every_starts, every_spots = atom_windows(every[:, :2].astype(jnp.int32), all_planes, rows_y, cols_x)
        for piece in v_sends[1:]:
            v_blocks.append(exchange_alone(piece, v_blocks[-1], pv, t))
        u = put_near(first, t)
        g_sends = pieces(pv + u)
        base = planar_second(
            jnp.stack([c2_8, c1_4, c0 - c2]), u, v, potential, planar_tables, orb_groups
        )
        second = partial_slab(u)

        abc = []
        weights = jnp.stack([c1_4, c2_8])
        for i in range(chunks):
            a, c, b = depth_out(weights, joined(v_blocks[i]), wells[i], some, depth_tables)
            abc.append((a, c, b))
            field = a.reshape(groups, all_planes, some, 128)
            first_row = grid_pos * rows + i * some
            if some % 8:
                padded = jnp.zeros((groups, all_planes, 8, 128), jnp.float32)
                field = lax.dynamic_update_slice(padded, field, (0, 0, first_row % 8, 0))
            corner = jnp.stack([zero, first_row // 8, zero])
            values = pick(total, every_starts, corner, every_spots, field, grouped=True)
            second = second + jnp.einsum("aj,apj->ap", values[:, 0], every_projs, precision=PRECISE)
        second = c2_8 * second
        if put_late:
            second = gather_steps(second[None], "orb")
            base_all = trade(base, "orb")

        g_blocks = []
        for i in range(chunks):
            waits = [v_blocks[-1], base] + g_blocks[-1:] + [x[1] for x in abc[:i]]
            if i < chunks - 1:
                g_blocks.append(exchange_alone(g_sends[i], *waits))
            else:
                g_last, second = exchange_with(g_sends[i], second, *waits)
                g_blocks.append(g_last)
        if put_late:
            corner = slab_corner + jnp.stack([zero, zero, orb_pos * (part // 128)])
            q_all = jnp.stack([put_near(second[o], base_all[o], corner) for o in range(orb_groups)])
        else:
            base = jnp.moveaxis(base, 0, 2).reshape(planes, rows_y, cols_x)
            q = put_near(second, base).reshape(planes, rows_y, orb_groups, part)
            q_all = trade(jnp.moveaxis(q, 2, 0), "orb")
        q_all = q_all.reshape(orb_groups, planes, grid_count, chunks, some, part)

        last = None
        for i in range(chunks):
            m = depth_back(weights, joined(g_blocks[i]), abc[i][1], abc[i][2], some, depth_tables)
            if part != 128:
                m = jnp.moveaxis(m.reshape(groups, all_planes * some, 128), 0, 1)
                m = jnp.moveaxis(m.reshape(all_planes * some, orb_groups, part), 1, 0)
            m = m.reshape(orb_groups * grid_count, planes, some, part)
            m = after(m, g_blocks[-1]) if last is None else after(m, last, q_all)
            last = exchange(m, ("orb", "grid"))
            m = last.reshape(orb_groups, grid_count, planes, some, part)
            filtered = q_all[:, :, :, i] + m.transpose(0, 2, 1, 3, 4)
            sums[i] = sums[i] + jnp.sum(filtered * filtered, axis=0)
    out = []
    for own in sums:
        own = own * (1.0 / (orb_count * orb_groups))
        out.append(jnp.moveaxis(gather_steps(own[None], "orb"), 0, 3))
    return jnp.stack(out, axis=2).reshape(planes, rows_y, cols_x)


def solution(mesh):
    in_specs = (
        P("orb", "grid", None, None),
        P("grid", None, None),
        P("grid", None, None),
        P("grid", None, None),
        P(),
        P(),
    )
    out_specs = P("grid", None, None)
    return jax.shard_map(local, mesh=mesh, in_specs=in_specs, out_specs=out_specs, check_vma=False)
```

```python
import functools
import math

import jax
import jax.numpy as jnp
from jax import lax
from jax.experimental import pallas as pl
from jax.experimental.pallas import tpu as pltpu
from jax.sharding import PartitionSpec as P

REACH = 3
WIDE = 2 * REACH + 1
STRIDE = 16
PRECISE = lax.Precision.HIGHEST
TOGETHER = 4
EARLY = True


def kinetic_table(length):
    places = jnp.arange(length)
    offset = places[:, None] - places[None, :]
    parity = jnp.where(offset % 2 == 0, 1.0, -1.0).astype(jnp.float32)
    angle_half = offset.astype(jnp.float32) * (math.pi / length)
    sine = jnp.where(offset == 0, 1.0, jnp.sin(angle_half))
    off_diag = parity / (2.0 * sine * sine)
    on_diag = jnp.float32(length * length / 12.0 + 1.0 / 6.0)
    return jnp.where(offset == 0, on_diag, off_diag) * (4.0 / (length * length))


def xor_route(size, bit):
    return [(i, i ^ bit) for i in range(size)]


def xor_bits(size):
    bits = []
    bit = size // 2
    while bit:
        bits.append(bit)
        bit //= 2
    return bits


def after(value, *others):
    return lax.optimization_barrier((value,) + others)[0]


def gather_steps(block, axis, waits=()):
    size = lax.axis_size(axis)
    place = lax.axis_index(axis)
    shape = block.shape
    bits = xor_bits(size)
    for i, bit in enumerate(bits):
        if i < len(waits) and waits[i] is not None:
            block = after(block, waits[i])
        other = lax.ppermute(block, axis, xor_route(size, bit))
        upper = (place & bit) != 0
        block = jnp.stack([jnp.where(upper, other, block), jnp.where(upper, block, other)])
    count = len(bits)
    block = jnp.transpose(block, tuple(range(count))[::-1] + tuple(range(count, block.ndim)))
    return block.reshape((size * shape[0],) + shape[1:])


def trade(blocks, axis):
    size = lax.axis_size(axis)
    place = lax.axis_index(axis)
    out = blocks
    for apart in range(1, size):
        sent = lax.dynamic_index_in_dim(blocks, place ^ apart, 0)
        got = lax.ppermute(sent, axis, xor_route(size, apart))
        out = lax.dynamic_update_slice_in_dim(out, got, place ^ apart, 0)
    return out


def exchange(block, axis):
    return lax.all_to_all(block, axis, split_axis=0, concat_axis=0, tiled=True)


def listed(starts, corner, total, planes, tiles, listing):
    all_planes, all_tiles, _ = total

    def one(atom, count):
        ahead = lax.rem(starts[atom, 0] - corner[0] + all_planes, all_planes)
        behind = lax.rem(corner[0] - starts[atom, 0] + all_planes, all_planes)
        tile = lax.rem(starts[atom, 1] // 8 - corner[1] + all_tiles, all_tiles)
        here = ((ahead < planes) | (behind < WIDE)) & ((tile < tiles) | (tile == all_tiles - 1))
        listing[count] = atom
        return count + here.astype(jnp.int32)

    return lax.fori_loop(0, starts.shape[0], one, jnp.int32(0))


def split3(block):
    high = block.astype(jnp.bfloat16).astype(jnp.float32)
    rest = block - high
    middle = rest.astype(jnp.bfloat16).astype(jnp.float32)
    return jnp.concatenate([high, middle, rest - middle], axis=0).astype(jnp.bfloat16)


def placed(starts, corner, total, atom, planes, tiles, lane):
    all_planes, all_tiles, all_groups = total
    z_start, y_start, x_start = starts[atom, 0], starts[atom, 1], starts[atom, 2]
    ahead = lax.rem(z_start - corner[0] + all_planes, all_planes)
    depth = [jnp.minimum(lax.rem(ahead + dz, all_planes), planes - 1) for dz in range(WIDE)]
    z_in = lax.rem(ahead + lane // STRIDE, all_planes) < planes
    first = lax.rem(y_start // 8 - corner[1] + all_tiles, all_tiles)
    tile_pair = (first, lax.rem(first + 1, all_tiles))
    lane_pair = (x_start // 128, lax.rem(x_start // 128 + 1, all_groups))
    return depth, z_in, tile_pair, lane_pair, lax.rem(y_start, 8), lax.rem(x_start, 128)


def corner_of(z, tile, group):
    return z, tile, slice(None), pl.ds(pl.multiple_of(group * 128, 128), 128)


def pick_kernel(total, grouped, starts, corner, spots, field, values, listing):
    values[...] = jnp.zeros_like(values)
    planes, tiles = (field.shape[1], 1) if grouped else field.shape[:2]

    def at(z, tile, group):
        return field[group, z] if grouped else field[corner_of(z, tile, group)]

    lane = lax.broadcasted_iota(jnp.int32, (8, 128), 1)
    row = lax.broadcasted_iota(jnp.int32, (8, 128), 0)
    slot = lax.broadcasted_iota(jnp.int32, (128, 128), 0)
    count = listed(starts, corner, total, planes, tiles, listing)

    def some(group, carry):
        for k in range(TOGETHER):
            atom = listing[jnp.minimum(group * TOGETHER + k, count - 1)]
            depth, z_in, tile_pair, groups, down, right = placed(
                starts, corner, total, atom, planes, tiles, lane
            )
            t0, t1 = (jnp.minimum(t, tiles - 1) for t in tile_pair)
            window = jnp.zeros((8, 128), jnp.float32)
            for dz, z in enumerate(depth):
                upper = jnp.where(lane >= right, at(z, t0, groups[0]), at(z, t0, groups[1]))
                lower = jnp.where(lane >= right, at(z, t1, groups[0]), at(z, t1, groups[1]))
                met = jnp.where(row >= down, upper, lower)
                met = pltpu.roll(met, lax.rem(STRIDE * dz - right + 128, 128), 1)
                window = jnp.where(lane // STRIDE == dz, met, window)
            window = pltpu.roll(window, lax.rem(8 - down, 8), 0)
            tile_of = jnp.where(row < 8 - down, tile_pair[0], tile_pair[1])
            window = jnp.where(z_in & (tile_of < tiles), window, 0.0)
            spot = spots[atom]
            chosen = (slot == spot[1:2]).astype(jnp.float32).astype(jnp.bfloat16)
            found = jnp.dot(split3(window), chosen, preferred_element_type=jnp.float32)
            found = found[0:8] + found[8:16] + found[16:24]
            found = jnp.where(row == spot[0:1], found, 0.0)
            values[pl.ds(atom, 1)] = jnp.sum(found, axis=0, keepdims=True)[None]
        return carry

    lax.fori_loop(0, (count + TOGETHER - 1) // TOGETHER, some, 0)


def put_kernel(total, starts, corner, spots, spread, base, field, listing):
    field[...] = base[...]
    planes, tiles = field.shape[:2]
    lane = lax.broadcasted_iota(jnp.int32, (8, 128), 1)
    row = lax.broadcasted_iota(jnp.int32, (8, 128), 0)
    slot = lax.broadcasted_iota(jnp.int32, (128, 128), 0)
    count = listed(starts, corner, total, planes, tiles, listing)

    def some(group, carry):
        for k in range(TOGETHER):
            at = group * TOGETHER + k
            atom = listing[jnp.minimum(at, count - 1)]
            depth, z_in, (t0, t1), groups, down, right = placed(
                starts, corner, total, atom, planes, tiles, lane
            )
            spot = spots[atom]
            chosen = (slot == spot[1:2]).astype(jnp.float32).astype(jnp.bfloat16)
            amounts = jnp.where(row == spot[0:1], spread[atom], 0.0)
            window = lax.dot_general(
                split3(amounts), chosen, (((1,), (1,)), ((), ())), preferred_element_type=jnp.float32
            )
            window = window[0:8] + window[8:16] + window[16:24]
            window = jnp.where(z_in & (at < count), window, 0.0)
            window = pltpu.roll(window, down, 0)
            for dz, z in enumerate(depth):
                part = jnp.where(lane // STRIDE == dz, window, 0.0)
                part = pltpu.roll(part, lax.rem(right - STRIDE * dz + 128, 128), 1)
                spans = range(field.shape[3] // 128)
                places = [(i, g, corner_of(z, t, g)) for i, t in enumerate((t0, t1)) for g in spans]
                before = [field[place] for _, _, place in places]
                for old, (i, g, place) in zip(before, places):
                    inside = (row < down) if i else (row >= down)
                    inside = inside & (jnp.where(lane >= right, groups[0], groups[1]) == g + corner[2])
                    field[place] = old + jnp.where(inside, part, 0.0)
        return carry

    lax.fori_loop(0, (count + TOGETHER - 1) // TOGETHER, some, 0)


def bf16_pair(block):
    high = block.astype(jnp.bfloat16)
    return high, (block - high.astype(jnp.float32)).astype(jnp.bfloat16)


def times(left, right):
    return jnp.dot(left, right, preferred_element_type=jnp.float32)


def in_plane(block, high_tables, low_tables):
    high, low = bf16_pair(block)
    kin = times(high, high_tables[0]) + (times(high, low_tables[0]) + times(low, high_tables[0]))
    return kin + (times(high_tables[1], high) + (times(low_tables[1], high) + times(high_tables[1], low)))


def first_kernel(field, potential, high_tables, low_tables, kin_out, all_out):
    block = field[0]
    kin = in_plane(block, high_tables, low_tables)
    kin_out[0] = kin
    all_out[0] = kin + (potential[0] - 2.0) * block


def second_kernel(weights, field, extra, potential, high_tables, low_tables, out):
    block = field[0]
    total = in_plane(block, high_tables, low_tables) + (potential[0] - 2.0) * block
    total = weights[0] * total + weights[1] * block + weights[2] * extra[0]
    part = out.shape[3]
    for i in range(out.shape[0]):
        out[i, 0] = total[:, i * part : (i + 1) * part]


def depth_times(high_table, low_table, block):
    high, low = bf16_pair(block)
    return times(high_table[...], high) + (times(low_table[...], high) + times(high_table[...], low))


def lines_of(ref, group, start, rows, planes, r):
    line = pl.ds(start + group * planes * rows + r, planes, stride=rows)
    return jnp.concatenate([ref[d, line, :] for d in range(ref.shape[0])], axis=0)


def out_kernel(rows, weights, field, potential, high_table, low_table, a_out, c_out, b_out):
    groups, everywhere = a_out.shape[0], high_table.shape[0]
    planes = everywhere // field.shape[0]

    def one(r, carry):
        v = jnp.concatenate([lines_of(field, g, 0, rows, planes, r) for g in range(groups)], axis=1)
        a = depth_times(high_table, low_table, v)
        for g in range(groups):
            cols = slice(128 * g, 128 * g + 128)
            well = lines_of(potential.at[g], 0, 0, rows, planes, r) - 2.0
            line = pl.ds(r, everywhere, stride=rows)
            a_out[g, line, :] = a[:, cols]
            c_out[g, line, :] = weights[0] * v[:, cols] + weights[1] * a[:, cols]
            b_out[g, line, :] = weights[1] * well * a[:, cols]
        return carry

    lax.fori_loop(0, rows, one, 0)


def back_kernel(rows, weights, g_in, c_in, b_in, high_table, low_table, *numbers_out):
    out = numbers_out[-1]
    groups, everywhere = c_in.shape[0], high_table.shape[0]
    planes = everywhere // g_in.shape[0]
    devices = out.shape[1]
    mine = everywhere // devices

    def one(r, carry):
        line = pl.ds(r, everywhere, stride=rows)
        parts = [
            c_in[g, line, :] + weights[1] * lines_of(g_in, g, 0, rows, planes, r) for g in range(groups)
        ]
        m = depth_times(high_table, low_table, jnp.concatenate(parts, axis=1))
        for g in range(groups):
            m_g = m[:, 128 * g : 128 * g + 128] + b_in[g, line, :]
            for d in range(devices):
                out[g, d, pl.ds(r, mine, stride=rows), :] = m_g[mine * d : mine * d + mine]
        return carry

    lax.fori_loop(0, rows, one, 0)
    for numbers in numbers_out[:-1]:
        for g in range(groups):
            for d in range(devices):
                out[g, d, mine * rows :, :] = numbers[...]


def tiled(field):
    return field.reshape(field.shape[0], field.shape[1] // 8, 8, field.shape[2])


SMEM = pl.BlockSpec(memory_space=pltpu.SMEM)
VMEM = pl.BlockSpec(memory_space=pltpu.VMEM)
PARAMS = pltpu.CompilerParams(vmem_limit_bytes=48 * 2**20)


def pick(total, starts, corner, spots, field, grouped=False):
    return pl.pallas_call(
        functools.partial(pick_kernel, total, grouped),
        out_shape=jax.ShapeDtypeStruct((starts.shape[0], 1, 128), jnp.float32),
        in_specs=[SMEM, SMEM, VMEM, VMEM],
        out_specs=VMEM,
        scratch_shapes=[pltpu.SMEM((starts.shape[0] + 1,), jnp.int32)],
        compiler_params=PARAMS,
        cost_estimate=pl.CostEstimate(flops=1 << 24, bytes_accessed=1 << 24, transcendentals=0),
        name="pick",
    )(starts, corner, spots, field if grouped else tiled(field))


def put(total, starts, corner, spots, spread, base):
    shaped = tiled(base)
    return pl.pallas_call(
        functools.partial(put_kernel, total),
        out_shape=jax.ShapeDtypeStruct(shaped.shape, jnp.float32),
        in_specs=[SMEM, SMEM, VMEM, VMEM, VMEM],
        out_specs=VMEM,
        scratch_shapes=[pltpu.SMEM((starts.shape[0] + 1,), jnp.int32)],
        compiler_params=PARAMS,
        cost_estimate=pl.CostEstimate(flops=1 << 24, bytes_accessed=1 << 24, transcendentals=0),
        name="put",
    )(starts, corner, spots, spread, shaped).reshape(base.shape)


def halves_of(table):
    high = lax.reduce_precision(table, 8, 7)
    return high.astype(jnp.bfloat16), (table - high).astype(jnp.bfloat16)


def plane_specs(shape):
    plane = pl.BlockSpec((1,) + shape[1:], lambda z: (z, 0, 0))
    return plane, pl.BlockSpec((2,) + shape[1:], lambda z: (0, 0, 0))


def cost(flops, numbers):
    return pl.CostEstimate(flops=flops, bytes_accessed=4 * numbers, transcendentals=0)


def planar_first(field, potential, tables):
    plane, pair = plane_specs(field.shape)
    return pl.pallas_call(
        first_kernel,
        grid=field.shape[:1],
        out_shape=[jax.ShapeDtypeStruct(field.shape, jnp.float32)] * 2,
        in_specs=[plane, plane, pair, pair],
        out_specs=[plane, plane],
        compiler_params=PARAMS,
        cost_estimate=cost(12 * field.shape[2] * field.size, 4 * field.size),
        name="planar_first",
    )(field, potential, *tables)


def planar_second(weights, field, extra, potential, tables, parts):
    plane, pair = plane_specs(field.shape)
    planes, rows_y, cols_x = field.shape
    shape = (parts, planes, rows_y, cols_x // parts)
    return pl.pallas_call(
        second_kernel,
        grid=field.shape[:1],
        out_shape=jax.ShapeDtypeStruct(shape, jnp.float32),
        in_specs=[SMEM, plane, plane, plane, pair, pair],
        out_specs=pl.BlockSpec((parts, 1) + shape[2:], lambda z: (0, z, 0, 0)),
        compiler_params=PARAMS,
        cost_estimate=cost(12 * field.shape[2] * field.size, 4 * field.size),
        name="planar_second",
    )(weights, field, extra, potential, *tables)


def depth_out(weights, field, potential, rows, tables):
    groups = potential.shape[0]
    lines = tables[0].shape[0] * rows
    return pl.pallas_call(
        functools.partial(out_kernel, rows),
        out_shape=[jax.ShapeDtypeStruct((groups, lines, 128), jnp.float32)] * 3,
        in_specs=[SMEM, VMEM, VMEM, VMEM, VMEM],
        out_specs=[VMEM] * 3,
        compiler_params=PARAMS,
        cost_estimate=cost(6 * tables[0].size * rows * groups * 128, 5 * groups * lines * 128),
        name="depth_out",
    )(weights, field, potential, *tables)


def depth_back(weights, g, c, b, rows, devices, tables, *numbers):
    groups, lines = c.shape[:2]
    shape = (groups, devices, lines // devices + sum(n.shape[0] for n in numbers), 128)
    return pl.pallas_call(
        functools.partial(back_kernel, rows),
        out_shape=jax.ShapeDtypeStruct(shape, jnp.float32),
        in_specs=[SMEM] + [VMEM] * (5 + len(numbers)),
        out_specs=VMEM,
        compiler_params=PARAMS,
        cost_estimate=cost(6 * tables[0].shape[0] * c.size, 4 * c.size),
        name="depth_back",
    )(weights, g, c, b, *tables, *numbers)


def atom_windows(cells, all_planes, rows_y, cols_x):
    parts = []
    for coords, size in (
        (cells[:, 0], all_planes),
        (cells[:, 1] // cols_x, rows_y),
        (cells[:, 1] % cols_x, cols_x),
    ):
        anchor = coords[:, :1]
        apart = (coords - anchor + size // 2) % size - size // 2
        least = jnp.min(apart, axis=1, keepdims=True)
        parts.append(((anchor + least) % size, apart - least))
    starts = jnp.concatenate([start for start, _ in parts], axis=1)
    (_, off_z), (_, off_y), (_, off_x) = parts
    spots = jnp.stack([off_y, off_z * STRIDE + off_x], axis=1)
    return starts.astype(jnp.int32), spots.astype(jnp.int32)


def local(random_orbitals, potential, sphere_cells, projectors, kb_energy, cheb_coef):
    grid_count = lax.axis_size("grid")
    grid_pos = lax.axis_index("grid")
    orb_groups = lax.axis_size("orb")
    orb_pos = lax.axis_index("orb")
    planes, rows_y, cols_x = potential.shape
    all_planes = planes * grid_count
    rows = rows_y // grid_count
    orb_count = random_orbitals.shape[0]
    per_dev, projs_each = projectors.shape[:2]
    atoms = per_dev * grid_count
    chunks = 2 if rows % 16 == 0 else 1
    some = rows // chunks
    part = cols_x // orb_groups
    put_late = part % 128 == 0
    c0, c1, c2 = cheb_coef[0], cheb_coef[1], cheb_coef[2]
    c1_4 = c1 / 4.0
    c2_8 = c2 / 8.0
    planar_tables = [jnp.stack(pair) for pair in zip(halves_of(kinetic_table(cols_x)), halves_of(kinetic_table(rows_y)))]
    depth_tables = halves_of(kinetic_table(all_planes))
    total = (all_planes, rows_y // 8, cols_x // 128)

    groups = cols_x // 128
    lines = groups * planes * some
    whole_tiles = planes % 8 == 0 and some % 8 == 0

    def pieces(field):
        field = field.reshape(planes, grid_count, chunks, some, groups, 128)
        return [field[:, :, i].transpose(1, 3, 0, 2, 4).reshape(grid_count, lines, 128) for i in range(chunks)]

    def exchange_after(piece, *others):
        return exchange(after(piece, *others), "grid")

    def joined(got):
        if whole_tiles:
            return got
        got = got[:, :lines].reshape(grid_count, groups, planes * some, 128)
        return got.transpose(1, 0, 2, 3).reshape(1, grid_count * lines, 128)

    raw = jnp.concatenate([sphere_cells.astype(jnp.float32), projectors], axis=1)
    here = [(grid_pos + grid_count + step) % grid_count for step in (-1, 0, 1)]

    def shifted(block, step):
        return lax.ppermute(block, "grid", [(i, (i + step) % grid_count) for i in range(grid_count)])

    near = jnp.concatenate([shifted(raw, 1), raw, shifted(raw, -1)])
    near_projs = near[:, 2:]
    near_starts, near_spots = atom_windows(near[:, :2].astype(jnp.int32), all_planes, rows_y, cols_x)
    zero = jnp.zeros_like(grid_pos)
    slab_corner = jnp.stack([grid_pos * planes, zero, zero])

    def partial_near(field):
        values = pick(total, near_starts, slab_corner, near_spots, field)
        coeffs = jnp.einsum("aj,apj->ap", values[:, 0], near_projs, precision=PRECISE)
        return coeffs.reshape(3, per_dev, projs_each)

    def whole_near(coeffs):
        steps = 1 if planes >= WIDE else 2
        whole = coeffs
        for step in [s for s in range(-steps, steps + 1) if s]:
            got = shifted(coeffs, step)
            moved = jnp.zeros_like(coeffs)
            for i in range(3):
                if 0 <= i - step < 3:
                    moved = moved.at[i - step].set(got[i])
            whole = whole + moved
        return whole.reshape(3 * per_dev, projs_each)

    def everywhere(coeffs):
        out = jnp.zeros((grid_count, per_dev, projs_each), jnp.float32)
        for i, slab in enumerate(here):
            out = lax.dynamic_update_slice_in_dim(out, coeffs[i : i + 1], slab, 0)
        return out.reshape(atoms, projs_each)

    def nearby(coeffs):
        coeffs = coeffs.reshape(grid_count, per_dev, projs_each)
        return jnp.concatenate([lax.dynamic_index_in_dim(coeffs, slab, 0, keepdims=False) for slab in here])

    def put_near(coeffs, base, corner=slab_corner):
        spread = jnp.einsum("ap,apj->aj", coeffs * kb_energy, near_projs, precision=PRECISE)
        return put(total, near_starts, corner, near_spots, spread[:, None], base)

    mine = lax.dynamic_slice_in_dim(potential, orb_pos * part, part, axis=2)
    mine = mine.reshape(planes, grid_count, rows, part).transpose(1, 0, 2, 3)
    if EARLY:
        mine = after(mine, near_starts)
    got_potential = exchange(mine, "grid")
    shared = gather_steps(got_potential[None], "orb")
    shared = jnp.moveaxis(shared.reshape(orb_groups, all_planes, rows, part), 0, 2)
    shared = jnp.moveaxis(shared.reshape(all_planes, rows, groups, 128), 2, 0)
    shared = shared.reshape(groups, grid_count, planes, chunks, some, 128)
    wells = [shared[:, :, :, i].reshape(groups, grid_count, planes * some, 128) for i in range(chunks)]
    if not whole_tiles:
        wells = [well.reshape(groups, 1, all_planes * some, 128) for well in wells]

    every = None
    sums = [0.0] * chunks
    weights = jnp.stack([c1_4, c2_8])
    for orb in range(orb_count):
        v = random_orbitals[orb]
        first = whole_near(partial_near(v))
        pv, t = planar_first(v, potential, planar_tables)
        v_send = jnp.concatenate(pieces(v), axis=1)
        v_got = exchange_after(v_send, got_potential, pv, t, first)
        v_blocks = [v_got[:, i * lines : (i + 1) * lines] for i in range(chunks)]
        if every is None:
            every = gather_steps(raw, "grid", (None, mine, got_potential, got_potential))
            every_projs = every[:, 2:]
            every_starts, every_spots = atom_windows(every[:, :2].astype(jnp.int32), all_planes, rows_y, cols_x)
        u = put_near(first, t)
        g_send = jnp.concatenate(pieces(pv + u), axis=1)
        base = planar_second(
            jnp.stack([c2_8, c1_4, c0 - c2]), u, v, potential, planar_tables, orb_groups
        )
        second = everywhere(partial_near(u))
        if put_late:
            base = trade(base, "orb")
        g_got = exchange_after(g_send, v_got, base, second, every_starts, every_spots)
        g_blocks = [g_got[:, i * lines : (i + 1) * lines] for i in range(chunks)]

        cb = []
        for i in range(chunks):
            a, c, b = depth_out(weights, joined(v_blocks[i]), wells[i], some, depth_tables)
            cb.append((c, b))
            field = a.reshape(groups, all_planes, some, 128)
            first_row = grid_pos * rows + i * some
            if some % 8:
                padded = jnp.zeros((groups, all_planes, 8, 128), jnp.float32)
                field = lax.dynamic_update_slice(padded, field, (0, 0, first_row % 8, 0))
            corner = jnp.stack([zero, first_row // 8, zero])
            values = pick(total, every_starts, corner, every_spots, field, grouped=True)
            second = second + jnp.einsum("aj,apj->ap", values[:, 0], every_projs, precision=PRECISE)
        second = (c2_8 * second).reshape(-1)
        more = -(-second.size // 1024) * 8
        extra = jnp.pad(second, (0, more * 128 - second.size)).reshape(more, 128)

        last = None
        for i in range(chunks):
            if part == 128:
                tail = [extra] if i == 0 else []
                m = depth_back(weights, joined(g_blocks[i]), *cb[i], some, grid_count, depth_tables, *tail)
                m = m.reshape(orb_groups * grid_count, -1, 128)
            else:
                m = depth_back(weights, joined(g_blocks[i]), *cb[i], some, 1, depth_tables)
                m = jnp.moveaxis(m.reshape(groups, all_planes * some, 128), 0, 1)
                m = jnp.moveaxis(m.reshape(all_planes * some, orb_groups, part), 1, 0)
                m = m.reshape(orb_groups * grid_count, planes * some * part // 128, 128)
                if i == 0:
                    tail = jnp.broadcast_to(extra, (orb_groups * grid_count, more, 128))
                    m = jnp.concatenate([m, tail], axis=1)
            if last is not None:
                m = after(m, last)
            last = exchange(m, ("orb", "grid"))
            length = planes * some * part // 128
            m = last[:, :length].reshape(orb_groups, grid_count, planes, some, part)
            if i == 0:
                sent = last[:, length:].reshape(orb_groups, grid_count, more * 128)
                second = jnp.sum(sent, axis=1)[:, : atoms * projs_each]
                if put_late:
                    corner = slab_corner + jnp.stack([zero, zero, orb_pos * (part // 128)])
                    q_all = jnp.stack([put_near(nearby(second[o]), base[o], corner) for o in range(orb_groups)])
                else:
                    base = jnp.moveaxis(base, 0, 2).reshape(planes, rows_y, cols_x)
                    own = lax.dynamic_index_in_dim(second, orb_pos, 0, keepdims=False)
                    q = put_near(nearby(own), base).reshape(planes, rows_y, orb_groups, part)
                    q_all = trade(jnp.moveaxis(q, 2, 0), "orb")
                q_all = q_all.reshape(orb_groups, planes, grid_count, chunks, some, part)
            filtered = q_all[:, :, :, i] + m.transpose(0, 2, 1, 3, 4)
            sums[i] = sums[i] + jnp.sum(filtered * filtered, axis=0)
    out = []
    for own in sums:
        own = own * (1.0 / (orb_count * orb_groups))
        out.append(jnp.moveaxis(gather_steps(own[None], "orb"), 0, 3))
    return jnp.stack(out, axis=2).reshape(planes, rows_y, cols_x)


def solution(mesh):
    in_specs = (
        P("orb", "grid", None, None),
        P("grid", None, None),
        P("grid", None, None),
        P("grid", None, None),
        P(),
        P(),
    )
    out_specs = P("grid", None, None)
    return jax.shard_map(local, mesh=mesh, in_specs=in_specs, out_specs=out_specs, check_vma=False)
```

```python
import functools
import math

import jax
import jax.numpy as jnp
from jax import lax
from jax.experimental import pallas as pl
from jax.experimental.pallas import tpu as pltpu
from jax.sharding import PartitionSpec as P

REACH = 3
WIDE = 2 * REACH + 1
STRIDE = 16
PRECISE = lax.Precision.HIGHEST
TOGETHER = 4


def kinetic_table(length):
    places = jnp.arange(length)
    offset = places[:, None] - places[None, :]
    parity = jnp.where(offset % 2 == 0, 1.0, -1.0).astype(jnp.float32)
    angle_half = offset.astype(jnp.float32) * (math.pi / length)
    sine = jnp.where(offset == 0, 1.0, jnp.sin(angle_half))
    off_diag = parity / (2.0 * sine * sine)
    on_diag = jnp.float32(length * length / 12.0 + 1.0 / 6.0)
    return jnp.where(offset == 0, on_diag, off_diag) * (4.0 / (length * length))


def xor_route(size, bit):
    return [(i, i ^ bit) for i in range(size)]


def gather_part(block, axis, shift, size):
    place = lax.axis_index(axis)
    own = lax.rem(lax.shift_right_logical(place, shift), size)
    out = jnp.broadcast_to(block, (size,) + block.shape)
    for apart in range(1, size):
        got = lax.ppermute(block, axis, xor_route(lax.axis_size(axis), apart << shift))
        out = lax.dynamic_update_slice_in_dim(out, got[None], own ^ apart, 0)
    return out


def gather_over(block, axis):
    size = lax.axis_size(axis)
    return gather_part(block, axis, 0, size).reshape((size * block.shape[0],) + block.shape[1:])


def trade(blocks, axis):
    size = lax.axis_size(axis)
    place = lax.axis_index(axis)
    out = blocks
    for apart in range(1, size):
        sent = lax.dynamic_index_in_dim(blocks, place ^ apart, 0)
        got = lax.ppermute(sent, axis, xor_route(size, apart))
        out = lax.dynamic_update_slice_in_dim(out, got, place ^ apart, 0)
    return out


def exchange(block, axis):
    return lax.all_to_all(block, axis, split_axis=0, concat_axis=0, tiled=True)


def wrapped(number, size):
    number = jnp.where(number < 0, number + size, number)
    return jnp.where(number >= size, number - size, number)


def listed(starts, corner, total, planes, tiles, listing):
    all_planes, all_tiles, _ = total

    def one(atom, count):
        ahead = wrapped(starts[atom, 0] - corner[0], all_planes)
        tile = wrapped(lax.shift_right_logical(starts[atom, 1], 3) - corner[1], all_tiles)
        near = (ahead < planes) | (ahead > all_planes - WIDE)
        here = near & ((tile < tiles) | (tile == all_tiles - 1))
        listing[count] = atom
        return count + here.astype(jnp.int32)

    return lax.fori_loop(0, starts.shape[0], one, jnp.int32(0), unroll=8)


def split3(block):
    high = block.astype(jnp.bfloat16).astype(jnp.float32)
    rest = block - high
    middle = rest.astype(jnp.bfloat16).astype(jnp.float32)
    return jnp.concatenate([high, middle, rest - middle], axis=0).astype(jnp.bfloat16)


def placed(starts, corner, total, atom, planes, tiles, lane):
    all_planes, all_tiles, all_groups = total
    z_start, y_start, x_start = starts[atom, 0], starts[atom, 1], starts[atom, 2]
    ahead = wrapped(z_start - corner[0], all_planes)
    depth = [jnp.minimum(wrapped(ahead + dz, all_planes), planes - 1) for dz in range(WIDE)]
    z_in = wrapped(ahead + lane // STRIDE, all_planes) < planes
    first = wrapped(lax.shift_right_logical(y_start, 3) - corner[1], all_tiles)
    tile_pair = (first, wrapped(first + 1, all_tiles))
    group = lax.shift_right_logical(x_start, 7)
    lane_pair = (group, wrapped(group + 1, all_groups))
    return depth, z_in, tile_pair, lane_pair, y_start & 7, x_start & 127


def corner_of(z, tile, group):
    return z, tile, slice(None), pl.ds(pl.multiple_of(group * 128, 128), 128)


def pick_kernel(total, grouped, starts, corner, spots, field, values, listing):
    values[...] = jnp.zeros_like(values)
    planes, tiles = (field.shape[1], 1) if grouped else field.shape[:2]

    def at(z, tile, group):
        return field[group, z] if grouped else field[corner_of(z, tile, group)]

    lane = lax.broadcasted_iota(jnp.int32, (8, 128), 1)
    row = lax.broadcasted_iota(jnp.int32, (8, 128), 0)
    slot = lax.broadcasted_iota(jnp.int32, (128, 128), 0)
    count = listed(starts, corner, total, planes, tiles, listing)

    def some(group, carry):
        for k in range(TOGETHER):
            atom = listing[jnp.minimum(group * TOGETHER + k, count - 1)]
            depth, z_in, tile_pair, groups, down, right = placed(
                starts, corner, total, atom, planes, tiles, lane
            )
            t0, t1 = (jnp.minimum(t, tiles - 1) for t in tile_pair)
            window = jnp.zeros((8, 128), jnp.float32)
            for dz, z in enumerate(depth):
                upper = jnp.where(lane >= right, at(z, t0, groups[0]), at(z, t0, groups[1]))
                lower = jnp.where(lane >= right, at(z, t1, groups[0]), at(z, t1, groups[1]))
                met = jnp.where(row >= down, upper, lower)
                met = pltpu.roll(met, (STRIDE * dz - right) & 127, 1)
                window = jnp.where(lane // STRIDE == dz, met, window)
            window = pltpu.roll(window, (8 - down) & 7, 0)
            tile_of = jnp.where(row < 8 - down, tile_pair[0], tile_pair[1])
            window = jnp.where(z_in & (tile_of < tiles), window, 0.0)
            spot = spots[atom]
            chosen = (slot == spot[1:2]).astype(jnp.float32).astype(jnp.bfloat16)
            found = jnp.dot(split3(window), chosen, preferred_element_type=jnp.float32)
            found = found[0:8] + found[8:16] + found[16:24]
            found = jnp.where(row == spot[0:1], found, 0.0)
            values[pl.ds(atom, 1)] = jnp.sum(found, axis=0, keepdims=True)[None]
        return carry

    lax.fori_loop(0, (count + TOGETHER - 1) // TOGETHER, some, 0)


def put_kernel(total, starts, corner, spots, spread, base, field, listing):
    field[...] = base[...]
    planes, tiles = field.shape[:2]
    lane = lax.broadcasted_iota(jnp.int32, (8, 128), 1)
    row = lax.broadcasted_iota(jnp.int32, (8, 128), 0)
    slot = lax.broadcasted_iota(jnp.int32, (128, 128), 0)
    count = listed(starts, corner, total, planes, tiles, listing)

    def some(group, carry):
        for k in range(TOGETHER):
            at = group * TOGETHER + k
            atom = listing[jnp.minimum(at, count - 1)]
            depth, z_in, (t0, t1), groups, down, right = placed(
                starts, corner, total, atom, planes, tiles, lane
            )
            spot = spots[atom]
            chosen = (slot == spot[1:2]).astype(jnp.float32).astype(jnp.bfloat16)
            amounts = jnp.where(row == spot[0:1], spread[atom], 0.0)
            window = lax.dot_general(
                split3(amounts), chosen, (((1,), (1,)), ((), ())), preferred_element_type=jnp.float32
            )
            window = window[0:8] + window[8:16] + window[16:24]
            window = jnp.where(z_in & (at < count), window, 0.0)
            window = pltpu.roll(window, down, 0)
            for dz, z in enumerate(depth):
                part = jnp.where(lane // STRIDE == dz, window, 0.0)
                part = pltpu.roll(part, (right - STRIDE * dz) & 127, 1)
                spans = range(field.shape[3] // 128)
                places = [(i, g, corner_of(z, t, g)) for i, t in enumerate((t0, t1)) for g in spans]
                before = [field[place] for _, _, place in places]
                for old, (i, g, place) in zip(before, places):
                    inside = (row < down) if i else (row >= down)
                    inside = inside & (jnp.where(lane >= right, groups[0], groups[1]) == g + corner[2])
                    field[place] = old + jnp.where(inside, part, 0.0)
        return carry

    lax.fori_loop(0, (count + TOGETHER - 1) // TOGETHER, some, 0)


def bf16_pair(block):
    high = block.astype(jnp.bfloat16)
    return high, (block - high.astype(jnp.float32)).astype(jnp.bfloat16)


def times(left, right):
    return jnp.dot(left, right, preferred_element_type=jnp.float32)


def in_plane(block, high_tables, low_tables):
    high, low = bf16_pair(block)
    kin = times(high, high_tables[0]) + (times(high, low_tables[0]) + times(low, high_tables[0]))
    return kin + (times(high_tables[1], high) + (times(low_tables[1], high) + times(high_tables[1], low)))


def first_kernel(field, potential, high_tables, low_tables, kin_out, all_out):
    block = field[0]
    kin = in_plane(block, high_tables, low_tables)
    kin_out[0] = kin
    all_out[0] = kin + (potential[0] - 2.0) * block


def second_kernel(weights, field, extra, potential, high_tables, low_tables, out):
    block = field[0]
    total = in_plane(block, high_tables, low_tables) + (potential[0] - 2.0) * block
    total = weights[0] * total + weights[1] * block + weights[2] * extra[0]
    part = out.shape[3]
    for i in range(out.shape[0]):
        out[i, 0] = total[:, i * part : (i + 1) * part]


def depth_times(high_table, low_table, block):
    high, low = bf16_pair(block)
    return times(high_table[...], high) + (times(low_table[...], high) + times(high_table[...], low))


def lines_of(ref, r, rows):
    devices, lines = ref.shape[:2]
    line = pl.ds(r, lines // rows, stride=rows)
    return jnp.concatenate([ref[d, line, :] for d in range(devices)], axis=0)


def side_by_side(rows):
    return [(r, r + 1) for r in range(0, rows - 1, 2)] + [(rows - 1,)] * (rows % 2)


def out_kernel(rows, weights, field, potential, high_table, low_table, a_out, c_out, b_out):
    everywhere = high_table.shape[0]
    for pair in side_by_side(rows):
        v = jnp.concatenate([lines_of(field, r, rows) for r in pair], axis=1)
        both = depth_times(high_table, low_table, v)
        for i, r in enumerate(pair):
            a, line = both[:, 128 * i : 128 * i + 128], pl.ds(r, everywhere, stride=rows)
            a_out[0, line, :] = a
            c_out[0, line, :] = weights[0] * v[:, 128 * i : 128 * i + 128] + weights[1] * a
            b_out[0, line, :] = weights[1] * (lines_of(potential.at[0], r, rows) - 2.0) * a


def back_kernel(rows, cuts, weights, g_in, c_in, b_in, high_table, low_table, *outs):
    everywhere = high_table.shape[0]
    devices = outs[0].shape[1]
    mine = everywhere // devices
    for pair in side_by_side(rows):
        lines = [pl.ds(r, everywhere, stride=rows) for r in pair]
        parts = [c_in[0, line, :] + weights[1] * lines_of(g_in, r, rows) for r, line in zip(pair, lines)]
        both = depth_times(high_table, low_table, jnp.concatenate(parts, axis=1))
        for i, (r, line) in enumerate(zip(pair, lines)):
            m = both[:, 128 * i : 128 * i + 128] + b_in[0, line, :]
            for out, (start, stop) in zip(outs, cuts):
                for d in range(devices):
                    out[0, d, pl.ds(r, stop - start, stride=rows), :] = m[mine * d + start : mine * d + stop]


def tiled(field):
    return field.reshape(field.shape[0], field.shape[1] // 8, 8, field.shape[2])


SMEM = pl.BlockSpec(memory_space=pltpu.SMEM)
VMEM = pl.BlockSpec(memory_space=pltpu.VMEM)
PARAMS = pltpu.CompilerParams(vmem_limit_bytes=48 * 2**20)


def ordered(kernel, count, others):
    def run(*refs):
        kernel(*refs[:count], *refs[count + others :])

    return run


ANY = pl.BlockSpec(memory_space=pl.ANY)


def pick(total, starts, corner, spots, field, grouped=False):
    return pl.pallas_call(
        functools.partial(pick_kernel, total, grouped),
        out_shape=jax.ShapeDtypeStruct((starts.shape[0], 1, 128), jnp.float32),
        in_specs=[SMEM, SMEM, VMEM, VMEM],
        out_specs=VMEM,
        scratch_shapes=[pltpu.SMEM((starts.shape[0] + 1,), jnp.int32)],
        compiler_params=PARAMS,
        cost_estimate=pl.CostEstimate(flops=1 << 24, bytes_accessed=1 << 24, transcendentals=0),
        name="pick",
    )(starts, corner, spots, field if grouped else tiled(field))


def put(total, starts, corner, spots, spread, base):
    shaped = tiled(base)
    return pl.pallas_call(
        functools.partial(put_kernel, total),
        out_shape=jax.ShapeDtypeStruct(shaped.shape, jnp.float32),
        in_specs=[SMEM, SMEM, VMEM, VMEM, VMEM],
        out_specs=VMEM,
        scratch_shapes=[pltpu.SMEM((starts.shape[0] + 1,), jnp.int32)],
        compiler_params=PARAMS,
        cost_estimate=pl.CostEstimate(flops=1 << 24, bytes_accessed=1 << 24, transcendentals=0),
        name="put",
    )(starts, corner, spots, spread, shaped).reshape(base.shape)


def halves_of(table):
    high = lax.reduce_precision(table, 8, 7)
    return high.astype(jnp.bfloat16), (table - high).astype(jnp.bfloat16)


def plane_specs(shape):
    plane = pl.BlockSpec((1,) + shape[1:], lambda z: (z, 0, 0))
    return plane, pl.BlockSpec((2,) + shape[1:], lambda z: (0, 0, 0))


def cost(flops, numbers):
    return pl.CostEstimate(flops=flops, bytes_accessed=4 * numbers, transcendentals=0)


def planar_first(field, potential, tables, *others):
    plane, pair = plane_specs(field.shape)
    return pl.pallas_call(
        ordered(first_kernel, 4, len(others)),
        grid=field.shape[:1],
        out_shape=[jax.ShapeDtypeStruct(field.shape, jnp.float32)] * 2,
        in_specs=[plane, plane, pair, pair] + [ANY] * len(others),
        out_specs=[plane, plane],
        compiler_params=PARAMS,
        cost_estimate=cost(12 * field.shape[2] * field.size, 4 * field.size),
        name="planar_first",
    )(field, potential, *tables, *others)


def planar_second(weights, field, extra, potential, tables, parts):
    plane, pair = plane_specs(field.shape)
    planes, rows_y, cols_x = field.shape
    shape = (parts, planes, rows_y, cols_x // parts)
    return pl.pallas_call(
        second_kernel,
        grid=field.shape[:1],
        out_shape=jax.ShapeDtypeStruct(shape, jnp.float32),
        in_specs=[SMEM, plane, plane, plane, pair, pair],
        out_specs=pl.BlockSpec((parts, 1) + shape[2:], lambda z: (0, z, 0, 0)),
        compiler_params=PARAMS,
        cost_estimate=cost(12 * field.shape[2] * field.size, 4 * field.size),
        name="planar_second",
    )(weights, field, extra, potential, *tables)


def tie(block, *others):
    return pl.pallas_call(
        lambda *refs: None,
        out_shape=jax.ShapeDtypeStruct(block.shape, block.dtype),
        in_specs=[ANY] * (1 + len(others)),
        out_specs=ANY,
        input_output_aliases={0: 0},
        cost_estimate=cost(0, 0),
        name="tie",
    )(block, *others)


def append_kernel(first, others, numbers, block, *refs):
    out, sem = refs[others], refs[others + 1]
    copies = [
        pltpu.make_async_copy(numbers, out.at[d, pl.ds(first, numbers.shape[0]), :], sem.at[d])
        for d in range(out.shape[0])
    ]
    for copy in copies:
        copy.start()
    for copy in copies:
        copy.wait()


def append(block, numbers, *others):
    devices, lines, wide = block.shape
    return pl.pallas_call(
        functools.partial(append_kernel, lines - numbers.shape[0], len(others)),
        out_shape=jax.ShapeDtypeStruct(block.shape, block.dtype),
        in_specs=[VMEM, ANY] + [ANY] * len(others),
        out_specs=ANY,
        scratch_shapes=[pltpu.SemaphoreType.DMA((devices,))],
        input_output_aliases={1: 0},
        cost_estimate=cost(0, devices * numbers.size),
        name="append",
    )(numbers, block, *others)


def pack_kernel(count, chunks, chosen, together, *refs):
    fields, out = refs[:count], refs[-1]
    planes, rows, cols = fields[0].shape
    some = rows // chunks // together
    lines = planes * some
    for d in range(together):
        at = 0
        for i in chosen:
            start = (d * chunks + i) * some
            for g in range(cols // 128):
                cells = (slice(None), slice(start, start + some), slice(128 * g, 128 * g + 128))
                part = fields[0][cells]
                for field in fields[1:]:
                    part = part + field[cells]
                out[d, at : at + lines, :] = part.reshape(lines, 128)
                at += lines


def pack(fields, devices, chunks, chosen, spare, *others):
    planes, rows_y, cols = fields[0].shape
    rows = rows_y // devices
    together = math.gcd(devices, 4)
    lines = planes * rows * cols // 128 * len(chosen) // chunks
    block = pl.BlockSpec((planes, rows * together, cols), lambda d: (0, d, 0))
    return pl.pallas_call(
        ordered(functools.partial(pack_kernel, len(fields), chunks, chosen, together), len(fields), len(others)),
        grid=(devices // together,),
        out_shape=jax.ShapeDtypeStruct((devices, lines + spare, 128), jnp.float32),
        in_specs=[block] * len(fields) + [ANY] * len(others),
        out_specs=pl.BlockSpec((together, lines, 128), lambda d: (d, 0, 0)),
        compiler_params=PARAMS,
        cost_estimate=cost(devices * lines * 128, 2 * devices * lines * 128),
        name="pack",
    )(*fields, *others)


def pack_part_kernel(place, field, out):
    planes, rows, _ = field.shape
    each = rows // out.shape[0]
    for d in range(out.shape[0]):
        out[d] = field[:, d * each : (d + 1) * each, :].reshape(planes * each, 128)


def pack_part(field, devices, place):
    planes, rows_y, _ = field.shape
    together = math.gcd(devices, 4)
    lines = planes * rows_y // devices
    return pl.pallas_call(
        pack_part_kernel,
        grid_spec=pltpu.PrefetchScalarGridSpec(
            num_scalar_prefetch=1,
            grid=(devices // together,),
            in_specs=[pl.BlockSpec((planes, rows_y // devices * together, 128), lambda d, place: (0, d, place[0]))],
            out_specs=pl.BlockSpec((together, lines, 128), lambda d, place: (d, 0, 0)),
        ),
        out_shape=jax.ShapeDtypeStruct((devices, lines, 128), jnp.float32),
        compiler_params=PARAMS,
        cost_estimate=cost(0, 2 * devices * lines * 128),
        name="pack_part",
    )(place, field)


def depth_specs(field, potential_shape, rows, chunk):
    groups, lines = potential_shape[0], potential_shape[1] * potential_shape[2]
    devices = field.shape[0]
    got = pl.BlockSpec((devices, lines // devices, 128), lambda g: (0, chunk * groups + g, 0))
    flat = pl.BlockSpec((1, lines, 128), lambda g: (g, 0, 0))
    table = pl.BlockSpec((lines // rows, lines // rows), lambda g: (0, 0))
    return got, flat, table


def depth_out(weights, field, potential, rows, chunk, tables):
    groups, devices, lines = potential.shape[:3]
    got, flat, table = depth_specs(field, potential.shape, rows, chunk)
    well = pl.BlockSpec((1, devices, lines, 128), lambda g: (g, 0, 0, 0))
    lines = devices * lines
    return pl.pallas_call(
        functools.partial(out_kernel, rows),
        grid=(groups,),
        out_shape=[jax.ShapeDtypeStruct((groups, lines, 128), jnp.float32)] * 3,
        in_specs=[SMEM, got, well, table, table],
        out_specs=[flat] * 3,
        compiler_params=PARAMS,
        cost_estimate=cost(6 * tables[0].size * rows * groups * 128, 5 * groups * lines * 128),
        name="depth_out",
    )(weights, field, potential, *tables)


def depth_back(weights, g, c, b, rows, devices, cuts, tables, *others):
    groups, lines = c.shape[:2]
    got, flat, table = depth_specs(g, (groups, 1, lines), rows, 0)
    each = [(stop - start) * rows for start, stop in cuts]
    return pl.pallas_call(
        ordered(functools.partial(back_kernel, rows, cuts), 6, len(others)),
        grid=(groups,),
        out_shape=[jax.ShapeDtypeStruct((groups, devices, n, 128), jnp.float32) for n in each],
        in_specs=[SMEM, got, flat, flat, table, table] + [ANY] * len(others),
        out_specs=[pl.BlockSpec((1, devices, n, 128), lambda g: (g, 0, 0, 0)) for n in each],
        compiler_params=PARAMS,
        cost_estimate=cost(6 * tables[0].shape[0] * c.size, 4 * c.size),
        name="depth_back",
    )(weights, g, c, b, *tables, *others)


def atom_windows(cells, all_planes, rows_y, cols_x):
    parts = []
    for coords, size in (
        (cells[:, 0], all_planes),
        (cells[:, 1] // cols_x, rows_y),
        (cells[:, 1] % cols_x, cols_x),
    ):
        anchor = coords[:, :1]
        apart = (coords - anchor + size // 2) % size - size // 2
        least = jnp.min(apart, axis=1, keepdims=True)
        parts.append(((anchor + least) % size, apart - least))
    starts = jnp.concatenate([start for start, _ in parts], axis=1)
    (_, off_z), (_, off_y), (_, off_x) = parts
    spots = jnp.stack([off_y, off_z * STRIDE + off_x], axis=1)
    return starts.astype(jnp.int32), spots.astype(jnp.int32)


def local(random_orbitals, potential, sphere_cells, projectors, kb_energy, cheb_coef):
    grid_count = lax.axis_size("grid")
    grid_pos = lax.axis_index("grid")
    orb_groups = lax.axis_size("orb")
    orb_pos = lax.axis_index("orb")
    planes, rows_y, cols_x = potential.shape
    all_planes = planes * grid_count
    rows = rows_y // grid_count
    orb_count = random_orbitals.shape[0]
    per_dev, projs_each = projectors.shape[:2]
    atoms = per_dev * grid_count
    chunks = 2 if rows % 16 == 0 else 1
    some = rows // chunks
    part = cols_x // orb_groups
    put_late = part % 128 == 0
    c0, c1, c2 = cheb_coef[0], cheb_coef[1], cheb_coef[2]
    c1_4 = c1 / 4.0
    c2_8 = c2 / 8.0
    planar_tables = [jnp.stack(pair) for pair in zip(halves_of(kinetic_table(cols_x)), halves_of(kinetic_table(rows_y)))]
    depth_tables = halves_of(kinetic_table(all_planes))
    total = (all_planes, rows_y // 8, cols_x // 128)

    groups = cols_x // 128
    lines = groups * planes * some
    whole_tiles = planes % 8 == 0 and some % 8 == 0

    def packed(fields, chosen, spare, *others):
        if whole_tiles:
            return pack(fields, grid_count, chunks, chosen, spare, *others)
        field = sum(fields[1:], fields[0]).reshape(planes, grid_count, chunks, some, groups, 128)
        sent = [field[:, :, i].transpose(1, 3, 0, 2, 4).reshape(grid_count, lines, 128) for i in chosen]
        return jnp.concatenate(sent + [jnp.zeros((grid_count, spare, 128), jnp.float32)], axis=1)

    def joined(got):
        if whole_tiles:
            return got
        got = got.reshape(grid_count, -1, planes * some, 128)
        return got.transpose(1, 0, 2, 3).reshape(1, -1, 128)

    if part == 128 and rows % 8 == 0:
        mine = pack_part(potential, grid_count, orb_pos[None])
        mine = mine.reshape(grid_count, planes, rows, part)
    else:
        mine = lax.dynamic_slice_in_dim(potential, orb_pos * part, part, axis=2)
        mine = mine.reshape(planes, grid_count, rows, part).transpose(1, 0, 2, 3)

    raw = tie(jnp.concatenate([sphere_cells.astype(jnp.float32), projectors], axis=1), mine)
    here = [(grid_pos + grid_count + step) % grid_count for step in (-1, 0, 1)]

    def shifted(block, step):
        return lax.ppermute(block, "grid", [(i, (i + step) % grid_count) for i in range(grid_count)])

    low = 1 << ((grid_count.bit_length() - 1) // 2)
    high = grid_count // low
    column = gather_part(raw, "grid", low.bit_length() - 1, high)
    gots = [shifted(raw, 1), shifted(raw, -1)]
    near = jnp.concatenate([gots[0], raw, gots[1]])
    near_projs = near[:, 2:]
    near_starts, near_spots = atom_windows(near[:, :2].astype(jnp.int32), all_planes, rows_y, cols_x)
    zero = jnp.zeros_like(grid_pos)
    slab_corner = jnp.stack([grid_pos * planes, zero, zero])

    def partial_near(field):
        values = pick(total, near_starts, slab_corner, near_spots, field)
        coeffs = jnp.einsum("aj,apj->ap", values[:, 0], near_projs, precision=PRECISE)
        return coeffs.reshape(3, per_dev, projs_each)

    def whole_near(coeffs):
        steps = 1 if planes >= WIDE else 2
        whole = coeffs
        for step in [s for s in range(-steps, steps + 1) if s]:
            got = shifted(coeffs, step)
            moved = jnp.zeros_like(coeffs)
            for i in range(3):
                if 0 <= i - step < 3:
                    moved = moved.at[i - step].set(got[i])
            whole = whole + moved
        return whole.reshape(3 * per_dev, projs_each)

    def everywhere(coeffs):
        out = jnp.zeros((grid_count, per_dev, projs_each), jnp.float32)
        for i, slab in enumerate(here):
            out = lax.dynamic_update_slice_in_dim(out, coeffs[i : i + 1], slab, 0)
        return out.reshape(atoms, projs_each)

    def nearby(coeffs):
        coeffs = coeffs.reshape(grid_count, per_dev, projs_each)
        return jnp.concatenate([lax.dynamic_index_in_dim(coeffs, slab, 0, keepdims=False) for slab in here])

    def put_near(coeffs, base, corner=slab_corner):
        spread = jnp.einsum("ap,apj->aj", coeffs * kb_energy, near_projs, precision=PRECISE)
        return put(total, near_starts, corner, near_spots, spread[:, None], base)

    got_potential = exchange(tie(mine, *gots), "grid")
    shared = gather_over(got_potential[None], "orb")
    shared = jnp.moveaxis(shared.reshape(orb_groups, all_planes, rows, part), 0, 2)
    shared = jnp.moveaxis(shared.reshape(all_planes, rows, groups, 128), 2, 0)
    shared = shared.reshape(groups, grid_count, planes, chunks, some, 128)
    wells = [shared[:, :, :, i].reshape(groups, grid_count, planes * some, 128) for i in range(chunks)]
    if not whole_tiles:
        wells = [well.reshape(groups, 1, all_planes * some, 128) for well in wells]

    halves = [(0, planes // 2), (planes // 2, planes)] if planes % 16 == 0 else [(0, planes)]
    cuts = [[(0, planes)]] * (chunks - 1) + [halves]
    sums = [[0.0] * len(cut) for cut in cuts]
    weights = jnp.stack([c1_4, c2_8])
    for orb in range(orb_count):
        v = random_orbitals[orb]
        first = whole_near(partial_near(v))
        pv, t = planar_first(v, potential, planar_tables, mine)
        v_send = packed([v], range(chunks), 0, mine)
        if orb == 0:
            every = gather_part(column, "grid", 0, low)
            every = jnp.swapaxes(every, 0, 1).reshape((atoms,) + raw.shape[1:])
            every_projs = every[:, 2:]
            every_starts, every_spots = atom_windows(every[:, :2].astype(jnp.int32), all_planes, rows_y, cols_x)
        v_got = exchange(tie(v_send, first, column), "grid")
        u = put_near(first, t)
        base = planar_second(
            jnp.stack([c2_8, c1_4, c0 - c2]), u, v, potential, planar_tables, orb_groups
        )
        second = everywhere(partial_near(u))
        if put_late:
            mixed = trade(base, "orb")
        g_gots = []
        for i in range(chunks - 1):
            g_gots.append(exchange(tie(packed([pv, u], [i], 0, base), every, *wells), "grid"))

        cb = []
        for i in range(chunks):
            a, c, b = depth_out(weights, joined(v_got), wells[i], some, i, depth_tables)
            cb.append((c, b))
            field = a.reshape(groups, all_planes, some, 128)
            first_row = grid_pos * rows + i * some
            if some % 8:
                padded = jnp.zeros((groups, all_planes, 8, 128), jnp.float32)
                field = lax.dynamic_update_slice(padded, field, (0, 0, first_row % 8, 0))
            corner = jnp.stack([zero, first_row // 8, zero])
            values = pick(total, every_starts, corner, every_spots, field, grouped=True)
            second = second + jnp.einsum("aj,apj->ap", values[:, 0], every_projs, precision=PRECISE)
        more = -(-orb_groups * second.size // 1024) * 8
        g_last = packed([pv, u], [chunks - 1], more, base)
        second = gather_over(c2_8 * second[None], "orb").reshape(-1)
        extra = jnp.pad(second, (0, more * 128 - second.size)).reshape(more, 128)
        g_last = exchange(append(g_last, extra, *([mixed] if put_late else [])), "grid")
        second = jnp.sum(g_last[:, lines:], axis=0).reshape(-1)[: second.size]
        second = second.reshape(orb_groups, atoms, projs_each)
        g_gots.append(g_last if whole_tiles else g_last[:, :lines])
        if put_late:
            corner = slab_corner + jnp.stack([zero, zero, orb_pos * (part // 128)])
            q_all = jnp.stack([put_near(nearby(second[o]), mixed[o], corner) for o in range(orb_groups)])
        else:
            base = jnp.moveaxis(base, 0, 2).reshape(planes, rows_y, cols_x)
            own = lax.dynamic_index_in_dim(second, orb_pos, 0, keepdims=False)
            q = put_near(nearby(own), base).reshape(planes, rows_y, orb_groups, part)
            q_all = trade(jnp.moveaxis(q, 2, 0), "orb")
        q_all = q_all.reshape(orb_groups, planes, grid_count, chunks, some, part)

        sends = []
        for i in range(chunks):
            if part == 128:
                later = [q_all] if i > 0 else []
                ms = depth_back(weights, joined(g_gots[i]), *cb[i], some, grid_count, cuts[i], depth_tables, *later)
                sends.append([m.reshape(orb_groups * grid_count, -1, 128) for m in ms])
            else:
                whole = [(0, all_planes)]
                (m,) = depth_back(weights, joined(g_gots[i]), *cb[i], some, 1, whole, depth_tables)
                m = jnp.moveaxis(m.reshape(groups, all_planes * some, 128), 0, 1)
                m = jnp.moveaxis(m.reshape(all_planes * some, orb_groups, part), 1, 0)
                m = m.reshape(orb_groups * grid_count, planes, some * part)
                sends.append([m[:, p:q].reshape(orb_groups * grid_count, -1, 128) for p, q in cuts[i]])
        done, kept = [], []
        for i in range(chunks):
            for k, (start, stop) in enumerate(cuts[i]):
                send = sends[i][k]
                if len(kept) > 1:
                    send = tie(send, kept[-2])
                got = exchange(send, ("orb", "grid"))
                if done:
                    got = tie(got, *done[-2:])
                m = got.reshape(orb_groups, grid_count, stop - start, some, part)
                filtered = q_all[:, start:stop, :, i] + m.transpose(0, 2, 1, 3, 4)
                own = jnp.sum(filtered * filtered, axis=0) * (1.0 / (orb_count * orb_groups))
                kept.append(own)
                done.append(gather_over(own[None], "orb"))
                sums[i][k] = sums[i][k] + done[-1]
    out = [jnp.moveaxis(jnp.concatenate(shares, axis=1), 0, 3) for shares in sums]
    return jnp.stack(out, axis=2).reshape(planes, rows_y, cols_x)


def solution(mesh):
    in_specs = (
        P("orb", "grid", None, None),
        P("grid", None, None),
        P("grid", None, None),
        P("grid", None, None),
        P(),
        P(),
    )
    out_specs = P("grid", None, None)
    return jax.shard_map(local, mesh=mesh, in_specs=in_specs, out_specs=out_specs, check_vma=False)
```

```python
import functools
import math

import jax
import jax.numpy as jnp
from jax import lax
from jax.experimental import pallas as pl
from jax.experimental.pallas import tpu as pltpu
from jax.sharding import PartitionSpec as P

REACH = 3
WIDE = 2 * REACH + 1
STRIDE = 16
PRECISE = lax.Precision.HIGHEST
TOGETHER = 4


def kinetic_table(length):
    places = jnp.arange(length)
    offset = places[:, None] - places[None, :]
    parity = jnp.where(offset % 2 == 0, 1.0, -1.0).astype(jnp.float32)
    angle_half = offset.astype(jnp.float32) * (math.pi / length)
    sine = jnp.where(offset == 0, 1.0, jnp.sin(angle_half))
    off_diag = parity / (2.0 * sine * sine)
    on_diag = jnp.float32(length * length / 12.0 + 1.0 / 6.0)
    return jnp.where(offset == 0, on_diag, off_diag) * (4.0 / (length * length))


def xor_route(size, bit):
    return [(i, i ^ bit) for i in range(size)]


def gather_part(block, axis, shift, size):
    place = lax.axis_index(axis)
    own = lax.rem(lax.shift_right_logical(place, shift), size)
    out = jnp.broadcast_to(block, (size,) + block.shape)
    for apart in range(1, size):
        got = lax.ppermute(block, axis, xor_route(lax.axis_size(axis), apart << shift))
        out = lax.dynamic_update_slice_in_dim(out, got[None], own ^ apart, 0)
    return out


def gather_over(block, axis):
    size = lax.axis_size(axis)
    return gather_part(block, axis, 0, size).reshape((size * block.shape[0],) + block.shape[1:])


def trade(blocks, axis, *others):
    size = lax.axis_size(axis)
    place = lax.axis_index(axis)
    out = blocks
    for apart in range(1, size):
        sent = lax.dynamic_index_in_dim(blocks, place ^ apart, 0)
        got = lax.ppermute(sent, axis, xor_route(size, apart))
        if others:
            got = tie(got, *others)
        out = lax.dynamic_update_slice_in_dim(out, got, place ^ apart, 0)
    return out


def exchange(block, axis):
    return lax.all_to_all(block, axis, split_axis=0, concat_axis=0, tiled=True)


def wrapped(number, size):
    number = jnp.where(number < 0, number + size, number)
    return jnp.where(number >= size, number - size, number)


def listed(starts, corner, total, planes, tiles, listing, one_group=False):
    all_planes, all_tiles, _ = total

    def one(atom, count):
        ahead = wrapped(starts[atom, 0] - corner[0], all_planes)
        tile = wrapped(lax.shift_right_logical(starts[atom, 1], 3) - corner[1], all_tiles)
        near = (ahead < planes) | (ahead > all_planes - WIDE)
        here = near & ((tile < tiles) | (tile == all_tiles - 1))
        if one_group:
            group = lax.shift_right_logical(starts[atom, 2], 7)
            crosses = ((starts[atom, 2] & 127) > 128 - WIDE) & (wrapped(group + 1, total[2]) == corner[2])
            here = here & ((group == corner[2]) | crosses)
        listing[count] = atom
        return count + here.astype(jnp.int32)

    return lax.fori_loop(0, starts.shape[0], one, jnp.int32(0), unroll=8)


def split3(block):
    high = block.astype(jnp.bfloat16).astype(jnp.float32)
    rest = block - high
    middle = rest.astype(jnp.bfloat16).astype(jnp.float32)
    return jnp.concatenate([high, middle, rest - middle], axis=0).astype(jnp.bfloat16)


def placed(starts, corner, total, atom, planes, tiles, lane):
    all_planes, all_tiles, all_groups = total
    z_start, y_start, x_start = starts[atom, 0], starts[atom, 1], starts[atom, 2]
    ahead = wrapped(z_start - corner[0], all_planes)
    depth = [jnp.minimum(wrapped(ahead + dz, all_planes), planes - 1) for dz in range(WIDE)]
    z_in = wrapped(ahead + lane // STRIDE, all_planes) < planes
    first = wrapped(lax.shift_right_logical(y_start, 3) - corner[1], all_tiles)
    tile_pair = (first, wrapped(first + 1, all_tiles))
    group = lax.shift_right_logical(x_start, 7)
    lane_pair = (group, wrapped(group + 1, all_groups))
    return depth, z_in, tile_pair, lane_pair, y_start & 7, x_start & 127


def corner_of(z, tile, group):
    return z, tile, slice(None), pl.ds(pl.multiple_of(group * 128, 128), 128)


def pick_kernel(total, starts, corner, spots, field, values, listing):
    values[...] = jnp.zeros_like(values)
    planes, tiles = field.shape[:2]

    def at(z, tile, group):
        return field[corner_of(z, tile, group)]

    lane = lax.broadcasted_iota(jnp.int32, (8, 128), 1)
    row = lax.broadcasted_iota(jnp.int32, (8, 128), 0)
    slot = lax.broadcasted_iota(jnp.int32, (128, 128), 0)
    count = listed(starts, corner, total, planes, tiles, listing)

    def some(group, carry):
        for k in range(TOGETHER):
            atom = listing[jnp.minimum(group * TOGETHER + k, count - 1)]
            depth, z_in, tile_pair, groups, down, right = placed(
                starts, corner, total, atom, planes, tiles, lane
            )
            t0, t1 = (jnp.minimum(t, tiles - 1) for t in tile_pair)
            window = jnp.zeros((8, 128), jnp.float32)
            for dz, z in enumerate(depth):
                upper = jnp.where(lane >= right, at(z, t0, groups[0]), at(z, t0, groups[1]))
                lower = jnp.where(lane >= right, at(z, t1, groups[0]), at(z, t1, groups[1]))
                met = jnp.where(row >= down, upper, lower)
                met = pltpu.roll(met, (STRIDE * dz - right) & 127, 1)
                window = jnp.where(lane // STRIDE == dz, met, window)
            window = pltpu.roll(window, (8 - down) & 7, 0)
            tile_of = jnp.where(row < 8 - down, tile_pair[0], tile_pair[1])
            window = jnp.where(z_in & (tile_of < tiles), window, 0.0)
            spot = spots[atom]
            chosen = (slot == spot[1:2]).astype(jnp.float32).astype(jnp.bfloat16)
            found = jnp.dot(split3(window), chosen, preferred_element_type=jnp.float32)
            found = found[0:8] + found[8:16] + found[16:24]
            found = jnp.where(row == spot[0:1], found, 0.0)
            values[pl.ds(atom, 1)] = jnp.sum(found, axis=0, keepdims=True)[None]
        return carry

    lax.fori_loop(0, (count + TOGETHER - 1) // TOGETHER, some, 0)


def pick_block_kernel(total, starts, corner, spots, field, values, listing):
    values[...] = jnp.zeros_like(values)
    orbitals, planes = field.shape[:2]
    lane = lax.broadcasted_iota(jnp.int32, (8, 128), 1)
    row = lax.broadcasted_iota(jnp.int32, (8, 128), 0)
    slot = lax.broadcasted_iota(jnp.int32, (128, 128), 0)
    count = listed(starts, corner, total, planes, 1, listing, one_group=True)

    def some(group, carry):
        for k in range(TOGETHER):
            atom = listing[jnp.minimum(group * TOGETHER + k, count - 1)]
            depth, z_in, tile_pair, groups, down, right = placed(
                starts, corner, total, atom, planes, 1, lane
            )
            inside = jnp.where(row >= down, tile_pair[0], tile_pair[1]) == 0
            inside = inside & (jnp.where(lane >= right, groups[0], groups[1]) == corner[2])
            spot = spots[atom]
            chosen = (slot == spot[1:2]).astype(jnp.float32).astype(jnp.bfloat16)
            for o in range(orbitals):
                window = jnp.zeros((8, 128), jnp.float32)
                for dz, z in enumerate(depth):
                    met = jnp.where(inside, field[o, z], 0.0)
                    met = pltpu.roll(met, (STRIDE * dz - right) & 127, 1)
                    window = jnp.where(lane // STRIDE == dz, met, window)
                window = jnp.where(z_in, pltpu.roll(window, (8 - down) & 7, 0), 0.0)
                found = jnp.dot(split3(window), chosen, preferred_element_type=jnp.float32)
                found = found[0:8] + found[8:16] + found[16:24]
                found = jnp.where(row == spot[0:1], found, 0.0)
                values[o, pl.ds(atom, 1)] = jnp.sum(found, axis=0, keepdims=True)[None]
        return carry

    lax.fori_loop(0, (count + TOGETHER - 1) // TOGETHER, some, 0)


def put_kernel(total, starts, corner, spots, spread, base, field, listing):
    field[...] = base[...]
    planes, tiles = field.shape[:2]
    lane = lax.broadcasted_iota(jnp.int32, (8, 128), 1)
    row = lax.broadcasted_iota(jnp.int32, (8, 128), 0)
    slot = lax.broadcasted_iota(jnp.int32, (128, 128), 0)
    count = listed(starts, corner, total, planes, tiles, listing)

    def some(group, carry):
        for k in range(TOGETHER):
            at = group * TOGETHER + k
            atom = listing[jnp.minimum(at, count - 1)]
            depth, z_in, (t0, t1), groups, down, right = placed(
                starts, corner, total, atom, planes, tiles, lane
            )
            spot = spots[atom]
            chosen = (slot == spot[1:2]).astype(jnp.float32).astype(jnp.bfloat16)
            amounts = jnp.where(row == spot[0:1], spread[atom], 0.0)
            window = lax.dot_general(
                split3(amounts), chosen, (((1,), (1,)), ((), ())), preferred_element_type=jnp.float32
            )
            window = window[0:8] + window[8:16] + window[16:24]
            window = jnp.where(z_in & (at < count), window, 0.0)
            window = pltpu.roll(window, down, 0)
            for dz, z in enumerate(depth):
                part = jnp.where(lane // STRIDE == dz, window, 0.0)
                part = pltpu.roll(part, (right - STRIDE * dz) & 127, 1)
                spans = range(field.shape[3] // 128)
                places = [(i, g, corner_of(z, t, g)) for i, t in enumerate((t0, t1)) for g in spans]
                before = [field[place] for _, _, place in places]
                for old, (i, g, place) in zip(before, places):
                    inside = (row < down) if i else (row >= down)
                    inside = inside & (jnp.where(lane >= right, groups[0], groups[1]) == g + corner[2])
                    field[place] = old + jnp.where(inside, part, 0.0)
        return carry

    lax.fori_loop(0, (count + TOGETHER - 1) // TOGETHER, some, 0)


def bf16_pair(block):
    high = block.astype(jnp.bfloat16)
    return high, (block - high.astype(jnp.float32)).astype(jnp.bfloat16)


def times(left, right):
    return jnp.dot(left, right, preferred_element_type=jnp.float32)


def in_plane(block, high_tables, low_tables):
    high, low = bf16_pair(block)
    kin = times(high, high_tables[0]) + (times(high, low_tables[0]) + times(low, high_tables[0]))
    return kin + (times(high_tables[1], high) + (times(low_tables[1], high) + times(high_tables[1], low)))


def first_kernel(field, potential, high_tables, low_tables, kin_out, all_out):
    block = field[0]
    kin = in_plane(block, high_tables, low_tables)
    kin_out[0] = kin
    all_out[0] = kin + (potential[0] - 2.0) * block


def second_kernel(weights, field, extra, potential, high_tables, low_tables, out):
    block = field[0]
    total = in_plane(block, high_tables, low_tables) + (potential[0] - 2.0) * block
    total = weights[0] * total + weights[1] * block + weights[2] * extra[0]
    part = out.shape[3]
    for i in range(out.shape[0]):
        out[i, 0] = total[:, i * part : (i + 1) * part]


def depth_times(high_table, low_table, block):
    high, low = bf16_pair(block)
    return times(high_table[...], high) + (times(low_table[...], high) + times(high_table[...], low))


def lines_of(ref, r, rows):
    devices, lines = ref.shape[:2]
    line = pl.ds(r, lines // rows, stride=rows)
    return jnp.concatenate([ref[d, line, :] for d in range(devices)], axis=0)


def out_kernel(some, rows, chunk, weights, field, potential, high_table, low_table, a_out, c_out, b_out):
    everywhere = high_table.shape[0]
    for pair in [(r, r + 1) for r in range(0, some, 2)]:
        v = jnp.concatenate([lines_of(field, r, some) for r in pair], axis=1)
        both = depth_times(high_table, low_table, v)
        for i, r in enumerate(pair):
            a, line = both[:, 128 * i : 128 * i + 128], pl.ds(r, everywhere, stride=some)
            a_out[0, line, :] = a
            c_out[0, line, :] = weights[0] * v[:, 128 * i : 128 * i + 128] + weights[1] * a
            b_out[0, line, :] = weights[1] * (lines_of(potential, chunk * some + r, rows) - 2.0) * a


def back_kernel(some, cuts, weights, g_in, c_in, b_in, high_table, low_table, *outs):
    everywhere = high_table.shape[0]
    devices = outs[0].shape[0]
    mine = everywhere // devices
    for pair in [(r, r + 1) for r in range(0, some, 2)]:
        lines = [pl.ds(r, everywhere, stride=some) for r in pair]
        parts = [c_in[0, line, :] + weights[1] * lines_of(g_in, r, some) for r, line in zip(pair, lines)]
        both = depth_times(high_table, low_table, jnp.concatenate(parts, axis=1))
        for i, (r, line) in enumerate(zip(pair, lines)):
            m = both[:, 128 * i : 128 * i + 128] + b_in[0, line, :]
            for out, (start, stop) in zip(outs, cuts):
                for d in range(devices):
                    out[d, 0, pl.ds(r, stop - start, stride=some), :] = m[mine * d + start : mine * d + stop]


def tiled(field):
    return field.reshape(field.shape[0], field.shape[1] // 8, 8, field.shape[2])


SMEM = pl.BlockSpec(memory_space=pltpu.SMEM)
VMEM = pl.BlockSpec(memory_space=pltpu.VMEM)
PARAMS = pltpu.CompilerParams(vmem_limit_bytes=48 * 2**20)


def ordered(kernel, count, others):
    def run(*refs):
        kernel(*refs[:count], *refs[count + others :])

    return run


ANY = pl.BlockSpec(memory_space=pl.ANY)


def pick(total, starts, corner, spots, field):
    return pl.pallas_call(
        functools.partial(pick_kernel, total),
        out_shape=jax.ShapeDtypeStruct((starts.shape[0], 1, 128), jnp.float32),
        in_specs=[SMEM, SMEM, VMEM, VMEM],
        out_specs=VMEM,
        scratch_shapes=[pltpu.SMEM((starts.shape[0] + 1,), jnp.int32)],
        compiler_params=PARAMS,
        cost_estimate=pl.CostEstimate(flops=1 << 24, bytes_accessed=1 << 24, transcendentals=0),
        name="pick",
    )(starts, corner, spots, tiled(field))


def pick_block(total, starts, corner, spots, field):
    return pl.pallas_call(
        functools.partial(pick_block_kernel, total),
        out_shape=jax.ShapeDtypeStruct((field.shape[0], starts.shape[0], 1, 128), jnp.float32),
        in_specs=[SMEM, SMEM, VMEM, VMEM],
        out_specs=VMEM,
        scratch_shapes=[pltpu.SMEM((starts.shape[0] + 1,), jnp.int32)],
        compiler_params=PARAMS,
        cost_estimate=pl.CostEstimate(flops=1 << 24, bytes_accessed=1 << 24, transcendentals=0),
        name="pick_block",
    )(starts, corner, spots, field)


def put(total, starts, corner, spots, spread, base):
    shaped = tiled(base)
    return pl.pallas_call(
        functools.partial(put_kernel, total),
        out_shape=jax.ShapeDtypeStruct(shaped.shape, jnp.float32),
        in_specs=[SMEM, SMEM, VMEM, VMEM, VMEM],
        out_specs=VMEM,
        scratch_shapes=[pltpu.SMEM((starts.shape[0] + 1,), jnp.int32)],
        compiler_params=PARAMS,
        cost_estimate=pl.CostEstimate(flops=1 << 24, bytes_accessed=1 << 24, transcendentals=0),
        name="put",
    )(starts, corner, spots, spread, shaped).reshape(base.shape)


def halves_of(table):
    high = lax.reduce_precision(table, 8, 7)
    return high.astype(jnp.bfloat16), (table - high).astype(jnp.bfloat16)


def plane_specs(shape):
    plane = pl.BlockSpec((1,) + shape[1:], lambda z: (z, 0, 0))
    return plane, pl.BlockSpec((2,) + shape[1:], lambda z: (0, 0, 0))


def cost(flops, numbers):
    return pl.CostEstimate(flops=flops, bytes_accessed=4 * numbers, transcendentals=0)


def planar_first(field, potential, tables, *others):
    plane, pair = plane_specs(field.shape)
    return pl.pallas_call(
        ordered(first_kernel, 4, len(others)),
        grid=field.shape[:1],
        out_shape=[jax.ShapeDtypeStruct(field.shape, jnp.float32)] * 2,
        in_specs=[plane, plane, pair, pair] + [ANY] * len(others),
        out_specs=[plane, plane],
        compiler_params=PARAMS,
        cost_estimate=cost(12 * field.shape[2] * field.size, 4 * field.size),
        name="planar_first",
    )(field, potential, *tables, *others)


def planar_second(weights, field, extra, potential, tables, parts):
    plane, pair = plane_specs(field.shape)
    planes, rows_y, cols_x = field.shape
    shape = (parts, planes, rows_y, cols_x // parts)
    return pl.pallas_call(
        second_kernel,
        grid=field.shape[:1],
        out_shape=jax.ShapeDtypeStruct(shape, jnp.float32),
        in_specs=[SMEM, plane, plane, plane, pair, pair],
        out_specs=pl.BlockSpec((parts, 1) + shape[2:], lambda z: (0, z, 0, 0)),
        compiler_params=PARAMS,
        cost_estimate=cost(12 * field.shape[2] * field.size, 4 * field.size),
        name="planar_second",
    )(weights, field, extra, potential, *tables)


def tie(block, *others):
    return pl.pallas_call(
        lambda *refs: None,
        out_shape=jax.ShapeDtypeStruct(block.shape, block.dtype),
        in_specs=[ANY] * (1 + len(others)),
        out_specs=ANY,
        input_output_aliases={0: 0},
        cost_estimate=cost(0, 0),
        name="tie",
    )(block, *others)


def append_kernel(first, others, numbers, block, *refs):
    out, sem = refs[others], refs[others + 1]
    copies = [
        pltpu.make_async_copy(
            numbers.at[d % numbers.shape[0]], out.at[d, pl.ds(first, numbers.shape[1]), :], sem.at[d]
        )
        for d in range(out.shape[0])
    ]
    for copy in copies:
        copy.start()
    for copy in copies:
        copy.wait()


def append(block, numbers, *others):
    devices, lines, wide = block.shape
    return pl.pallas_call(
        functools.partial(append_kernel, lines - numbers.shape[1], len(others)),
        out_shape=jax.ShapeDtypeStruct(block.shape, block.dtype),
        in_specs=[VMEM, ANY] + [ANY] * len(others),
        out_specs=ANY,
        scratch_shapes=[pltpu.SemaphoreType.DMA((devices,))],
        input_output_aliases={1: 0},
        cost_estimate=cost(0, 2 * numbers.size),
        name="append",
    )(numbers, block, *others)


def pack_kernel(count, chunks, chosen, together, *refs):
    fields, out = refs[:count], refs[-1]
    planes, rows, _ = fields[0].shape
    some = rows // chunks // together
    lines = planes * some
    for d in range(together):
        for g in range(out.shape[0]):
            for at, i in enumerate(chosen):
                start = (d * chunks + i) * some
                cells = (slice(None), slice(start, start + some), slice(128 * g, 128 * g + 128))
                part = fields[0][cells]
                for field in fields[1:]:
                    part = part + field[cells]
                out[g, d, at * lines : at * lines + lines, :] = part.reshape(lines, 128)


def pack(fields, devices, chunks, chosen, spare, *others):
    planes, rows_y, cols = fields[0].shape
    rows, groups = rows_y // devices, cols // 128
    together = math.gcd(devices, 4)
    lines = planes * rows * len(chosen) // chunks
    block = pl.BlockSpec((planes, rows * together, cols), lambda d: (0, d, 0))
    got = pl.pallas_call(
        ordered(functools.partial(pack_kernel, len(fields), chunks, chosen, together), len(fields), len(others)),
        grid=(devices // together,),
        out_shape=jax.ShapeDtypeStruct((groups, devices, lines + spare, 128), jnp.float32),
        in_specs=[block] * len(fields) + [ANY] * len(others),
        out_specs=pl.BlockSpec((groups, together, lines, 128), lambda d: (0, d, 0, 0)),
        compiler_params=PARAMS,
        cost_estimate=cost(groups * devices * lines * 128, 2 * groups * devices * lines * 128),
        name="pack",
    )(*fields, *others)
    return got.reshape(groups * devices, lines + spare, 128)


def pack_part_kernel(place, field, out):
    planes, rows, _ = field.shape
    each = rows // out.shape[0]
    for d in range(out.shape[0]):
        out[d] = field[:, d * each : (d + 1) * each, :].reshape(planes * each, 128)


def pack_part(field, devices, place):
    planes, rows_y, _ = field.shape
    together = math.gcd(devices, 4)
    lines = planes * rows_y // devices
    return pl.pallas_call(
        pack_part_kernel,
        grid_spec=pltpu.PrefetchScalarGridSpec(
            num_scalar_prefetch=1,
            grid=(devices // together,),
            in_specs=[pl.BlockSpec((planes, rows_y // devices * together, 128), lambda d, place: (0, d, place[0]))],
            out_specs=pl.BlockSpec((together, lines, 128), lambda d, place: (d, 0, 0)),
        ),
        out_shape=jax.ShapeDtypeStruct((devices, lines, 128), jnp.float32),
        compiler_params=PARAMS,
        cost_estimate=cost(0, 2 * devices * lines * 128),
        name="pack_part",
    )(place, field)


def join_kernel(spans, planes, begin, place, *refs):
    out = refs[-1]
    devices, some = refs[0].shape[1:3]
    rows = out.shape[1] // devices
    first = begin + pl.program_id(0) * planes
    mine = place[0] == 0
    for (chunk, start, stop), own, other in zip(spans, refs[0::2], refs[1::2]):

        @pl.when((first >= start) & (first < stop))
        def _(chunk=chunk, own=own, other=other):
            a, b = own[...], other[...]
            left, right = jnp.where(mine, a, b), jnp.where(mine, b, a)
            for d in range(devices):
                lines = slice(d * rows + chunk * some, d * rows + (chunk + 1) * some)
                out[:, lines, 0:128] = left[:, d]
                out[:, lines, 128:256] = right[:, d]


def join(shape, spans, place, pairs, begin, end, before):
    planes = end - begin
    for _, start, stop in spans:
        planes = math.gcd(planes, start, stop)
    planes = math.gcd(planes, begin, 4)
    specs, blocks = [SMEM], []
    for (_, start, stop), pair in zip(spans, pairs):
        shift, count = (begin - start) // planes, (stop - start) // planes
        block = (planes,) + pair[0].shape[1:]
        spec = pl.BlockSpec(block, lambda z, shift=shift, count=count: (jnp.clip(z + shift, 0, count - 1), 0, 0, 0))
        specs += [spec, spec]
        blocks += pair
    return pl.pallas_call(
        ordered(functools.partial(join_kernel, spans, planes, begin), 1 + len(blocks), len(before)),
        grid=((end - begin) // planes,),
        out_shape=jax.ShapeDtypeStruct(shape, jnp.float32),
        in_specs=specs + [ANY] * len(before),
        out_specs=pl.BlockSpec((planes,) + shape[1:], lambda z: (z + begin // planes, 0, 0)),
        input_output_aliases={1 + len(blocks): 0} if before else {},
        compiler_params=PARAMS,
        cost_estimate=cost(0, 2 * math.prod(shape) * (end - begin) // shape[0]),
        name="join",
    )(place, *blocks, *before)


def depth_specs(planes, some, devices, chunk):
    got = pl.BlockSpec((devices, planes // devices * some, 128), lambda o: (o, chunk, 0))
    flat = pl.BlockSpec((1, planes * some, 128), lambda o: (o, 0, 0))
    return got, flat, pl.BlockSpec((planes, planes), lambda o: (0, 0))


def depth_out(weights, field, potential, some, chunk, orbitals, tables):
    devices, planes = potential.shape[0], tables[0].shape[0]
    rows = potential.shape[1] * devices // planes
    got, flat, table = depth_specs(planes, some, devices, chunk)
    well = pl.BlockSpec(potential.shape, lambda o: (0, 0, 0))
    size = orbitals * planes * some * 128
    return pl.pallas_call(
        functools.partial(out_kernel, some, rows, chunk),
        grid=(orbitals,),
        out_shape=[jax.ShapeDtypeStruct((orbitals, planes * some, 128), jnp.float32)] * 3,
        in_specs=[SMEM, got, well, table, table],
        out_specs=[flat] * 3,
        compiler_params=PARAMS,
        cost_estimate=cost(6 * planes * size, 5 * size),
        name="depth_out",
    )(weights, field, potential, *tables)


def depth_back(weights, g, c, b, some, devices, cuts, tables, *others):
    orbitals, planes = c.shape[0], tables[0].shape[0]
    got, flat, table = depth_specs(planes, some, devices, 0)
    each = [(stop - start) * some for start, stop in cuts]
    return pl.pallas_call(
        ordered(functools.partial(back_kernel, some, cuts), 6, len(others)),
        grid=(orbitals,),
        out_shape=[jax.ShapeDtypeStruct((devices, orbitals, n, 128), jnp.float32) for n in each],
        in_specs=[SMEM, got, flat, flat, table, table] + [ANY] * len(others),
        out_specs=[pl.BlockSpec((devices, 1, n, 128), lambda o: (0, o, 0, 0)) for n in each],
        compiler_params=PARAMS,
        cost_estimate=cost(6 * planes * c.size, 4 * c.size),
        name="depth_back",
    )(weights, g, c, b, *tables, *others)


def atom_windows(cells, all_planes, rows_y, cols_x):
    parts = []
    for coords, size in (
        (cells[:, 0], all_planes),
        (cells[:, 1] // cols_x, rows_y),
        (cells[:, 1] % cols_x, cols_x),
    ):
        anchor = coords[:, :1]
        apart = (coords - anchor + size // 2) % size - size // 2
        least = jnp.min(apart, axis=1, keepdims=True)
        parts.append(((anchor + least) % size, apart - least))
    starts = jnp.concatenate([start for start, _ in parts], axis=1)
    (_, off_z), (_, off_y), (_, off_x) = parts
    spots = jnp.stack([off_y, off_z * STRIDE + off_x], axis=1)
    return starts.astype(jnp.int32), spots.astype(jnp.int32)


def local(random_orbitals, potential, sphere_cells, projectors, kb_energy, cheb_coef):
    grid_count = lax.axis_size("grid")
    grid_pos = lax.axis_index("grid")
    orb_groups = lax.axis_size("orb")
    orb_pos = lax.axis_index("orb")
    planes, rows_y, cols_x = potential.shape
    all_planes = planes * grid_count
    rows = rows_y // grid_count
    orb_count = random_orbitals.shape[0]
    per_dev, projs_each = projectors.shape[:2]
    atoms = per_dev * grid_count
    chunks = 2 if rows % 16 == 0 else 1
    some = rows // chunks
    part = cols_x // orb_groups
    put_late = part % 128 == 0
    joint = orb_groups == 2 and part == 128
    c0, c1, c2 = cheb_coef[0], cheb_coef[1], cheb_coef[2]
    c1_4 = c1 / 4.0
    c2_8 = c2 / 8.0
    planar_tables = [jnp.stack(pair) for pair in zip(halves_of(kinetic_table(cols_x)), halves_of(kinetic_table(rows_y)))]
    kinetic_z = kinetic_table(all_planes)
    depth_tables = halves_of(kinetic_z)
    total = (all_planes, rows_y // 8, cols_x // 128)

    lines = planes * some
    fast = part == 128 and planes % 8 == 0 and some % 8 == 0
    orbitals = orb_groups

    def packed(fields, chosen, spare, *others):
        if fast:
            return pack(fields, grid_count, chunks, chosen, spare, *others)
        field = sum(fields[1:], fields[0]).reshape(planes, grid_count, chunks, some, orb_groups, part)
        field = jnp.stack([field[:, :, i] for i in chosen]).transpose(4, 2, 0, 1, 3, 5)
        field = field.reshape(orb_groups * grid_count, len(chosen) * lines, part)
        return jnp.concatenate([field, jnp.zeros((field.shape[0], spare, part), jnp.float32)], axis=1)

    def along_z(field):
        return jnp.einsum("wz,ozyx->owyx", kinetic_z, field, precision=PRECISE)

    def everyones(block):
        return exchange(block, ("orb", "grid"))

    if fast:
        mine = pack_part(potential, grid_count, orb_pos[None])
        mine = mine.reshape(grid_count, planes, rows, part)
    else:
        mine = lax.dynamic_slice_in_dim(potential, orb_pos * part, part, axis=2)
        mine = mine.reshape(planes, grid_count, rows, part).transpose(1, 0, 2, 3)

    raw = jnp.concatenate([sphere_cells.astype(jnp.float32), projectors], axis=1)
    here = [(grid_pos + grid_count + step) % grid_count for step in (-1, 0, 1)]

    def shifted(block, step):
        return lax.ppermute(block, "grid", [(i, (i + step) % grid_count) for i in range(grid_count)])

    low = 1 << ((grid_count.bit_length() - 1) // 2)
    high = grid_count // low
    column = gather_part(raw, "grid", low.bit_length() - 1, high)
    gots = [shifted(raw, 1), shifted(raw, -1)]
    near = jnp.concatenate([gots[0], raw, gots[1]])
    near_projs = near[:, 2:]
    near_starts, near_spots = atom_windows(near[:, :2].astype(jnp.int32), all_planes, rows_y, cols_x)
    zero = jnp.zeros_like(grid_pos)
    slab_corner = jnp.stack([grid_pos * planes, zero, zero])

    def partial_near(field):
        values = pick(total, near_starts, slab_corner, near_spots, field)
        coeffs = jnp.einsum("aj,apj->ap", values[:, 0], near_projs, precision=PRECISE)
        return coeffs.reshape(3, per_dev, projs_each)

    def whole_near(coeffs):
        steps = 1 if planes >= WIDE else 2
        whole = coeffs
        for step in [s for s in range(-steps, steps + 1) if s]:
            got = shifted(coeffs, step)
            moved = jnp.zeros_like(coeffs)
            for i in range(3):
                if 0 <= i - step < 3:
                    moved = moved.at[i - step].set(got[i])
            whole = whole + moved
        return whole.reshape(3 * per_dev, projs_each)

    def everywhere(coeffs):
        out = jnp.zeros((grid_count, per_dev, projs_each), jnp.float32)
        for i, slab in enumerate(here):
            out = lax.dynamic_update_slice_in_dim(out, coeffs[i : i + 1], slab, 0)
        return out.reshape(atoms, projs_each)

    def nearby(coeffs):
        coeffs = coeffs.reshape(grid_count, per_dev, projs_each)
        return jnp.concatenate([lax.dynamic_index_in_dim(coeffs, slab, 0, keepdims=False) for slab in here])

    def put_near(coeffs, base, corner=slab_corner):
        spread = jnp.einsum("ap,apj->aj", coeffs * kb_energy, near_projs, precision=PRECISE)
        return put(total, near_starts, corner, near_spots, spread[:, None], base)

    got_potential = exchange(tie(mine, *gots), "grid")
    got_potential = got_potential.reshape(grid_count, planes * rows, part)

    late = planes // 4 * 3
    cuts = [[(0, planes)]] * (chunks - 1) + [[(0, late), (late, planes)] if planes % 16 == 0 else [(0, planes)]]
    sums = [[0.0] * len(cut) for cut in cuts]
    weights = jnp.stack([c1_4, c2_8])
    for orb in range(orb_count):
        v = random_orbitals[orb]
        first = whole_near(partial_near(v))
        pv, t = planar_first(v, potential, planar_tables, near_spots)
        v_send = packed([v], range(chunks), 0, near_spots)
        if orb == 0:
            every = gather_part(column, "grid", 0, low)
            every = jnp.swapaxes(every, 0, 1).reshape((atoms,) + raw.shape[1:])
            every_projs = every[:, 2:]
            every_starts, every_spots = atom_windows(every[:, :2].astype(jnp.int32), all_planes, rows_y, cols_x)
        v_got = everyones(tie(v_send, first, column))
        u = put_near(first, t)
        base = planar_second(
            jnp.stack([c2_8, c1_4, c0 - c2]), u, v, potential, planar_tables, orb_groups
        )
        second = jnp.zeros((orbitals, atoms, projs_each), jnp.float32)
        second = lax.dynamic_update_slice_in_dim(second, everywhere(partial_near(u))[None], orb_pos, 0)
        g_gots = []
        for i in range(chunks - 1):
            g_gots.append(everyones(tie(packed([pv, u], [i], 0, base), every)))

        cb = []
        for i in range(chunks):
            first_row = grid_pos * rows + i * some
            if fast:
                a, c, b = depth_out(weights, v_got, got_potential, some, i, orbitals, depth_tables)
                corner = jnp.stack([zero, first_row // 8, orb_pos])
                values = pick_block(total, every_starts, corner, every_spots, a.reshape(orbitals, all_planes, some, 128))
            else:
                v_i = v_got.reshape(orbitals, grid_count, chunks, planes, some, part)[:, :, i]
                v_i = v_i.reshape(orbitals, all_planes, some, part)
                well = got_potential.reshape(all_planes, rows, part)[:, i * some : (i + 1) * some]
                a = along_z(v_i)
                c, b = c1_4 * v_i + c2_8 * a, c2_8 * (well - 2.0) * a
                corner = jnp.stack([zero, first_row // 8, zero])
                values = []
                for o in range(orbitals):
                    padded = jnp.zeros((all_planes, -(-some // 8) * 8, cols_x), jnp.float32)
                    padded = lax.dynamic_update_slice(padded, a[o], (0, first_row % 8, orb_pos * part))
                    values.append(pick(total, every_starts, corner, every_spots, padded))
                values = jnp.stack(values)
            cb.append((c, b))
            second = second + jnp.einsum("oaj,apj->oap", values[:, :, 0], every_projs, precision=PRECISE)
        if put_late:
            mixed = trade(base, "orb", values)
        second = c2_8 * second
        if fast:
            each = second.reshape(orbitals, grid_count, per_dev, projs_each)
            each = jnp.stack([jnp.roll(each, 1, axis=1), each, jnp.roll(each, -1, axis=1)], axis=2)
            each = jnp.moveaxis(each, 1, 0).reshape(grid_count, -1)
            size = each.shape[1]
            more = -(-size // 1024) * 8
            each = jnp.pad(each, ((0, 0), (0, more * 128 - size))).reshape(grid_count, more, 128)
            g_last = everyones(append(packed([pv, u], [chunks - 1], more, base), each, mixed))
            second = jnp.sum(g_last[:, lines:], axis=0).reshape(-1)[:size]
            second = second.reshape(orbitals, 3 * per_dev, projs_each)
        else:
            g_last = everyones(packed([pv, u], [chunks - 1], 0, base))
            second = lax.psum(second, ("orb", "grid"))
            second = jnp.stack([nearby(second[o]) for o in range(orbitals)])
        g_gots.append(g_last)
        if put_late:
            corner = slab_corner + jnp.stack([zero, zero, orb_pos * (part // 128)])
            q_all = jnp.stack([put_near(second[o], mixed[o], corner) for o in range(orb_groups)])
        else:
            base = jnp.moveaxis(base, 0, 2).reshape(planes, rows_y, cols_x)
            own = lax.dynamic_index_in_dim(second, orb_pos, 0, keepdims=False)
            q = put_near(own, base).reshape(planes, rows_y, orb_groups, part)
            q_all = trade(jnp.moveaxis(q, 2, 0), "orb")
        q_all = q_all.reshape(orb_groups, planes, grid_count, chunks, some, part)

        sends = []
        for i in range(chunks):
            if fast:
                later = [q_all] if i > 0 else []
                ms = depth_back(weights, g_gots[i], *cb[i], some, grid_count, cuts[i], depth_tables, *later)
            else:
                c, b = cb[i]
                g = g_gots[i][:, :lines].reshape(orbitals, all_planes, some, part)
                m = (along_z(c + c2_8 * g) + b).reshape(orbitals, grid_count, planes, some, part)
                m = jnp.moveaxis(m, 1, 0)
                ms = [m[:, :, p:q].reshape(grid_count, orbitals, -1, part) for p, q in cuts[i]]
            sends.append(ms)
        kept, pairs, spans = [], [], []
        for i in range(chunks):
            for k, (start, stop) in enumerate(cuts[i]):
                send = sends[i][k]
                if len(kept) > 1:
                    send = tie(send, *([pairs[0][1]] if pairs else kept[:1]), kept[-1])
                got = exchange(send, "grid")
                m = got.reshape(grid_count, orbitals, stop - start, some, part)
                filtered = q_all[:, start:stop, :, i] + m.transpose(1, 2, 0, 3, 4)
                own = jnp.sum(filtered * filtered, axis=0) * (1.0 / (orb_count * orb_groups))
                kept.append(own)
                sums[i][k] = sums[i][k] + own
                if orb == orb_count - 1 and joint:
                    own = sums[i][k]
                    spans.append((i, start, stop))
                    pairs.append((own, lax.ppermute(own, "orb", [(0, 1), (1, 0)])))
    if joint:
        out, begin = [], 0
        for end in sorted({stop for _, _, stop in spans}):
            some = [i for i, (_, start, stop) in enumerate(spans) if start < end and stop > begin]
            parts = [[each[i] for i in some] for each in (spans, pairs)]
            out = [join(potential.shape, parts[0], orb_pos[None], parts[1], begin, end, out)]
            begin = end
        return out[0]
    out = []
    for parts in sums:
        shares = [gather_over(own[None], "orb") for own in parts]
        out.append(jnp.moveaxis(jnp.concatenate(shares, axis=1), 0, 3))
    return jnp.stack(out, axis=2).reshape(planes, rows_y, cols_x)


def solution(mesh):
    in_specs = (
        P("orb", "grid", None, None),
        P("grid", None, None),
        P("grid", None, None),
        P("grid", None, None),
        P(),
        P(),
    )
    out_specs = P("grid", None, None)
    return jax.shard_map(local, mesh=mesh, in_specs=in_specs, out_specs=out_specs, check_vma=False)
```

```python
import functools
import math

import jax
import jax.numpy as jnp
from jax import lax
from jax.experimental import pallas as pl
from jax.experimental.pallas import tpu as pltpu
from jax.sharding import PartitionSpec as P

REACH = 3
WIDE = 2 * REACH + 1
STRIDE = 16
PRECISE = lax.Precision.HIGHEST
TOGETHER = 4


def kinetic_table(length):
    places = jnp.arange(length)
    offset = places[:, None] - places[None, :]
    parity = jnp.where(offset % 2 == 0, 1.0, -1.0).astype(jnp.float32)
    angle_half = offset.astype(jnp.float32) * (math.pi / length)
    sine = jnp.where(offset == 0, 1.0, jnp.sin(angle_half))
    off_diag = parity / (2.0 * sine * sine)
    on_diag = jnp.float32(length * length / 12.0 + 1.0 / 6.0)
    return jnp.where(offset == 0, on_diag, off_diag) * (4.0 / (length * length))


def xor_route(size, bit):
    return [(i, i ^ bit) for i in range(size)]


def gather_part(block, axis, shift, size):
    place = lax.axis_index(axis)
    own = lax.rem(lax.shift_right_logical(place, shift), size)
    out = jnp.broadcast_to(block, (size,) + block.shape)
    for apart in range(1, size):
        got = lax.ppermute(block, axis, xor_route(lax.axis_size(axis), apart << shift))
        out = lax.dynamic_update_slice_in_dim(out, got[None], own ^ apart, 0)
    return out


def gather_over(block, axis):
    size = lax.axis_size(axis)
    return gather_part(block, axis, 0, size).reshape((size * block.shape[0],) + block.shape[1:])


def trade(blocks, axis, *others):
    size = lax.axis_size(axis)
    place = lax.axis_index(axis)
    out = blocks
    for apart in range(1, size):
        sent = lax.dynamic_index_in_dim(blocks, place ^ apart, 0)
        got = lax.ppermute(sent, axis, xor_route(size, apart))
        if others:
            got = tie(got, *others)
        out = lax.dynamic_update_slice_in_dim(out, got, place ^ apart, 0)
    return out, got


def exchange(block, axis):
    return lax.all_to_all(block, axis, split_axis=0, concat_axis=0, tiled=True)


def wrapped(number, size):
    number = jnp.where(number < 0, number + size, number)
    return jnp.where(number >= size, number - size, number)


def listed(starts, corner, total, planes, tiles, listing, one_group=False):
    all_planes, all_tiles, _ = total

    def one(atom, count):
        ahead = wrapped(starts[atom, 0] - corner[0], all_planes)
        tile = wrapped(lax.shift_right_logical(starts[atom, 1], 3) - corner[1], all_tiles)
        near = (ahead < planes) | (ahead > all_planes - WIDE)
        here = near & ((tile < tiles) | (tile == all_tiles - 1))
        if one_group:
            group = lax.shift_right_logical(starts[atom, 2], 7)
            crosses = ((starts[atom, 2] & 127) > 128 - WIDE) & (wrapped(group + 1, total[2]) == corner[2])
            here = here & ((group == corner[2]) | crosses)
        listing[count] = atom
        return count + here.astype(jnp.int32)

    return lax.fori_loop(0, starts.shape[0], one, jnp.int32(0), unroll=8)


def split3(block):
    high = block.astype(jnp.bfloat16).astype(jnp.float32)
    rest = block - high
    middle = rest.astype(jnp.bfloat16).astype(jnp.float32)
    return jnp.concatenate([high, middle, rest - middle], axis=0).astype(jnp.bfloat16)


def placed(starts, corner, total, atom, planes, tiles, lane):
    all_planes, all_tiles, all_groups = total
    z_start, y_start, x_start = starts[atom, 0], starts[atom, 1], starts[atom, 2]
    ahead = wrapped(z_start - corner[0], all_planes)
    depth = [jnp.minimum(wrapped(ahead + dz, all_planes), planes - 1) for dz in range(WIDE)]
    z_in = wrapped(ahead + lane // STRIDE, all_planes) < planes
    first = wrapped(lax.shift_right_logical(y_start, 3) - corner[1], all_tiles)
    tile_pair = (first, wrapped(first + 1, all_tiles))
    group = lax.shift_right_logical(x_start, 7)
    lane_pair = (group, wrapped(group + 1, all_groups))
    return depth, z_in, tile_pair, lane_pair, y_start & 7, x_start & 127


def corner_of(z, tile, group):
    return z, tile, slice(None), pl.ds(pl.multiple_of(group * 128, 128), 128)


def pick_kernel(total, starts, corner, spots, field, values, listing):
    values[...] = jnp.zeros_like(values)
    planes, tiles = field.shape[:2]

    def at(z, tile, group):
        return field[corner_of(z, tile, group)]

    lane = lax.broadcasted_iota(jnp.int32, (8, 128), 1)
    row = lax.broadcasted_iota(jnp.int32, (8, 128), 0)
    slot = lax.broadcasted_iota(jnp.int32, (128, 128), 0)
    count = listed(starts, corner, total, planes, tiles, listing)

    def some(group, carry):
        for k in range(TOGETHER):
            atom = listing[jnp.minimum(group * TOGETHER + k, count - 1)]
            depth, z_in, tile_pair, groups, down, right = placed(
                starts, corner, total, atom, planes, tiles, lane
            )
            t0, t1 = (jnp.minimum(t, tiles - 1) for t in tile_pair)
            window = jnp.zeros((8, 128), jnp.float32)
            for dz, z in enumerate(depth):
                upper = jnp.where(lane >= right, at(z, t0, groups[0]), at(z, t0, groups[1]))
                lower = jnp.where(lane >= right, at(z, t1, groups[0]), at(z, t1, groups[1]))
                met = jnp.where(row >= down, upper, lower)
                met = pltpu.roll(met, (STRIDE * dz - right) & 127, 1)
                window = jnp.where(lane // STRIDE == dz, met, window)
            window = pltpu.roll(window, (8 - down) & 7, 0)
            tile_of = jnp.where(row < 8 - down, tile_pair[0], tile_pair[1])
            window = jnp.where(z_in & (tile_of < tiles), window, 0.0)
            spot = spots[atom]
            chosen = (slot == spot[1:2]).astype(jnp.float32).astype(jnp.bfloat16)
            found = jnp.dot(split3(window), chosen, preferred_element_type=jnp.float32)
            found = found[0:8] + found[8:16] + found[16:24]
            found = jnp.where(row == spot[0:1], found, 0.0)
            values[pl.ds(atom, 1)] = jnp.sum(found, axis=0, keepdims=True)[None]
        return carry

    lax.fori_loop(0, (count + TOGETHER - 1) // TOGETHER, some, 0)


def pick_block_kernel(total, starts, corner, spots, field, values, listing):
    values[...] = jnp.zeros_like(values)
    orbitals, planes = field.shape[:2]
    lane = lax.broadcasted_iota(jnp.int32, (8, 128), 1)
    row = lax.broadcasted_iota(jnp.int32, (8, 128), 0)
    slot = lax.broadcasted_iota(jnp.int32, (128, 128), 0)
    count = listed(starts, corner, total, planes, 1, listing, one_group=True)

    def some(group, carry):
        for k in range(TOGETHER):
            atom = listing[jnp.minimum(group * TOGETHER + k, count - 1)]
            depth, z_in, tile_pair, groups, down, right = placed(
                starts, corner, total, atom, planes, 1, lane
            )
            inside = jnp.where(row >= down, tile_pair[0], tile_pair[1]) == 0
            inside = inside & (jnp.where(lane >= right, groups[0], groups[1]) == corner[2])
            spot = spots[atom]
            chosen = (slot == spot[1:2]).astype(jnp.float32).astype(jnp.bfloat16)
            for o in range(orbitals):
                window = jnp.zeros((8, 128), jnp.float32)
                for dz, z in enumerate(depth):
                    met = jnp.where(inside, field[o, z], 0.0)
                    met = pltpu.roll(met, (STRIDE * dz - right) & 127, 1)
                    window = jnp.where(lane // STRIDE == dz, met, window)
                window = jnp.where(z_in, pltpu.roll(window, (8 - down) & 7, 0), 0.0)
                found = jnp.dot(split3(window), chosen, preferred_element_type=jnp.float32)
                found = found[0:8] + found[8:16] + found[16:24]
                found = jnp.where(row == spot[0:1], found, 0.0)
                values[o, pl.ds(atom, 1)] = jnp.sum(found, axis=0, keepdims=True)[None]
        return carry

    lax.fori_loop(0, (count + TOGETHER - 1) // TOGETHER, some, 0)


def put_kernel(total, starts, corner, spots, spread, base, field, listing):
    field[...] = base[...]
    planes, tiles = field.shape[:2]
    lane = lax.broadcasted_iota(jnp.int32, (8, 128), 1)
    row = lax.broadcasted_iota(jnp.int32, (8, 128), 0)
    slot = lax.broadcasted_iota(jnp.int32, (128, 128), 0)
    count = listed(starts, corner, total, planes, tiles, listing)

    def some(group, carry):
        for k in range(TOGETHER):
            at = group * TOGETHER + k
            atom = listing[jnp.minimum(at, count - 1)]
            depth, z_in, (t0, t1), groups, down, right = placed(
                starts, corner, total, atom, planes, tiles, lane
            )
            spot = spots[atom]
            chosen = (slot == spot[1:2]).astype(jnp.float32).astype(jnp.bfloat16)
            amounts = jnp.where(row == spot[0:1], spread[atom], 0.0)
            window = lax.dot_general(
                split3(amounts), chosen, (((1,), (1,)), ((), ())), preferred_element_type=jnp.float32
            )
            window = window[0:8] + window[8:16] + window[16:24]
            window = jnp.where(z_in & (at < count), window, 0.0)
            window = pltpu.roll(window, down, 0)
            for dz, z in enumerate(depth):
                part = jnp.where(lane // STRIDE == dz, window, 0.0)
                part = pltpu.roll(part, (right - STRIDE * dz) & 127, 1)
                spans = range(field.shape[3] // 128)
                places = [(i, g, corner_of(z, t, g)) for i, t in enumerate((t0, t1)) for g in spans]
                before = [field[place] for _, _, place in places]
                for old, (i, g, place) in zip(before, places):
                    inside = (row < down) if i else (row >= down)
                    inside = inside & (jnp.where(lane >= right, groups[0], groups[1]) == g + corner[2])
                    field[place] = old + jnp.where(inside, part, 0.0)
        return carry

    lax.fori_loop(0, (count + TOGETHER - 1) // TOGETHER, some, 0)


def bf16_pair(block):
    high = block.astype(jnp.bfloat16)
    return high, (block - high.astype(jnp.float32)).astype(jnp.bfloat16)


def times(left, right):
    return jnp.dot(left, right, preferred_element_type=jnp.float32)


def in_plane(block, high_tables, low_tables):
    high, low = bf16_pair(block)
    kin = times(high, high_tables[0]) + (times(high, low_tables[0]) + times(low, high_tables[0]))
    return kin + (times(high_tables[1], high) + (times(low_tables[1], high) + times(high_tables[1], low)))


def first_kernel(field, potential, high_tables, low_tables, kin_out, all_out):
    block = field[0]
    kin = in_plane(block, high_tables, low_tables)
    kin_out[0] = kin
    all_out[0] = kin + (potential[0] - 2.0) * block


def second_kernel(weights, field, extra, potential, high_tables, low_tables, out):
    block = field[0]
    total = in_plane(block, high_tables, low_tables) + (potential[0] - 2.0) * block
    total = weights[0] * total + weights[1] * block + weights[2] * extra[0]
    part = out.shape[3]
    for i in range(out.shape[0]):
        out[i, 0] = total[:, i * part : (i + 1) * part]


def depth_times(high_table, low_table, block):
    high, low = bf16_pair(block)
    return times(high_table[...], high) + (times(low_table[...], high) + times(high_table[...], low))


def lines_of(ref, r, rows):
    devices, lines = ref.shape[:2]
    line = pl.ds(r, lines // rows, stride=rows)
    return jnp.concatenate([ref[d, line, :] for d in range(devices)], axis=0)


def out_kernel(some, rows, chunk, weights, field, potential, high_table, low_table, a_out, c_out, b_out):
    everywhere = high_table.shape[0]
    for pair in [(r, r + 1) for r in range(0, some, 2)]:
        v = jnp.concatenate([lines_of(field, r, some) for r in pair], axis=1)
        both = depth_times(high_table, low_table, v)
        for i, r in enumerate(pair):
            a, line = both[:, 128 * i : 128 * i + 128], pl.ds(r, everywhere, stride=some)
            a_out[0, line, :] = a
            c_out[0, line, :] = weights[0] * v[:, 128 * i : 128 * i + 128] + weights[1] * a
            b_out[0, line, :] = weights[1] * (lines_of(potential, chunk * some + r, rows) - 2.0) * a


def back_kernel(some, cuts, weights, g_in, c_in, b_in, high_table, low_table, *outs):
    everywhere = high_table.shape[0]
    devices = outs[0].shape[0]
    mine = everywhere // devices
    for pair in [(r, r + 1) for r in range(0, some, 2)]:
        lines = [pl.ds(r, everywhere, stride=some) for r in pair]
        parts = [c_in[0, line, :] + weights[1] * lines_of(g_in, r, some) for r, line in zip(pair, lines)]
        both = depth_times(high_table, low_table, jnp.concatenate(parts, axis=1))
        for i, (r, line) in enumerate(zip(pair, lines)):
            m = both[:, 128 * i : 128 * i + 128] + b_in[0, line, :]
            for out, (start, stop) in zip(outs, cuts):
                for d in range(devices):
                    out[d, 0, pl.ds(r, stop - start, stride=some), :] = m[mine * d + start : mine * d + stop]


def tiled(field):
    return field.reshape(field.shape[0], field.shape[1] // 8, 8, field.shape[2])


SMEM = pl.BlockSpec(memory_space=pltpu.SMEM)
VMEM = pl.BlockSpec(memory_space=pltpu.VMEM)
PARAMS = pltpu.CompilerParams(vmem_limit_bytes=48 * 2**20)


def ordered(kernel, count, others):
    def run(*refs):
        kernel(*refs[:count], *refs[count + others :])

    return run


ANY = pl.BlockSpec(memory_space=pl.ANY)


def pick(total, starts, corner, spots, field):
    return pl.pallas_call(
        functools.partial(pick_kernel, total),
        out_shape=jax.ShapeDtypeStruct((starts.shape[0], 1, 128), jnp.float32),
        in_specs=[SMEM, SMEM, VMEM, VMEM],
        out_specs=VMEM,
        scratch_shapes=[pltpu.SMEM((starts.shape[0] + 1,), jnp.int32)],
        compiler_params=PARAMS,
        cost_estimate=pl.CostEstimate(flops=1 << 24, bytes_accessed=1 << 24, transcendentals=0),
        name="pick",
    )(starts, corner, spots, tiled(field))


def pick_block(total, starts, corner, spots, field):
    return pl.pallas_call(
        functools.partial(pick_block_kernel, total),
        out_shape=jax.ShapeDtypeStruct((field.shape[0], starts.shape[0], 1, 128), jnp.float32),
        in_specs=[SMEM, SMEM, VMEM, VMEM],
        out_specs=VMEM,
        scratch_shapes=[pltpu.SMEM((starts.shape[0] + 1,), jnp.int32)],
        compiler_params=PARAMS,
        cost_estimate=pl.CostEstimate(flops=1 << 24, bytes_accessed=1 << 24, transcendentals=0),
        name="pick_block",
    )(starts, corner, spots, field)


def put(total, starts, corner, spots, spread, base):
    shaped = tiled(base)
    return pl.pallas_call(
        functools.partial(put_kernel, total),
        out_shape=jax.ShapeDtypeStruct(shaped.shape, jnp.float32),
        in_specs=[SMEM, SMEM, VMEM, VMEM, VMEM],
        out_specs=VMEM,
        scratch_shapes=[pltpu.SMEM((starts.shape[0] + 1,), jnp.int32)],
        compiler_params=PARAMS,
        cost_estimate=pl.CostEstimate(flops=1 << 24, bytes_accessed=1 << 24, transcendentals=0),
        name="put",
    )(starts, corner, spots, spread, shaped).reshape(base.shape)


def halves_of(table):
    high = lax.reduce_precision(table, 8, 7)
    return high.astype(jnp.bfloat16), (table - high).astype(jnp.bfloat16)


def plane_specs(shape):
    plane = pl.BlockSpec((1,) + shape[1:], lambda z: (z, 0, 0))
    return plane, pl.BlockSpec((2,) + shape[1:], lambda z: (0, 0, 0))


def cost(flops, numbers):
    return pl.CostEstimate(flops=flops, bytes_accessed=4 * numbers, transcendentals=0)


def planar_first(field, potential, tables, *others):
    plane, pair = plane_specs(field.shape)
    return pl.pallas_call(
        ordered(first_kernel, 4, len(others)),
        grid=field.shape[:1],
        out_shape=[jax.ShapeDtypeStruct(field.shape, jnp.float32)] * 2,
        in_specs=[plane, plane, pair, pair] + [ANY] * len(others),
        out_specs=[plane, plane],
        compiler_params=PARAMS,
        cost_estimate=cost(12 * field.shape[2] * field.size, 4 * field.size),
        name="planar_first",
    )(field, potential, *tables, *others)


def planar_second(weights, field, extra, potential, tables, parts):
    plane, pair = plane_specs(field.shape)
    planes, rows_y, cols_x = field.shape
    shape = (parts, planes, rows_y, cols_x // parts)
    return pl.pallas_call(
        second_kernel,
        grid=field.shape[:1],
        out_shape=jax.ShapeDtypeStruct(shape, jnp.float32),
        in_specs=[SMEM, plane, plane, plane, pair, pair],
        out_specs=pl.BlockSpec((parts, 1) + shape[2:], lambda z: (0, z, 0, 0)),
        compiler_params=PARAMS,
        cost_estimate=cost(12 * field.shape[2] * field.size, 4 * field.size),
        name="planar_second",
    )(weights, field, extra, potential, *tables)


def tie(block, *others):
    return pl.pallas_call(
        lambda *refs: None,
        out_shape=jax.ShapeDtypeStruct(block.shape, block.dtype),
        in_specs=[ANY] * (1 + len(others)),
        out_specs=ANY,
        input_output_aliases={0: 0},
        cost_estimate=cost(0, 0),
        name="tie",
    )(block, *others)


def append_kernel(first, others, numbers, block, *refs):
    out, sem = refs[others], refs[others + 1]
    copies = [
        pltpu.make_async_copy(
            numbers.at[d % numbers.shape[0]], out.at[d, pl.ds(first, numbers.shape[1]), :], sem.at[d]
        )
        for d in range(out.shape[0])
    ]
    for copy in copies:
        copy.start()
    for copy in copies:
        copy.wait()


def append(block, numbers, *others):
    devices, lines, wide = block.shape
    return pl.pallas_call(
        functools.partial(append_kernel, lines - numbers.shape[1], len(others)),
        out_shape=jax.ShapeDtypeStruct(block.shape, block.dtype),
        in_specs=[VMEM, ANY] + [ANY] * len(others),
        out_specs=ANY,
        scratch_shapes=[pltpu.SemaphoreType.DMA((devices,))],
        input_output_aliases={1: 0},
        cost_estimate=cost(0, 2 * numbers.size),
        name="append",
    )(numbers, block, *others)


def pack_kernel(count, chunks, chosen, together, *refs):
    fields, out = refs[:count], refs[-1]
    planes, rows, _ = fields[0].shape
    some = rows // chunks // together
    lines = planes * some
    for d in range(together):
        for g in range(out.shape[0]):
            for at, i in enumerate(chosen):
                start = (d * chunks + i) * some
                cells = (slice(None), slice(start, start + some), slice(128 * g, 128 * g + 128))
                part = fields[0][cells]
                for field in fields[1:]:
                    part = part + field[cells]
                out[g, d, at * lines : at * lines + lines, :] = part.reshape(lines, 128)


def pack(fields, devices, chunks, chosen, spare, *others):
    planes, rows_y, cols = fields[0].shape
    rows, groups = rows_y // devices, cols // 128
    together = math.gcd(devices, 4)
    lines = planes * rows * len(chosen) // chunks
    block = pl.BlockSpec((planes, rows * together, cols), lambda d: (0, d, 0))
    got = pl.pallas_call(
        ordered(functools.partial(pack_kernel, len(fields), chunks, chosen, together), len(fields), len(others)),
        grid=(devices // together,),
        out_shape=jax.ShapeDtypeStruct((groups, devices, lines + spare, 128), jnp.float32),
        in_specs=[block] * len(fields) + [ANY] * len(others),
        out_specs=pl.BlockSpec((groups, together, lines, 128), lambda d: (0, d, 0, 0)),
        compiler_params=PARAMS,
        cost_estimate=cost(groups * devices * lines * 128, 2 * groups * devices * lines * 128),
        name="pack",
    )(*fields, *others)
    return got.reshape(groups * devices, lines + spare, 128)


def pack_part_kernel(place, field, out):
    planes, rows, _ = field.shape
    each = rows // out.shape[0]
    for d in range(out.shape[0]):
        out[d] = field[:, d * each : (d + 1) * each, :].reshape(planes * each, 128)


def pack_part(field, devices, place):
    planes, rows_y, _ = field.shape
    together = math.gcd(devices, 4)
    lines = planes * rows_y // devices
    return pl.pallas_call(
        pack_part_kernel,
        grid_spec=pltpu.PrefetchScalarGridSpec(
            num_scalar_prefetch=1,
            grid=(devices // together,),
            in_specs=[pl.BlockSpec((planes, rows_y // devices * together, 128), lambda d, place: (0, d, place[0]))],
            out_specs=pl.BlockSpec((together, lines, 128), lambda d, place: (d, 0, 0)),
        ),
        out_shape=jax.ShapeDtypeStruct((devices, lines, 128), jnp.float32),
        compiler_params=PARAMS,
        cost_estimate=cost(0, 2 * devices * lines * 128),
        name="pack_part",
    )(place, field)


def join_kernel(spans, planes, begin, place, *refs):
    out = refs[-1]
    devices, some = refs[0].shape[1:3]
    rows = out.shape[1] // devices
    first = begin + pl.program_id(0) * planes
    mine = place[0] == 0
    for (chunk, start, stop), own, other in zip(spans, refs[0::2], refs[1::2]):

        @pl.when((first >= start) & (first < stop))
        def _(chunk=chunk, own=own, other=other):
            a, b = own[...], other[...]
            left, right = jnp.where(mine, a, b), jnp.where(mine, b, a)
            for d in range(devices):
                lines = slice(d * rows + chunk * some, d * rows + (chunk + 1) * some)
                out[:, lines, 0:128] = left[:, d]
                out[:, lines, 128:256] = right[:, d]


def join(shape, spans, place, pairs, begin, end, before):
    planes = end - begin
    for _, start, stop in spans:
        planes = math.gcd(planes, start, stop)
    planes = math.gcd(planes, begin, 4)
    specs, blocks = [SMEM], []
    for (_, start, stop), pair in zip(spans, pairs):
        shift, count = (begin - start) // planes, (stop - start) // planes
        block = (planes,) + pair[0].shape[1:]
        spec = pl.BlockSpec(block, lambda z, shift=shift, count=count: (jnp.clip(z + shift, 0, count - 1), 0, 0, 0))
        specs += [spec, spec]
        blocks += pair
    return pl.pallas_call(
        ordered(functools.partial(join_kernel, spans, planes, begin), 1 + len(blocks), len(before)),
        grid=((end - begin) // planes,),
        out_shape=jax.ShapeDtypeStruct(shape, jnp.float32),
        in_specs=specs + [ANY] * len(before),
        out_specs=pl.BlockSpec((planes,) + shape[1:], lambda z: (z + begin // planes, 0, 0)),
        input_output_aliases={1 + len(blocks): 0} if before else {},
        compiler_params=PARAMS,
        cost_estimate=cost(0, 2 * math.prod(shape) * (end - begin) // shape[0]),
        name="join",
    )(place, *blocks, *before)


def depth_specs(planes, some, devices, chunk):
    got = pl.BlockSpec((devices, planes // devices * some, 128), lambda o: (o, chunk, 0))
    flat = pl.BlockSpec((1, planes * some, 128), lambda o: (o, 0, 0))
    return got, flat, pl.BlockSpec((planes, planes), lambda o: (0, 0))


def depth_out(weights, field, potential, some, chunk, orbitals, tables):
    devices, planes = potential.shape[0], tables[0].shape[0]
    rows = potential.shape[1] * devices // planes
    got, flat, table = depth_specs(planes, some, devices, chunk)
    well = pl.BlockSpec(potential.shape, lambda o: (0, 0, 0))
    size = orbitals * planes * some * 128
    return pl.pallas_call(
        functools.partial(out_kernel, some, rows, chunk),
        grid=(orbitals,),
        out_shape=[jax.ShapeDtypeStruct((orbitals, planes * some, 128), jnp.float32)] * 3,
        in_specs=[SMEM, got, well, table, table],
        out_specs=[flat] * 3,
        compiler_params=PARAMS,
        cost_estimate=cost(6 * planes * size, 5 * size),
        name="depth_out",
    )(weights, field, potential, *tables)


def depth_back(weights, g, c, b, some, devices, cuts, tables, *others):
    orbitals, planes = c.shape[0], tables[0].shape[0]
    got, flat, table = depth_specs(planes, some, devices, 0)
    each = [(stop - start) * some for start, stop in cuts]
    return pl.pallas_call(
        ordered(functools.partial(back_kernel, some, cuts), 6, len(others)),
        grid=(orbitals,),
        out_shape=[jax.ShapeDtypeStruct((devices, orbitals, n, 128), jnp.float32) for n in each],
        in_specs=[SMEM, got, flat, flat, table, table] + [ANY] * len(others),
        out_specs=[pl.BlockSpec((devices, 1, n, 128), lambda o: (0, o, 0, 0)) for n in each],
        compiler_params=PARAMS,
        cost_estimate=cost(6 * planes * c.size, 4 * c.size),
        name="depth_back",
    )(weights, g, c, b, *tables, *others)


def atom_windows(cells, all_planes, rows_y, cols_x):
    parts = []
    for coords, size in (
        (cells[:, 0], all_planes),
        (cells[:, 1] // cols_x, rows_y),
        (cells[:, 1] % cols_x, cols_x),
    ):
        anchor = coords[:, :1]
        apart = (coords - anchor + size // 2) % size - size // 2
        least = jnp.min(apart, axis=1, keepdims=True)
        parts.append(((anchor + least) % size, apart - least))
    starts = jnp.concatenate([start for start, _ in parts], axis=1)
    (_, off_z), (_, off_y), (_, off_x) = parts
    spots = jnp.stack([off_y, off_z * STRIDE + off_x], axis=1)
    return starts.astype(jnp.int32), spots.astype(jnp.int32)


def local(random_orbitals, potential, sphere_cells, projectors, kb_energy, cheb_coef):
    grid_count = lax.axis_size("grid")
    grid_pos = lax.axis_index("grid")
    orb_groups = lax.axis_size("orb")
    orb_pos = lax.axis_index("orb")
    planes, rows_y, cols_x = potential.shape
    all_planes = planes * grid_count
    rows = rows_y // grid_count
    orb_count = random_orbitals.shape[0]
    per_dev, projs_each = projectors.shape[:2]
    atoms = per_dev * grid_count
    chunks = 2 if rows % 16 == 0 else 1
    some = rows // chunks
    part = cols_x // orb_groups
    put_late = part % 128 == 0
    joint = orb_groups == 2 and part == 128
    c0, c1, c2 = cheb_coef[0], cheb_coef[1], cheb_coef[2]
    c1_4 = c1 / 4.0
    c2_8 = c2 / 8.0
    planar_tables = [jnp.stack(pair) for pair in zip(halves_of(kinetic_table(cols_x)), halves_of(kinetic_table(rows_y)))]
    kinetic_z = kinetic_table(all_planes)
    depth_tables = halves_of(kinetic_z)
    total = (all_planes, rows_y // 8, cols_x // 128)

    lines = planes * some
    fast = part == 128 and planes % 8 == 0 and some % 8 == 0
    orbitals = orb_groups

    def packed(fields, chosen, spare, *others):
        if fast:
            return pack(fields, grid_count, chunks, chosen, spare, *others)
        field = sum(fields[1:], fields[0]).reshape(planes, grid_count, chunks, some, orb_groups, part)
        field = jnp.stack([field[:, :, i] for i in chosen]).transpose(4, 2, 0, 1, 3, 5)
        field = field.reshape(orb_groups * grid_count, len(chosen) * lines, part)
        return jnp.concatenate([field, jnp.zeros((field.shape[0], spare, part), jnp.float32)], axis=1)

    def along_z(field):
        return jnp.einsum("wz,ozyx->owyx", kinetic_z, field, precision=PRECISE)

    def everyones(block):
        return exchange(block, ("orb", "grid"))

    if fast:
        mine = pack_part(potential, grid_count, orb_pos[None])
        mine = mine.reshape(grid_count, planes, rows, part)
    else:
        mine = lax.dynamic_slice_in_dim(potential, orb_pos * part, part, axis=2)
        mine = mine.reshape(planes, grid_count, rows, part).transpose(1, 0, 2, 3)

    raw = jnp.concatenate([sphere_cells.astype(jnp.float32), projectors], axis=1)
    here = [(grid_pos + grid_count + step) % grid_count for step in (-1, 0, 1)]

    def shifted(block, step):
        return lax.ppermute(block, "grid", [(i, (i + step) % grid_count) for i in range(grid_count)])

    low = 1 << ((grid_count.bit_length() - 1) // 2)
    high = grid_count // low
    column = gather_part(raw, "grid", low.bit_length() - 1, high)
    gots = [shifted(raw, 1), shifted(raw, -1)]
    near = jnp.concatenate([gots[0], raw, gots[1]])
    near_projs = near[:, 2:]
    near_starts, near_spots = atom_windows(near[:, :2].astype(jnp.int32), all_planes, rows_y, cols_x)
    zero = jnp.zeros_like(grid_pos)
    slab_corner = jnp.stack([grid_pos * planes, zero, zero])

    def partial_near(field):
        values = pick(total, near_starts, slab_corner, near_spots, field)
        coeffs = jnp.einsum("aj,apj->ap", values[:, 0], near_projs, precision=PRECISE)
        return coeffs.reshape(3, per_dev, projs_each)

    def whole_near(coeffs):
        steps = 1 if planes >= WIDE else 2
        whole = coeffs
        for step in [s for s in range(-steps, steps + 1) if s]:
            got = shifted(coeffs, step)
            moved = jnp.zeros_like(coeffs)
            for i in range(3):
                if 0 <= i - step < 3:
                    moved = moved.at[i - step].set(got[i])
            whole = whole + moved
        return whole.reshape(3 * per_dev, projs_each)

    def everywhere(coeffs):
        out = jnp.zeros((grid_count, per_dev, projs_each), jnp.float32)
        for i, slab in enumerate(here):
            out = lax.dynamic_update_slice_in_dim(out, coeffs[i : i + 1], slab, 0)
        return out.reshape(atoms, projs_each)

    def nearby(coeffs):
        coeffs = coeffs.reshape(grid_count, per_dev, projs_each)
        return jnp.concatenate([lax.dynamic_index_in_dim(coeffs, slab, 0, keepdims=False) for slab in here])

    def put_near(coeffs, base, corner=slab_corner):
        spread = jnp.einsum("ap,apj->aj", coeffs * kb_energy, near_projs, precision=PRECISE)
        return put(total, near_starts, corner, near_spots, spread[:, None], base)

    got_potential = exchange(tie(mine, *gots), "grid")
    got_potential = got_potential.reshape(grid_count, planes * rows, part)

    late = planes // 4 * 3
    cuts = [[(0, planes)]] * (chunks - 1) + [[(0, late), (late, planes)] if planes % 16 == 0 else [(0, planes)]]
    sums = [[0.0] * len(cut) for cut in cuts]
    weights = jnp.stack([c1_4, c2_8])
    for orb in range(orb_count):
        v = random_orbitals[orb]
        first = whole_near(partial_near(v))
        pv, t = planar_first(v, potential, planar_tables, near_spots)
        v_send = packed([v], range(chunks), 0, near_spots)
        if orb == 0:
            every = gather_part(column, "grid", 0, low)
            every = jnp.swapaxes(every, 0, 1).reshape((atoms,) + raw.shape[1:])
            every_projs = every[:, 2:]
            every_starts, every_spots = atom_windows(every[:, :2].astype(jnp.int32), all_planes, rows_y, cols_x)
        v_got = everyones(tie(v_send, first, column))
        u = put_near(first, t)
        base = planar_second(
            jnp.stack([c2_8, c1_4, c0 - c2]), u, v, potential, planar_tables, orb_groups
        )
        second = jnp.zeros((orbitals, atoms, projs_each), jnp.float32)
        second = lax.dynamic_update_slice_in_dim(second, everywhere(partial_near(u))[None], orb_pos, 0)
        g_gots = []
        for i in range(chunks - 1):
            g_gots.append(everyones(tie(packed([pv, u], [i], 0, base), every)))

        cb, picked = [], []
        for i in range(chunks):
            first_row = grid_pos * rows + i * some
            if fast:
                a, c, b = depth_out(weights, v_got, got_potential, some, i, orbitals, depth_tables)
                corner = jnp.stack([zero, first_row // 8, orb_pos])
                values = pick_block(total, every_starts, corner, every_spots, a.reshape(orbitals, all_planes, some, 128))
            else:
                v_i = v_got.reshape(orbitals, grid_count, chunks, planes, some, part)[:, :, i]
                v_i = v_i.reshape(orbitals, all_planes, some, part)
                well = got_potential.reshape(all_planes, rows, part)[:, i * some : (i + 1) * some]
                a = along_z(v_i)
                c, b = c1_4 * v_i + c2_8 * a, c2_8 * (well - 2.0) * a
                corner = jnp.stack([zero, first_row // 8, zero])
                values = []
                for o in range(orbitals):
                    padded = jnp.zeros((all_planes, -(-some // 8) * 8, cols_x), jnp.float32)
                    padded = lax.dynamic_update_slice(padded, a[o], (0, first_row % 8, orb_pos * part))
                    values.append(pick(total, every_starts, corner, every_spots, padded))
                values = jnp.stack(values)
            cb.append((c, b))
            picked.append(values)
        if put_late:
            mixed, _ = trade(base, "orb", values)
        values = jnp.einsum("oaj,apj->oap", functools.reduce(jnp.add, picked)[:, :, 0], every_projs, precision=PRECISE)
        second = c2_8 * (second + values)
        if fast:
            each = second.reshape(orbitals, grid_count, per_dev, projs_each)
            each = jnp.stack([jnp.roll(each, 1, axis=1), each, jnp.roll(each, -1, axis=1)], axis=2)
            each = jnp.moveaxis(each, 1, 0).reshape(grid_count, -1)
            size = each.shape[1]
            more = -(-size // 1024) * 8
            each = jnp.pad(each, ((0, 0), (0, more * 128 - size))).reshape(grid_count, more, 128)
            g_last = everyones(append(packed([pv, u], [chunks - 1], more, base), each, mixed))
            second = jnp.sum(g_last[:, lines:], axis=0).reshape(-1)[:size]
            second = second.reshape(orbitals, 3 * per_dev, projs_each)
        else:
            g_last = everyones(packed([pv, u], [chunks - 1], 0, base))
            second = lax.psum(second, ("orb", "grid"))
            second = jnp.stack([nearby(second[o]) for o in range(orbitals)])
        g_gots.append(g_last)
        if put_late:
            corner = slab_corner + jnp.stack([zero, zero, orb_pos * (part // 128)])
            q_all = jnp.stack([put_near(second[o], mixed[o], corner) for o in range(orb_groups)])
        else:
            base = jnp.moveaxis(base, 0, 2).reshape(planes, rows_y, cols_x)
            own = lax.dynamic_index_in_dim(second, orb_pos, 0, keepdims=False)
            q = put_near(own, base).reshape(planes, rows_y, orb_groups, part)
            q_all, _ = trade(jnp.moveaxis(q, 2, 0), "orb")
        q_all = q_all.reshape(orb_groups, planes, grid_count, chunks, some, part)

        sends = []
        for i in range(chunks):
            if fast:
                later = [q_all] if i > 0 else []
                ms = depth_back(weights, g_gots[i], *cb[i], some, grid_count, cuts[i], depth_tables, *later)
            else:
                c, b = cb[i]
                g = g_gots[i][:, :lines].reshape(orbitals, all_planes, some, part)
                m = (along_z(c + c2_8 * g) + b).reshape(orbitals, grid_count, planes, some, part)
                m = jnp.moveaxis(m, 1, 0)
                ms = [m[:, :, p:q].reshape(grid_count, orbitals, -1, part) for p, q in cuts[i]]
            sends.append(ms)
        kept, pairs, spans = [], [], []
        for i in range(chunks):
            for k, (start, stop) in enumerate(cuts[i]):
                send = sends[i][k]
                if len(kept) > 1:
                    send = tie(send, *([pairs[0][1]] if pairs else kept[:1]))
                got = exchange(send, "grid")
                m = got.reshape(grid_count, orbitals, stop - start, some, part)
                filtered = q_all[:, start:stop, :, i] + m.transpose(1, 2, 0, 3, 4)
                own = jnp.sum(filtered * filtered, axis=0) * (1.0 / (orb_count * orb_groups))
                kept.append(own)
                sums[i][k] = sums[i][k] + own
                if orb == orb_count - 1 and joint:
                    own = sums[i][k]
                    spans.append((i, start, stop))
                    pairs.append((own, lax.ppermute(own, "orb", [(0, 1), (1, 0)])))
    if joint:
        out, begin = [], 0
        for end in sorted({stop for _, _, stop in spans}):
            some = [i for i, (_, start, stop) in enumerate(spans) if start < end and stop > begin]
            parts = [[each[i] for i in some] for each in (spans, pairs)]
            out = [join(potential.shape, parts[0], orb_pos[None], parts[1], begin, end, out)]
            begin = end
        return out[0]
    out = []
    for parts in sums:
        shares = [gather_over(own[None], "orb") for own in parts]
        out.append(jnp.moveaxis(jnp.concatenate(shares, axis=1), 0, 3))
    return jnp.stack(out, axis=2).reshape(planes, rows_y, cols_x)


def solution(mesh):
    in_specs = (
        P("orb", "grid", None, None),
        P("grid", None, None),
        P("grid", None, None),
        P("grid", None, None),
        P(),
        P(),
    )
    out_specs = P("grid", None, None)
    return jax.shard_map(local, mesh=mesh, in_specs=in_specs, out_specs=out_specs, check_vma=False)
```

```python
import functools
import math

import jax
import jax.numpy as jnp
from jax import lax
from jax.experimental import pallas as pl
from jax.experimental.pallas import tpu as pltpu
from jax.sharding import PartitionSpec as P

REACH = 3
WIDE = 2 * REACH + 1
STRIDE = 16
PRECISE = lax.Precision.HIGHEST
TOGETHER = 4


def kinetic_table(length):
    places = jnp.arange(length)
    offset = places[:, None] - places[None, :]
    parity = jnp.where(offset % 2 == 0, 1.0, -1.0).astype(jnp.float32)
    angle_half = offset.astype(jnp.float32) * (math.pi / length)
    sine = jnp.where(offset == 0, 1.0, jnp.sin(angle_half))
    off_diag = parity / (2.0 * sine * sine)
    on_diag = jnp.float32(length * length / 12.0 + 1.0 / 6.0)
    return jnp.where(offset == 0, on_diag, off_diag) * (4.0 / (length * length))


def xor_route(size, bit):
    return [(i, i ^ bit) for i in range(size)]


def gather_part(block, axis, shift, size):
    place = lax.axis_index(axis)
    own = lax.rem(lax.shift_right_logical(place, shift), size)
    out = jnp.broadcast_to(block, (size,) + block.shape)
    for apart in range(1, size):
        got = lax.ppermute(block, axis, xor_route(lax.axis_size(axis), apart << shift))
        out = lax.dynamic_update_slice_in_dim(out, got[None], own ^ apart, 0)
    return out


def gather_over(block, axis):
    size = lax.axis_size(axis)
    return gather_part(block, axis, 0, size).reshape((size * block.shape[0],) + block.shape[1:])


def trade(blocks, axis, *others):
    size = lax.axis_size(axis)
    place = lax.axis_index(axis)
    out = blocks
    for apart in range(1, size):
        sent = lax.dynamic_index_in_dim(blocks, place ^ apart, 0)
        got = lax.ppermute(sent, axis, xor_route(size, apart))
        if others:
            got = tie(got, *others)
        out = lax.dynamic_update_slice_in_dim(out, got, place ^ apart, 0)
    return out, got


def exchange(block, axis):
    return lax.all_to_all(block, axis, split_axis=0, concat_axis=0, tiled=True)


def wrapped(number, size):
    number = jnp.where(number < 0, number + size, number)
    return jnp.where(number >= size, number - size, number)


def listed(starts, corner, total, planes, tiles, listing, one_group=False):
    all_planes, all_tiles, _ = total

    def one(atom, count):
        ahead = wrapped(starts[atom, 0] - corner[0], all_planes)
        tile = wrapped(lax.shift_right_logical(starts[atom, 1], 3) - corner[1], all_tiles)
        near = (ahead < planes) | (ahead > all_planes - WIDE)
        here = near & ((tile < tiles) | (tile == all_tiles - 1))
        if one_group:
            group = lax.shift_right_logical(starts[atom, 2], 7)
            crosses = ((starts[atom, 2] & 127) > 128 - WIDE) & (wrapped(group + 1, total[2]) == corner[2])
            here = here & ((group == corner[2]) | crosses)
        listing[count] = atom
        return count + here.astype(jnp.int32)

    return lax.fori_loop(0, starts.shape[0], one, jnp.int32(0), unroll=8)


def split3(block):
    high = block.astype(jnp.bfloat16).astype(jnp.float32)
    rest = block - high
    middle = rest.astype(jnp.bfloat16).astype(jnp.float32)
    return jnp.concatenate([high, middle, rest - middle], axis=0).astype(jnp.bfloat16)


def placed(starts, corner, total, atom, planes, tiles, lane):
    all_planes, all_tiles, all_groups = total
    z_start, y_start, x_start = starts[atom, 0], starts[atom, 1], starts[atom, 2]
    ahead = wrapped(z_start - corner[0], all_planes)
    depth = [jnp.minimum(wrapped(ahead + dz, all_planes), planes - 1) for dz in range(WIDE)]
    z_in = wrapped(ahead + lane // STRIDE, all_planes) < planes
    first = wrapped(lax.shift_right_logical(y_start, 3) - corner[1], all_tiles)
    tile_pair = (first, wrapped(first + 1, all_tiles))
    group = lax.shift_right_logical(x_start, 7)
    lane_pair = (group, wrapped(group + 1, all_groups))
    return depth, z_in, tile_pair, lane_pair, y_start & 7, x_start & 127


def corner_of(z, tile, group):
    return z, tile, slice(None), pl.ds(pl.multiple_of(group * 128, 128), 128)


def pick_kernel(total, starts, corner, spots, field, values, listing):
    values[...] = jnp.zeros_like(values)
    planes, tiles = field.shape[:2]

    def at(z, tile, group):
        return field[corner_of(z, tile, group)]

    lane = lax.broadcasted_iota(jnp.int32, (8, 128), 1)
    row = lax.broadcasted_iota(jnp.int32, (8, 128), 0)
    slot = lax.broadcasted_iota(jnp.int32, (128, 128), 0)
    count = listed(starts, corner, total, planes, tiles, listing)

    def some(group, carry):
        for k in range(TOGETHER):
            atom = listing[jnp.minimum(group * TOGETHER + k, count - 1)]
            depth, z_in, tile_pair, groups, down, right = placed(
                starts, corner, total, atom, planes, tiles, lane
            )
            t0, t1 = (jnp.minimum(t, tiles - 1) for t in tile_pair)
            window = jnp.zeros((8, 128), jnp.float32)
            for dz, z in enumerate(depth):
                upper = jnp.where(lane >= right, at(z, t0, groups[0]), at(z, t0, groups[1]))
                lower = jnp.where(lane >= right, at(z, t1, groups[0]), at(z, t1, groups[1]))
                met = jnp.where(row >= down, upper, lower)
                met = pltpu.roll(met, (STRIDE * dz - right) & 127, 1)
                window = jnp.where(lane // STRIDE == dz, met, window)
            window = pltpu.roll(window, (8 - down) & 7, 0)
            tile_of = jnp.where(row < 8 - down, tile_pair[0], tile_pair[1])
            window = jnp.where(z_in & (tile_of < tiles), window, 0.0)
            spot = spots[atom]
            chosen = (slot == spot[1:2]).astype(jnp.float32).astype(jnp.bfloat16)
            found = jnp.dot(split3(window), chosen, preferred_element_type=jnp.float32)
            found = found[0:8] + found[8:16] + found[16:24]
            found = jnp.where(row == spot[0:1], found, 0.0)
            values[pl.ds(atom, 1)] = jnp.sum(found, axis=0, keepdims=True)[None]
        return carry

    lax.fori_loop(0, (count + TOGETHER - 1) // TOGETHER, some, 0)


def pick_block_kernel(total, starts, corner, spots, field, values, listing):
    values[...] = jnp.zeros_like(values)
    orbitals, planes = field.shape[:2]
    lane = lax.broadcasted_iota(jnp.int32, (8, 128), 1)
    row = lax.broadcasted_iota(jnp.int32, (8, 128), 0)
    slot = lax.broadcasted_iota(jnp.int32, (128, 128), 0)
    count = listed(starts, corner, total, planes, 1, listing, one_group=True)

    def some(group, carry):
        for k in range(TOGETHER):
            atom = listing[jnp.minimum(group * TOGETHER + k, count - 1)]
            depth, z_in, tile_pair, groups, down, right = placed(
                starts, corner, total, atom, planes, 1, lane
            )
            inside = jnp.where(row >= down, tile_pair[0], tile_pair[1]) == 0
            inside = inside & (jnp.where(lane >= right, groups[0], groups[1]) == corner[2])
            spot = spots[atom]
            chosen = (slot == spot[1:2]).astype(jnp.float32).astype(jnp.bfloat16)
            for o in range(orbitals):
                window = jnp.zeros((8, 128), jnp.float32)
                for dz, z in enumerate(depth):
                    met = jnp.where(inside, field[o, z], 0.0)
                    met = pltpu.roll(met, (STRIDE * dz - right) & 127, 1)
                    window = jnp.where(lane // STRIDE == dz, met, window)
                window = jnp.where(z_in, pltpu.roll(window, (8 - down) & 7, 0), 0.0)
                found = jnp.dot(split3(window), chosen, preferred_element_type=jnp.float32)
                found = found[0:8] + found[8:16] + found[16:24]
                found = jnp.where(row == spot[0:1], found, 0.0)
                values[o, pl.ds(atom, 1)] = jnp.sum(found, axis=0, keepdims=True)[None]
        return carry

    lax.fori_loop(0, (count + TOGETHER - 1) // TOGETHER, some, 0)


def put_kernel(total, starts, corner, spots, spread, base, field, listing):
    field[...] = base[...]
    planes, tiles = field.shape[:2]
    lane = lax.broadcasted_iota(jnp.int32, (8, 128), 1)
    row = lax.broadcasted_iota(jnp.int32, (8, 128), 0)
    slot = lax.broadcasted_iota(jnp.int32, (128, 128), 0)
    count = listed(starts, corner, total, planes, tiles, listing)

    def some(group, carry):
        for k in range(TOGETHER):
            at = group * TOGETHER + k
            atom = listing[jnp.minimum(at, count - 1)]
            depth, z_in, (t0, t1), groups, down, right = placed(
                starts, corner, total, atom, planes, tiles, lane
            )
            spot = spots[atom]
            chosen = (slot == spot[1:2]).astype(jnp.float32).astype(jnp.bfloat16)
            amounts = jnp.where(row == spot[0:1], spread[atom], 0.0)
            window = lax.dot_general(
                split3(amounts), chosen, (((1,), (1,)), ((), ())), preferred_element_type=jnp.float32
            )
            window = window[0:8] + window[8:16] + window[16:24]
            window = jnp.where(z_in & (at < count), window, 0.0)
            window = pltpu.roll(window, down, 0)
            for dz, z in enumerate(depth):
                part = jnp.where(lane // STRIDE == dz, window, 0.0)
                part = pltpu.roll(part, (right - STRIDE * dz) & 127, 1)
                spans = range(field.shape[3] // 128)
                places = [(i, g, corner_of(z, t, g)) for i, t in enumerate((t0, t1)) for g in spans]
                before = [field[place] for _, _, place in places]
                for old, (i, g, place) in zip(before, places):
                    inside = (row < down) if i else (row >= down)
                    inside = inside & (jnp.where(lane >= right, groups[0], groups[1]) == g + corner[2])
                    field[place] = old + jnp.where(inside, part, 0.0)
        return carry

    lax.fori_loop(0, (count + TOGETHER - 1) // TOGETHER, some, 0)


def bf16_pair(block):
    high = block.astype(jnp.bfloat16)
    return high, (block - high.astype(jnp.float32)).astype(jnp.bfloat16)


def times(left, right):
    return jnp.dot(left, right, preferred_element_type=jnp.float32)


def in_plane(block, high_tables, low_tables):
    high, low = bf16_pair(block)
    kin = times(high, high_tables[0]) + (times(high, low_tables[0]) + times(low, high_tables[0]))
    return kin + (times(high_tables[1], high) + (times(low_tables[1], high) + times(high_tables[1], low)))


def first_kernel(field, potential, high_tables, low_tables, kin_out, all_out):
    block = field[0]
    kin = in_plane(block, high_tables, low_tables)
    kin_out[0] = kin
    all_out[0] = kin + (potential[0] - 2.0) * block


def second_kernel(weights, field, extra, potential, high_tables, low_tables, out):
    block = field[0]
    total = in_plane(block, high_tables, low_tables) + (potential[0] - 2.0) * block
    total = weights[0] * total + weights[1] * block + weights[2] * extra[0]
    part = out.shape[3]
    for i in range(out.shape[0]):
        out[i, 0] = total[:, i * part : (i + 1) * part]


def depth_times(high_table, low_table, block):
    high, low = bf16_pair(block)
    return times(high_table[...], high) + (times(low_table[...], high) + times(high_table[...], low))


def lines_of(ref, r, rows):
    devices, lines = ref.shape[:2]
    line = pl.ds(r, lines // rows, stride=rows)
    return jnp.concatenate([ref[d, line, :] for d in range(devices)], axis=0)


def out_kernel(some, rows, chunk, weights, field, potential, high_table, low_table, a_out, c_out, b_out):
    everywhere = high_table.shape[0]
    for pair in [(r, r + 1) for r in range(0, some, 2)]:
        v = jnp.concatenate([lines_of(field, r, some) for r in pair], axis=1)
        both = depth_times(high_table, low_table, v)
        for i, r in enumerate(pair):
            a, line = both[:, 128 * i : 128 * i + 128], pl.ds(r, everywhere, stride=some)
            a_out[0, line, :] = a
            c_out[0, line, :] = weights[0] * v[:, 128 * i : 128 * i + 128] + weights[1] * a
            b_out[0, line, :] = weights[1] * (lines_of(potential, chunk * some + r, rows) - 2.0) * a


def back_kernel(some, cuts, weights, g_in, c_in, b_in, high_table, low_table, *outs):
    everywhere = high_table.shape[0]
    devices = outs[0].shape[0]
    mine = everywhere // devices
    for pair in [(r, r + 1) for r in range(0, some, 2)]:
        lines = [pl.ds(r, everywhere, stride=some) for r in pair]
        parts = [c_in[0, line, :] + weights[1] * lines_of(g_in, r, some) for r, line in zip(pair, lines)]
        both = depth_times(high_table, low_table, jnp.concatenate(parts, axis=1))
        for i, (r, line) in enumerate(zip(pair, lines)):
            m = both[:, 128 * i : 128 * i + 128] + b_in[0, line, :]
            for out, (start, stop) in zip(outs, cuts):
                for d in range(devices):
                    out[d, 0, pl.ds(r, stop - start, stride=some), :] = m[mine * d + start : mine * d + stop]


def tiled(field):
    return field.reshape(field.shape[0], field.shape[1] // 8, 8, field.shape[2])


SMEM = pl.BlockSpec(memory_space=pltpu.SMEM)
VMEM = pl.BlockSpec(memory_space=pltpu.VMEM)
PARAMS = pltpu.CompilerParams(vmem_limit_bytes=48 * 2**20)


def ordered(kernel, count, others):
    def run(*refs):
        kernel(*refs[:count], *refs[count + others :])

    return run


ANY = pl.BlockSpec(memory_space=pl.ANY)


def pick(total, starts, corner, spots, field):
    return pl.pallas_call(
        functools.partial(pick_kernel, total),
        out_shape=jax.ShapeDtypeStruct((starts.shape[0], 1, 128), jnp.float32),
        in_specs=[SMEM, SMEM, VMEM, VMEM],
        out_specs=VMEM,
        scratch_shapes=[pltpu.SMEM((starts.shape[0] + 1,), jnp.int32)],
        compiler_params=PARAMS,
        cost_estimate=pl.CostEstimate(flops=1 << 24, bytes_accessed=1 << 24, transcendentals=0),
        name="pick",
    )(starts, corner, spots, tiled(field))


def pick_block(total, starts, corner, spots, field):
    return pl.pallas_call(
        functools.partial(pick_block_kernel, total),
        out_shape=jax.ShapeDtypeStruct((field.shape[0], starts.shape[0], 1, 128), jnp.float32),
        in_specs=[SMEM, SMEM, VMEM, VMEM],
        out_specs=VMEM,
        scratch_shapes=[pltpu.SMEM((starts.shape[0] + 1,), jnp.int32)],
        compiler_params=PARAMS,
        cost_estimate=pl.CostEstimate(flops=1 << 24, bytes_accessed=1 << 24, transcendentals=0),
        name="pick_block",
    )(starts, corner, spots, field)


def put(total, starts, corner, spots, spread, base):
    shaped = tiled(base)
    return pl.pallas_call(
        functools.partial(put_kernel, total),
        out_shape=jax.ShapeDtypeStruct(shaped.shape, jnp.float32),
        in_specs=[SMEM, SMEM, VMEM, VMEM, VMEM],
        out_specs=VMEM,
        scratch_shapes=[pltpu.SMEM((starts.shape[0] + 1,), jnp.int32)],
        compiler_params=PARAMS,
        cost_estimate=pl.CostEstimate(flops=1 << 24, bytes_accessed=1 << 24, transcendentals=0),
        name="put",
    )(starts, corner, spots, spread, shaped).reshape(base.shape)


def halves_of(table):
    high = lax.reduce_precision(table, 8, 7)
    return high.astype(jnp.bfloat16), (table - high).astype(jnp.bfloat16)


def plane_specs(shape):
    plane = pl.BlockSpec((1,) + shape[1:], lambda z: (z, 0, 0))
    return plane, pl.BlockSpec((2,) + shape[1:], lambda z: (0, 0, 0))


def cost(flops, numbers):
    return pl.CostEstimate(flops=flops, bytes_accessed=4 * numbers, transcendentals=0)


def planar_first(field, potential, tables, *others):
    plane, pair = plane_specs(field.shape)
    return pl.pallas_call(
        ordered(first_kernel, 4, len(others)),
        grid=field.shape[:1],
        out_shape=[jax.ShapeDtypeStruct(field.shape, jnp.float32)] * 2,
        in_specs=[plane, plane, pair, pair] + [ANY] * len(others),
        out_specs=[plane, plane],
        compiler_params=PARAMS,
        cost_estimate=cost(12 * field.shape[2] * field.size, 4 * field.size),
        name="planar_first",
    )(field, potential, *tables, *others)


def planar_second(weights, field, extra, potential, tables, parts):
    plane, pair = plane_specs(field.shape)
    planes, rows_y, cols_x = field.shape
    shape = (parts, planes, rows_y, cols_x // parts)
    return pl.pallas_call(
        second_kernel,
        grid=field.shape[:1],
        out_shape=jax.ShapeDtypeStruct(shape, jnp.float32),
        in_specs=[SMEM, plane, plane, plane, pair, pair],
        out_specs=pl.BlockSpec((parts, 1) + shape[2:], lambda z: (0, z, 0, 0)),
        compiler_params=PARAMS,
        cost_estimate=cost(12 * field.shape[2] * field.size, 4 * field.size),
        name="planar_second",
    )(weights, field, extra, potential, *tables)


def tie(block, *others):
    return pl.pallas_call(
        lambda *refs: None,
        out_shape=jax.ShapeDtypeStruct(block.shape, block.dtype),
        in_specs=[ANY] * (1 + len(others)),
        out_specs=ANY,
        input_output_aliases={0: 0},
        cost_estimate=cost(0, 0),
        name="tie",
    )(block, *others)


def append_kernel(first, others, numbers, block, *refs):
    out, sem = refs[others], refs[others + 1]
    copies = [
        pltpu.make_async_copy(
            numbers.at[d % numbers.shape[0]], out.at[d, pl.ds(first, numbers.shape[1]), :], sem.at[d]
        )
        for d in range(out.shape[0])
    ]
    for copy in copies:
        copy.start()
    for copy in copies:
        copy.wait()


def append(block, numbers, *others):
    devices, lines, wide = block.shape
    return pl.pallas_call(
        functools.partial(append_kernel, lines - numbers.shape[1], len(others)),
        out_shape=jax.ShapeDtypeStruct(block.shape, block.dtype),
        in_specs=[VMEM, ANY] + [ANY] * len(others),
        out_specs=ANY,
        scratch_shapes=[pltpu.SemaphoreType.DMA((devices,))],
        input_output_aliases={1: 0},
        cost_estimate=cost(0, 2 * numbers.size),
        name="append",
    )(numbers, block, *others)


def pack_kernel(count, chunks, chosen, together, *refs):
    fields, out = refs[:count], refs[-1]
    planes, rows, _ = fields[0].shape
    some = rows // chunks // together
    lines = planes * some
    for d in range(together):
        for g in range(out.shape[0]):
            for at, i in enumerate(chosen):
                start = (d * chunks + i) * some
                cells = (slice(None), slice(start, start + some), slice(128 * g, 128 * g + 128))
                part = fields[0][cells]
                for field in fields[1:]:
                    part = part + field[cells]
                out[g, d, at * lines : at * lines + lines, :] = part.reshape(lines, 128)


def pack(fields, devices, chunks, chosen, spare, *others):
    planes, rows_y, cols = fields[0].shape
    rows, groups = rows_y // devices, cols // 128
    together = math.gcd(devices, 4)
    lines = planes * rows * len(chosen) // chunks
    block = pl.BlockSpec((planes, rows * together, cols), lambda d: (0, d, 0))
    got = pl.pallas_call(
        ordered(functools.partial(pack_kernel, len(fields), chunks, chosen, together), len(fields), len(others)),
        grid=(devices // together,),
        out_shape=jax.ShapeDtypeStruct((groups, devices, lines + spare, 128), jnp.float32),
        in_specs=[block] * len(fields) + [ANY] * len(others),
        out_specs=pl.BlockSpec((groups, together, lines, 128), lambda d: (0, d, 0, 0)),
        compiler_params=PARAMS,
        cost_estimate=cost(groups * devices * lines * 128, 2 * groups * devices * lines * 128),
        name="pack",
    )(*fields, *others)
    return got.reshape(groups * devices, lines + spare, 128)


def pack_part_kernel(place, field, out):
    planes, rows, _ = field.shape
    each = rows // out.shape[0]
    for d in range(out.shape[0]):
        out[d] = field[:, d * each : (d + 1) * each, :].reshape(planes * each, 128)


def pack_part(field, devices, place):
    planes, rows_y, _ = field.shape
    together = math.gcd(devices, 4)
    lines = planes * rows_y // devices
    return pl.pallas_call(
        pack_part_kernel,
        grid_spec=pltpu.PrefetchScalarGridSpec(
            num_scalar_prefetch=1,
            grid=(devices // together,),
            in_specs=[pl.BlockSpec((planes, rows_y // devices * together, 128), lambda d, place: (0, d, place[0]))],
            out_specs=pl.BlockSpec((together, lines, 128), lambda d, place: (d, 0, 0)),
        ),
        out_shape=jax.ShapeDtypeStruct((devices, lines, 128), jnp.float32),
        compiler_params=PARAMS,
        cost_estimate=cost(0, 2 * devices * lines * 128),
        name="pack_part",
    )(place, field)


def join_kernel(spans, planes, begin, place, *refs):
    out = refs[-1]
    devices, some = refs[0].shape[1:3]
    rows = out.shape[1] // devices
    first = begin + pl.program_id(0) * planes
    mine = place[0] == 0
    for (chunk, start, stop), own, other in zip(spans, refs[0::2], refs[1::2]):

        @pl.when((first >= start) & (first < stop))
        def _(chunk=chunk, own=own, other=other):
            a, b = own[...], other[...]
            left, right = jnp.where(mine, a, b), jnp.where(mine, b, a)
            for d in range(devices):
                lines = slice(d * rows + chunk * some, d * rows + (chunk + 1) * some)
                out[:, lines, 0:128] = left[:, d]
                out[:, lines, 128:256] = right[:, d]


def join(shape, spans, place, pairs, begin, end, before):
    planes = end - begin
    for _, start, stop in spans:
        planes = math.gcd(planes, start, stop)
    planes = math.gcd(planes, begin, 4)
    specs, blocks = [SMEM], []
    for (_, start, stop), pair in zip(spans, pairs):
        shift, count = (begin - start) // planes, (stop - start) // planes
        block = (planes,) + pair[0].shape[1:]
        spec = pl.BlockSpec(block, lambda z, shift=shift, count=count: (jnp.clip(z + shift, 0, count - 1), 0, 0, 0))
        specs += [spec, spec]
        blocks += pair
    return pl.pallas_call(
        ordered(functools.partial(join_kernel, spans, planes, begin), 1 + len(blocks), len(before)),
        grid=((end - begin) // planes,),
        out_shape=jax.ShapeDtypeStruct(shape, jnp.float32),
        in_specs=specs + [ANY] * len(before),
        out_specs=pl.BlockSpec((planes,) + shape[1:], lambda z: (z + begin // planes, 0, 0)),
        input_output_aliases={1 + len(blocks): 0} if before else {},
        compiler_params=PARAMS,
        cost_estimate=cost(0, 2 * math.prod(shape) * (end - begin) // shape[0]),
        name="join",
    )(place, *blocks, *before)


def depth_specs(planes, some, devices, chunk):
    got = pl.BlockSpec((devices, planes // devices * some, 128), lambda o: (o, chunk, 0))
    flat = pl.BlockSpec((1, planes * some, 128), lambda o: (o, 0, 0))
    return got, flat, pl.BlockSpec((planes, planes), lambda o: (0, 0))


def depth_out(weights, field, potential, some, chunk, orbitals, tables):
    devices, planes = potential.shape[0], tables[0].shape[0]
    rows = potential.shape[1] * devices // planes
    got, flat, table = depth_specs(planes, some, devices, chunk)
    well = pl.BlockSpec(potential.shape, lambda o: (0, 0, 0))
    size = orbitals * planes * some * 128
    return pl.pallas_call(
        functools.partial(out_kernel, some, rows, chunk),
        grid=(orbitals,),
        out_shape=[jax.ShapeDtypeStruct((orbitals, planes * some, 128), jnp.float32)] * 3,
        in_specs=[SMEM, got, well, table, table],
        out_specs=[flat] * 3,
        compiler_params=PARAMS,
        cost_estimate=cost(6 * planes * size, 5 * size),
        name="depth_out",
    )(weights, field, potential, *tables)


def depth_back(weights, g, c, b, some, devices, cuts, tables, *others):
    orbitals, planes = c.shape[0], tables[0].shape[0]
    got, flat, table = depth_specs(planes, some, devices, 0)
    each = [(stop - start) * some for start, stop in cuts]
    return pl.pallas_call(
        ordered(functools.partial(back_kernel, some, cuts), 6, len(others)),
        grid=(orbitals,),
        out_shape=[jax.ShapeDtypeStruct((devices, orbitals, n, 128), jnp.float32) for n in each],
        in_specs=[SMEM, got, flat, flat, table, table] + [ANY] * len(others),
        out_specs=[pl.BlockSpec((devices, 1, n, 128), lambda o: (0, o, 0, 0)) for n in each],
        compiler_params=PARAMS,
        cost_estimate=cost(6 * planes * c.size, 4 * c.size),
        name="depth_back",
    )(weights, g, c, b, *tables, *others)


def atom_windows(cells, all_planes, rows_y, cols_x):
    parts = []
    for coords, size in (
        (cells[:, 0], all_planes),
        (cells[:, 1] // cols_x, rows_y),
        (cells[:, 1] % cols_x, cols_x),
    ):
        anchor = coords[:, :1]
        apart = (coords - anchor + size // 2) % size - size // 2
        least = jnp.min(apart, axis=1, keepdims=True)
        parts.append(((anchor + least) % size, apart - least))
    starts = jnp.concatenate([start for start, _ in parts], axis=1)
    (_, off_z), (_, off_y), (_, off_x) = parts
    spots = jnp.stack([off_y, off_z * STRIDE + off_x], axis=1)
    return starts.astype(jnp.int32), spots.astype(jnp.int32)


def local(random_orbitals, potential, sphere_cells, projectors, kb_energy, cheb_coef):
    grid_count = lax.axis_size("grid")
    grid_pos = lax.axis_index("grid")
    orb_groups = lax.axis_size("orb")
    orb_pos = lax.axis_index("orb")
    planes, rows_y, cols_x = potential.shape
    all_planes = planes * grid_count
    rows = rows_y // grid_count
    orb_count = random_orbitals.shape[0]
    per_dev, projs_each = projectors.shape[:2]
    atoms = per_dev * grid_count
    chunks = 2 if rows % 16 == 0 else 1
    some = rows // chunks
    part = cols_x // orb_groups
    put_late = part % 128 == 0
    joint = orb_groups == 2 and part == 128
    c0, c1, c2 = cheb_coef[0], cheb_coef[1], cheb_coef[2]
    c1_4 = c1 / 4.0
    c2_8 = c2 / 8.0
    planar_tables = [jnp.stack(pair) for pair in zip(halves_of(kinetic_table(cols_x)), halves_of(kinetic_table(rows_y)))]
    kinetic_z = kinetic_table(all_planes)
    depth_tables = halves_of(kinetic_z)
    total = (all_planes, rows_y // 8, cols_x // 128)

    lines = planes * some
    fast = part == 128 and planes % 8 == 0 and some % 8 == 0
    orbitals = orb_groups

    def packed(fields, chosen, spare, *others):
        if fast:
            return pack(fields, grid_count, chunks, chosen, spare, *others)
        field = sum(fields[1:], fields[0]).reshape(planes, grid_count, chunks, some, orb_groups, part)
        field = jnp.stack([field[:, :, i] for i in chosen]).transpose(4, 2, 0, 1, 3, 5)
        field = field.reshape(orb_groups * grid_count, len(chosen) * lines, part)
        return jnp.concatenate([field, jnp.zeros((field.shape[0], spare, part), jnp.float32)], axis=1)

    def along_z(field):
        return jnp.einsum("wz,ozyx->owyx", kinetic_z, field, precision=PRECISE)

    def everyones(block):
        return exchange(block, ("orb", "grid"))

    if fast:
        mine = pack_part(potential, grid_count, orb_pos[None])
        mine = mine.reshape(grid_count, planes, rows, part)
    else:
        mine = lax.dynamic_slice_in_dim(potential, orb_pos * part, part, axis=2)
        mine = mine.reshape(planes, grid_count, rows, part).transpose(1, 0, 2, 3)

    raw = jnp.concatenate([sphere_cells.astype(jnp.float32), projectors], axis=1)
    here = [(grid_pos + grid_count + step) % grid_count for step in (-1, 0, 1)]

    def shifted(block, step):
        return lax.ppermute(block, "grid", [(i, (i + step) % grid_count) for i in range(grid_count)])

    low = 1 << ((grid_count.bit_length() - 1) // 2)
    high = grid_count // low
    column = gather_part(raw, "grid", low.bit_length() - 1, high)
    gots = [shifted(raw, 1), shifted(raw, -1)]
    near = jnp.concatenate([gots[0], raw, gots[1]])
    near_projs = near[:, 2:]
    near_starts, near_spots = atom_windows(near[:, :2].astype(jnp.int32), all_planes, rows_y, cols_x)
    zero = jnp.zeros_like(grid_pos)
    slab_corner = jnp.stack([grid_pos * planes, zero, zero])

    def partial_near(field):
        values = pick(total, near_starts, slab_corner, near_spots, field)
        coeffs = jnp.einsum("aj,apj->ap", values[:, 0], near_projs, precision=PRECISE)
        return coeffs.reshape(3, per_dev, projs_each)

    def whole_near(coeffs):
        steps = 1 if planes >= WIDE else 2
        whole = coeffs
        for step in [s for s in range(-steps, steps + 1) if s]:
            got = shifted(coeffs, step)
            moved = jnp.zeros_like(coeffs)
            for i in range(3):
                if 0 <= i - step < 3:
                    moved = moved.at[i - step].set(got[i])
            whole = whole + moved
        return whole.reshape(3 * per_dev, projs_each)

    def everywhere(coeffs):
        out = jnp.zeros((grid_count, per_dev, projs_each), jnp.float32)
        for i, slab in enumerate(here):
            out = lax.dynamic_update_slice_in_dim(out, coeffs[i : i + 1], slab, 0)
        return out.reshape(atoms, projs_each)

    def nearby(coeffs):
        coeffs = coeffs.reshape(grid_count, per_dev, projs_each)
        return jnp.concatenate([lax.dynamic_index_in_dim(coeffs, slab, 0, keepdims=False) for slab in here])

    def put_near(coeffs, base, corner=slab_corner):
        spread = jnp.einsum("ap,apj->aj", coeffs * kb_energy, near_projs, precision=PRECISE)
        return put(total, near_starts, corner, near_spots, spread[:, None], base)

    got_potential = exchange(tie(mine, *gots), "grid")
    got_potential = got_potential.reshape(grid_count, planes * rows, part)

    late = planes // 8 * 5
    cuts = [[(0, planes)]] * (chunks - 1) + [[(0, late), (late, planes)] if planes % 16 == 0 else [(0, planes)]]
    sums = [[0.0] * len(cut) for cut in cuts]
    weights = jnp.stack([c1_4, c2_8])
    for orb in range(orb_count):
        v = random_orbitals[orb]
        first = whole_near(partial_near(v))
        pv, t = planar_first(v, potential, planar_tables, near_spots)
        v_send = packed([v], range(chunks), 0, near_spots)
        if orb == 0:
            every = gather_part(column, "grid", 0, low)
            every = jnp.swapaxes(every, 0, 1).reshape((atoms,) + raw.shape[1:])
            every_projs = every[:, 2:]
            every_starts, every_spots = atom_windows(every[:, :2].astype(jnp.int32), all_planes, rows_y, cols_x)
        v_got = everyones(tie(v_send, first, column))
        u = put_near(first, t)
        base = planar_second(
            jnp.stack([c2_8, c1_4, c0 - c2]), u, v, potential, planar_tables, orb_groups
        )
        second = jnp.zeros((orbitals, atoms, projs_each), jnp.float32)
        second = lax.dynamic_update_slice_in_dim(second, everywhere(partial_near(u))[None], orb_pos, 0)
        g_gots = []
        for i in range(chunks - 1):
            g_gots.append(everyones(tie(packed([pv, u], [i], 0, base), every)))

        cb, picked = [], []
        for i in range(chunks):
            first_row = grid_pos * rows + i * some
            if fast:
                a, c, b = depth_out(weights, v_got, got_potential, some, i, orbitals, depth_tables)
                corner = jnp.stack([zero, first_row // 8, orb_pos])
                values = pick_block(total, every_starts, corner, every_spots, a.reshape(orbitals, all_planes, some, 128))
            else:
                v_i = v_got.reshape(orbitals, grid_count, chunks, planes, some, part)[:, :, i]
                v_i = v_i.reshape(orbitals, all_planes, some, part)
                well = got_potential.reshape(all_planes, rows, part)[:, i * some : (i + 1) * some]
                a = along_z(v_i)
                c, b = c1_4 * v_i + c2_8 * a, c2_8 * (well - 2.0) * a
                corner = jnp.stack([zero, first_row // 8, zero])
                values = []
                for o in range(orbitals):
                    padded = jnp.zeros((all_planes, -(-some // 8) * 8, cols_x), jnp.float32)
                    padded = lax.dynamic_update_slice(padded, a[o], (0, first_row % 8, orb_pos * part))
                    values.append(pick(total, every_starts, corner, every_spots, padded))
                values = jnp.stack(values)
            cb.append((c, b))
            picked.append(values)
        if put_late:
            mixed, _ = trade(base, "orb", values)
        values = jnp.einsum("oaj,apj->oap", functools.reduce(jnp.add, picked)[:, :, 0], every_projs, precision=PRECISE)
        second = c2_8 * (second + values)
        if fast:
            each = second.reshape(orbitals, grid_count, per_dev, projs_each)
            each = jnp.stack([jnp.roll(each, 1, axis=1), each, jnp.roll(each, -1, axis=1)], axis=2)
            each = jnp.moveaxis(each, 1, 0).reshape(grid_count, -1)
            size = each.shape[1]
            more = -(-size // 1024) * 8
            each = jnp.pad(each, ((0, 0), (0, more * 128 - size))).reshape(grid_count, more, 128)
            g_last = everyones(append(packed([pv, u], [chunks - 1], more, base), each, mixed))
            second = jnp.sum(g_last[:, lines:], axis=0).reshape(-1)[:size]
            second = second.reshape(orbitals, 3 * per_dev, projs_each)
        else:
            g_last = everyones(packed([pv, u], [chunks - 1], 0, base))
            second = lax.psum(second, ("orb", "grid"))
            second = jnp.stack([nearby(second[o]) for o in range(orbitals)])
        g_gots.append(g_last)
        if put_late:
            corner = slab_corner + jnp.stack([zero, zero, orb_pos * (part // 128)])
            q_all = jnp.stack([put_near(second[o], mixed[o], corner) for o in range(orb_groups)])
        else:
            base = jnp.moveaxis(base, 0, 2).reshape(planes, rows_y, cols_x)
            own = lax.dynamic_index_in_dim(second, orb_pos, 0, keepdims=False)
            q = put_near(own, base).reshape(planes, rows_y, orb_groups, part)
            q_all, _ = trade(jnp.moveaxis(q, 2, 0), "orb")
        q_all = q_all.reshape(orb_groups, planes, grid_count, chunks, some, part)

        sends = []
        for i in range(chunks):
            if fast:
                later = [q_all] if i > 0 else []
                ms = depth_back(weights, g_gots[i], *cb[i], some, grid_count, cuts[i], depth_tables, *later)
            else:
                c, b = cb[i]
                g = g_gots[i][:, :lines].reshape(orbitals, all_planes, some, part)
                m = (along_z(c + c2_8 * g) + b).reshape(orbitals, grid_count, planes, some, part)
                m = jnp.moveaxis(m, 1, 0)
                ms = [m[:, :, p:q].reshape(grid_count, orbitals, -1, part) for p, q in cuts[i]]
            sends.append(ms)
        kept, pairs, spans = [], [], []
        for i in range(chunks):
            for k, (start, stop) in enumerate(cuts[i]):
                send = sends[i][k]
                if len(kept) > 1:
                    send = tie(send, *([pairs[0][1]] if pairs else kept[:1]))
                got = exchange(send, "grid")
                m = got.reshape(grid_count, orbitals, stop - start, some, part)
                filtered = q_all[:, start:stop, :, i] + m.transpose(1, 2, 0, 3, 4)
                own = jnp.sum(filtered * filtered, axis=0) * (1.0 / (orb_count * orb_groups))
                kept.append(own)
                sums[i][k] = sums[i][k] + own
                if orb == orb_count - 1 and joint:
                    own = sums[i][k]
                    spans.append((i, start, stop))
                    pairs.append((own, lax.ppermute(own, "orb", [(0, 1), (1, 0)])))
    if joint:
        out, begin = [], 0
        for end in sorted({stop for _, _, stop in spans}):
            some = [i for i, (_, start, stop) in enumerate(spans) if start < end and stop > begin]
            parts = [[each[i] for i in some] for each in (spans, pairs)]
            out = [join(potential.shape, parts[0], orb_pos[None], parts[1], begin, end, out)]
            begin = end
        return out[0]
    out = []
    for parts in sums:
        shares = [gather_over(own[None], "orb") for own in parts]
        out.append(jnp.moveaxis(jnp.concatenate(shares, axis=1), 0, 3))
    return jnp.stack(out, axis=2).reshape(planes, rows_y, cols_x)


def solution(mesh):
    in_specs = (
        P("orb", "grid", None, None),
        P("grid", None, None),
        P("grid", None, None),
        P("grid", None, None),
        P(),
        P(),
    )
    out_specs = P("grid", None, None)
    return jax.shard_map(local, mesh=mesh, in_specs=in_specs, out_specs=out_specs, check_vma=False)
```
